32 devices in a mesh: dp: 8 (over z, y), grp: 4 (over x, core).
Axes of the slice: x: 2, y: 2, z: 4, core: 2. Of those that a mesh axis runs over, the one named last changes fastest.
Arguments:
- image_global: bfloat16 [128, 14, 14, 1024], P(('dp', 'grp')), may hold values from -50 to 50
- image_local: bfloat16 [512, 6, 6, 1024], P(('dp', 'grp')), may hold values from -50 to 50
- w_reduce: bfloat16 [1024, 512], replicated, may hold values from -0.1875 to 0.1875
- w_spatial: bfloat16 [4608, 512], replicated, may hold values from -0.09375 to 0.09375
- w_expand: bfloat16 [512, 2048], replicated, may hold values from -0.25 to 0.25
- w_short: bfloat16 [1024, 2048], replicated, may hold values from -0.1875 to 0.1875
- w_reduce2: bfloat16 [2048, 512], replicated, may hold values from -0.125 to 0.125
- w_spatial2: bfloat16 [4608, 512], replicated, may hold values from -0.09375 to 0.09375
- w_expand2: bfloat16 [512, 2048], replicated, may hold values from -0.25 to 0.25
- gain_mid: float32 [4, 512], replicated, may hold values from 0.25 to 1.75
- shift_mid: float32 [4, 512], replicated, may hold values from -3 to 3
- gain_wide: float32 [3, 2048], replicated, may hold values from 0.25 to 1.75
- shift_wide: float32 [3, 2048], replicated, may hold values from -3 to 3
- cotangent_global: bfloat16 [128, 7, 7, 2048], P(('dp', 'grp')), may hold values from -6 to 6
- cotangent_local: bfloat16 [512, 3, 3, 2048], P(('dp', 'grp')), may hold values from -6 to 6
Outputs:
- output_global: bfloat16 [128, 7, 7, 2048], P(('dp', 'grp'))
- output_local: bfloat16 [512, 3, 3, 2048], P(('dp', 'grp'))
- grad_image_global: bfloat16 [128, 14, 14, 1024], P(('dp', 'grp'))
- grad_image_local: bfloat16 [512, 6, 6, 1024], P(('dp', 'grp'))
- grad_w_reduce: float32 [1024, 512], P('dp')
- grad_w_spatial: float32 [4608, 512], P('dp')
- grad_w_expand: float32 [512, 2048], P('dp')
- grad_w_short: float32 [1024, 2048], P('dp')
- grad_w_reduce2: float32 [2048, 512], P('dp')
- grad_w_spatial2: float32 [4608, 512], P('dp')
- grad_w_expand2: float32 [512, 2048], P('dp')
- grad_gain_mid: float32 [4, 512], replicated
- grad_shift_mid: float32 [4, 512], replicated
- grad_gain_wide: float32 [3, 2048], replicated
- grad_shift_wide: float32 [3, 2048], replicated
The draws below stay inside these ranges and needn't reach their ends.
All inputs are finite; a program needn't handle non-finite values.
Results may differ from the reference program's by a relative error of at most 0.018.
Values sent between devices are 32-bit elements; how exact they have to be, the bound alone decides.
A program may use at most 192 MiB of HBM per device.

```python
import math
import jax
import jax.numpy as jnp
from jax import lax

CIN = 1024
MID = 512
COUT = 2048
GHW = 7
LHW = 3
NG = 128
NL = 512


def crop_field(key, noise):
    crops = noise.shape[0]
    width = noise.shape[3]
    place = jnp.arange(crops, dtype=jnp.float32) / max(crops - 1, 1)
    factor = jnp.exp(jax.random.uniform(jax.random.fold_in(key, 2), (crops,), minval=0.0, maxval=math.log(3.0)))
    scale = (jnp.exp(place * math.log(3.0)) * factor)[:, None, None, None]
    offset = jax.random.uniform(jax.random.fold_in(key, 3), (crops, 1, 1, width), minval=-1.5, maxval=1.5)
    return (scale * (offset + noise)).astype(jnp.bfloat16)


def draw_image_global(key, part):
    key = jax.random.fold_in(key, 11)
    shape = (NG, 2 * GHW, 2 * GHW, CIN)
    noise = jnp.clip(jax.random.normal(jax.random.fold_in(key, 1), shape), -4.0, 4.0)
    return crop_field(key, noise)


def draw_image_local(key, part):
    key = jax.random.fold_in(key, 23)
    shape = (NL, 2 * LHW, 2 * LHW, CIN)
    noise = jnp.clip(jax.random.normal(jax.random.fold_in(key, 1), shape), -4.0, 4.0)
    return crop_field(key, noise)


def strengthened(drawn, own_key, source, target, parts, factor):
    owner, partner = [(jnp.arange(drawn.shape[position]) // (drawn.shape[position] // parts)).reshape([-1 if axis == position else 1 for axis in range(drawn.ndim)]) for position in (source, target)]
    chosen = jax.random.permutation(own_key, parts)[partner]
    strong = (owner == chosen) | (owner == (partner + parts // 2) % parts)
    return jnp.where(strong, factor * drawn, drawn)


def shard_levels(own_key, shape, split, least, largest):
    level = 1.0
    for dim, shards_of in split:
        steps = jax.random.uniform(jax.random.fold_in(jax.random.fold_in(own_key, 6), dim), (shards_of,), jnp.float32, least / len(split), largest / len(split))
        level = level * jnp.repeat(jnp.exp(steps), shape[dim] // shards_of).reshape((-1,) + (1,) * (len(shape) - 1 - dim))
    return level


def scatter_about(key, shape, deviation, most, pieces=(), held_as=jnp.bfloat16):
    drawn = deviation * jax.random.normal(key, shape, jnp.float32)
    if pieces:
        drawn = drawn * shard_levels(key, shape, pieces, -0.22, 0.18)
    return jnp.clip(drawn, -most, most).astype(held_as)


def gaussian_with(rng, extent, scale, bound, pieces, heavy, held_as=jnp.bfloat16):
    entries = scale * jax.random.normal(rng, extent, jnp.float32)
    if pieces:
        entries = entries * shard_levels(rng, extent, pieces, -0.22, 0.18)
    return jnp.clip(strengthened(entries, jax.random.fold_in(rng, 3), *heavy), -bound, bound).astype(held_as)


def setup_inputs(seed: int = 0) -> dict:
    streams_of = jax.random.split(jax.random.key(seed), 16)
    image_global = draw_image_global(jax.random.fold_in(streams_of[15], 71), 0)
    image_local = draw_image_local(jax.random.fold_in(streams_of[15], 71), 0)
    w_reduce = scatter_about(streams_of[2], (CIN, MID), CIN ** -0.5, 0.1875)
    w_spatial = scatter_about(streams_of[3], (9 * MID, MID), (9 * MID) ** -0.5, 0.09375)
    w_expand = scatter_about(streams_of[4], (MID, COUT), MID ** -0.5, 0.25)
    w_short = scatter_about(streams_of[5], (CIN, COUT), CIN ** -0.5, 0.1875)
    w_reduce2 = scatter_about(streams_of[6], (COUT, MID), COUT ** -0.5, 0.125)
    w_spatial2 = scatter_about(streams_of[7], (9 * MID, MID), (9 * MID) ** -0.5, 0.09375)
    w_expand2 = scatter_about(streams_of[8], (MID, COUT), MID ** -0.5, 0.25)
    gain_mid = jnp.clip(1.0 + 0.15 * jax.random.normal(streams_of[9], (4, MID), jnp.float32), 0.25, 1.75)
    shift_mid = scatter_about(streams_of[10], (4, MID), 0.5, 3.0, (), jnp.float32)
    gain_wide = jnp.clip(1.0 + 0.15 * jax.random.normal(streams_of[11], (3, COUT), jnp.float32), 0.25, 1.75)
    shift_wide = scatter_about(streams_of[12], (3, COUT), 0.5, 3.0, (), jnp.float32)
    cotangent_global = gaussian_with(streams_of[13], (NG, GHW, GHW, COUT), 1.0, 6.0, ((0, 32),), (0, 3, 32, 2.75))
    cotangent_local = gaussian_with(streams_of[14], (NL, LHW, LHW, COUT), 1.0, 6.0, ((0, 32),), (0, 3, 32, 2.75))
    return dict(image_global=image_global, image_local=image_local, w_reduce=w_reduce, w_spatial=w_spatial, w_expand=w_expand, w_short=w_short, w_reduce2=w_reduce2, w_spatial2=w_spatial2, w_expand2=w_expand2, gain_mid=gain_mid, shift_mid=shift_mid, gain_wide=gain_wide, shift_wide=shift_wide, cotangent_global=cotangent_global, cotangent_local=cotangent_local)


EPS = 1e-05

@jax.custom_vjp
def low(v):
    return lax.optimization_barrier(v.astype(jnp.bfloat16)).astype(jnp.float32)

@jax.custom_vjp
def low_back(v):
    return v

def low_keep(v):
    return (low(v), None)

def low_pass(kept, grad):
    return (grad,)

def back_keep(v):
    return (v, None)

def back_low(kept, grad):
    return (low(grad),)
low.defvjp(low_keep, low_pass)
low_back.defvjp(back_keep, back_low)

def gelu(value):
    return jax.nn.gelu(value, approximate=True)

def mix(value, weight):
    return jnp.einsum('nhwc,cd->nhwd', value, weight, precision=lax.Precision.HIGHEST)

def spatial(value, weight, stride):
    kernel = weight.reshape(3, 3, value.shape[3], weight.shape[1])
    return lax.conv_general_dilated(value, kernel, (stride, stride), ((1, 1), (1, 1)), dimension_numbers=('NHWC', 'HWIO', 'NHWC'), precision=lax.Precision.HIGHEST)

def normalize(hidden, gain, shift):
    mean = lax.optimization_barrier(jnp.mean(hidden, axis=(0, 1, 2)))
    spread = lax.optimization_barrier(jnp.mean(hidden * hidden, axis=(0, 1, 2))) - mean * mean
    return (hidden - mean) * lax.rsqrt(spread + EPS) * gain + shift

def project(image, w_reduce, w_spatial, w_expand, w_short, gain_mid, shift_mid, gain_wide, shift_wide):
    first = low_back(mix(image, w_reduce))
    inner = low(gelu(normalize(first, gain_mid[0], shift_mid[0])))
    second = low_back(spatial(inner, w_spatial, 2))
    inner = low(gelu(normalize(second, gain_mid[1], shift_mid[1])))
    third = low_back(mix(inner, w_expand))
    side = low_back(mix(image[:, ::2, ::2, :], w_short))
    joined = normalize(third, gain_wide[0], shift_wide[0]) + normalize(side, gain_wide[1], shift_wide[1])
    return low(gelu(joined))

def identity(middle, w_reduce2, w_spatial2, w_expand2, gain_mid, shift_mid, gain_wide, shift_wide):
    fourth = low_back(mix(middle, w_reduce2))
    inner = low(gelu(normalize(fourth, gain_mid[2], shift_mid[2])))
    fifth = low_back(spatial(inner, w_spatial2, 1))
    inner = low(gelu(normalize(fifth, gain_mid[3], shift_mid[3])))
    sixth = low_back(mix(inner, w_expand2))
    return gelu(normalize(sixth, gain_wide[2], shift_wide[2]) + middle)

def forward(image_global, image_local, w_reduce, w_spatial, w_expand, w_short, w_reduce2, w_spatial2, w_expand2, gain_mid, shift_mid, gain_wide, shift_wide):
    results = []
    for image in (image_global, image_local):
        middle = project(image, w_reduce, w_spatial, w_expand, w_short, gain_mid, shift_mid, gain_wide, shift_wide)
        results.append(identity(middle, w_reduce2, w_spatial2, w_expand2, gain_mid, shift_mid, gain_wide, shift_wide))
    return (results[0], results[1])

def reference(image_global, image_local, w_reduce, w_spatial, w_expand, w_short, w_reduce2, w_spatial2, w_expand2, gain_mid, shift_mid, gain_wide, shift_wide, cotangent_global, cotangent_local):
    floats = [value.astype(jnp.float32) for value in (image_global, image_local, w_reduce, w_spatial, w_expand, w_short, w_reduce2, w_spatial2, w_expand2, gain_mid, shift_mid, gain_wide, shift_wide)]
    outputs, pull = jax.vjp(forward, floats[0], floats[1], floats[2], floats[3], floats[4], floats[5], floats[6], floats[7], floats[8], floats[9], floats[10], floats[11], floats[12])
    grads = pull((cotangent_global.astype(jnp.float32), cotangent_local.astype(jnp.float32)))
    return (outputs[0].astype(jnp.bfloat16), outputs[1].astype(jnp.bfloat16), grads[0].astype(jnp.bfloat16), grads[1].astype(jnp.bfloat16), grads[2], grads[3], grads[4], grads[5], grads[6], grads[7], grads[8], grads[9], grads[10], grads[11], grads[12])
```

```python
import functools

import jax
import jax.numpy as jnp
from jax import lax
from jax.experimental import pallas as pl
from jax.experimental.pallas import tpu as pltpu
from jax.sharding import PartitionSpec as P

EPS = 1e-05
MESH_ID = pl.DeviceIdType.MESH


def gelu(value):
    return jax.nn.gelu(value, approximate=True)


def gelu_back(before, grad):
    return jax.vjp(gelu, before)[1](grad)[0]


def stats_kernel(sizes, in_ref, out_ref, grp_buf, part, dp_buf, send_g, recv_g, send_d, recv_d):
    dp_size, grp_size = sizes
    dp = lax.axis_index("dp")
    grp = lax.axis_index("grp")
    barrier = pltpu.get_barrier_semaphore()
    for k in range(1, grp_size):
        pl.semaphore_signal(barrier, inc=1, device_id=(dp, grp ^ k), device_id_type=MESH_ID)
    for k in range(1, dp_size):
        pl.semaphore_signal(barrier, inc=1, device_id=(dp ^ k, grp), device_id_type=MESH_ID)
    pl.semaphore_wait(barrier, grp_size + dp_size - 2)
    copies = []
    for k in range(1, grp_size):
        copy = pltpu.make_async_remote_copy(
            src_ref=in_ref,
            dst_ref=grp_buf.at[grp],
            send_sem=send_g.at[k],
            recv_sem=recv_g.at[k],
            device_id=(dp, grp ^ k),
            device_id_type=MESH_ID,
        )
        copy.start()
        copies.append(copy)
    grp_buf[grp] = in_ref[...]
    for copy in copies:
        copy.wait()
    total = grp_buf[0]
    for k in range(1, grp_size):
        total = total + grp_buf[k]
    part[...] = total
    copies = []
    for k in range(1, dp_size):
        copy = pltpu.make_async_remote_copy(
            src_ref=part,
            dst_ref=dp_buf.at[dp],
            send_sem=send_d.at[k],
            recv_sem=recv_d.at[k],
            device_id=(dp ^ k, grp),
            device_id_type=MESH_ID,
        )
        copy.start()
        copies.append(copy)
    dp_buf[dp] = total
    for copy in copies:
        copy.wait()
    total = dp_buf[0]
    for k in range(1, dp_size):
        total = total + dp_buf[k]
    out_ref[...] = total


def all_sum(values):
    dp_size = lax.axis_size("dp")
    grp_size = lax.axis_size("grp")
    shape = values.shape
    number = {(4, 512): 1, (8, 2048): 2, (4, 2048): 3}[shape]
    return pl.pallas_call(
        functools.partial(stats_kernel, (dp_size, grp_size)),
        out_shape=jax.ShapeDtypeStruct(shape, jnp.float32),
        in_specs=[pl.BlockSpec(memory_space=pltpu.VMEM)],
        out_specs=pl.BlockSpec(memory_space=pltpu.VMEM),
        scratch_shapes=[
            pltpu.VMEM((grp_size,) + shape, jnp.float32),
            pltpu.VMEM(shape, jnp.float32),
            pltpu.VMEM((dp_size,) + shape, jnp.float32),
            pltpu.SemaphoreType.DMA((grp_size,)),
            pltpu.SemaphoreType.DMA((grp_size,)),
            pltpu.SemaphoreType.DMA((dp_size,)),
            pltpu.SemaphoreType.DMA((dp_size,)),
        ],
        compiler_params=pltpu.CompilerParams(collective_id=number, has_side_effects=True),
    )(values)


PANEL = 512
DEPTH = 8


def chunk_list(shapes, dp_size, half):
    chunks = []
    for number, (rows, columns) in enumerate(shapes):
        own = rows // dp_size
        for panel in range(columns // PANEL):
            for start in range(0, own, 2 * half):
                chunks.append((number, start, panel * PANEL))
    return chunks


class Reducer:
    def __init__(self, sizes, shapes, half, weights, outs, scratch):
        dp_size, grp_size = sizes
        self.half = half
        self.weights = weights
        self.outs = outs
        (
            self.acc,
            self.rc,
            self.rd,
            self.fin,
            self.load_sem,
            self.out_sem,
            self.send_sem,
            self.recv_sem,
            self.credit,
        ) = scratch
        self.chunks = chunk_list(shapes, dp_size, half)
        self.dp = lax.axis_index("dp")
        self.grp = lax.axis_index("grp")
        x_bits, dp_bits, y_bits = bit_counts(sizes)
        self.x_bits, self.dp_bits = x_bits, dp_bits
        self.orders = axis_orders(sizes)
        self.steps = x_bits + dp_bits
        self.groups = -(-len(self.chunks) // 3)
        self.stages = self.steps + x_bits + 3
        self.slots = self.steps + 2

    def bit(self, step):
        kind, index = step
        return ((self.grp >> (index + 1)) & 1) if kind == "x" else ((self.dp >> index) & 1)

    def partner(self, step):
        kind, index = step
        if kind == "x":
            return (self.dp, self.grp ^ (2 << index))
        return (self.dp ^ (1 << index), self.grp)

    def sibling(self):
        return (self.dp, self.grp ^ 1)

    def region(self, done, last_flip):
        place = [slice(None)] * self.dp_bits
        width = PANEL
        column = 0
        for number, step in enumerate(done):
            bit = self.bit(step)
            if last_flip and number == len(done) - 1:
                bit = 1 - bit
            if step[0] == "d":
                place[self.dp_bits - 1 - step[1]] = bit
            else:
                width = width // 2
                column = column + bit * width
        return place, column, width

    def view(self, ref, slot, done, flip=False):
        place, column, width = self.region(done, flip)
        if isinstance(column, int):
            cols = pl.ds(column, width)
        else:
            cols = pl.ds(pl.multiple_of(column, width), width)
        return ref.at[(slot, *place, slice(None), cols)]

    def landing(self, slot, order, count):
        return self.rd[slot % 3][count - 1].at[slot // 3]

    def c_copy(self, k, slot):
        number, start, column = self.chunks[k]
        source = self.weights[number].at[
            (slice(None),) * self.dp_bits
            + (
                pl.ds(start + (1 - self.grp % 2) * self.half, self.half),
                pl.ds(column, PANEL),
            )
        ]
        return pltpu.make_async_remote_copy(
            src_ref=source,
            dst_ref=self.rc.at[slot],
            send_sem=self.send_sem.at[slot, 0],
            recv_sem=self.recv_sem.at[slot, 0],
            device_id=self.sibling(),
            device_id_type=MESH_ID,
        )

    def load(self, k, slot):
        number, start, column = self.chunks[k]
        source = self.weights[number].at[
            (slice(None),) * self.dp_bits
            + (pl.ds(start + (self.grp % 2) * self.half, self.half), pl.ds(column, PANEL))
        ]
        return pltpu.make_async_copy(source, self.acc.at[slot], self.load_sem.at[slot])

    def d_copy(self, k, slot, count):
        order = self.orders[k % 3]
        return pltpu.make_async_remote_copy(
            src_ref=self.view(self.acc, slot, order[:count], True),
            dst_ref=self.landing(slot, order, count),
            send_sem=self.send_sem.at[slot, count],
            recv_sem=self.recv_sem.at[slot, count],
            device_id=self.partner(order[count - 1]),
            device_id_type=MESH_ID,
        )

    def x_columns(self, count):
        steps = [("x", i) for i in range(self.x_bits - count)]
        place, column, width = self.region(steps, False)
        if isinstance(column, int):
            return pl.ds(column, width)
        return pl.ds(pl.multiple_of(column, width), width)

    def ag_copy(self, k, slot, count):
        columns = self.x_columns(count)
        block = self.fin.at[slot, :, columns]
        stage = self.steps + 1 + count
        return pltpu.make_async_remote_copy(
            src_ref=block,
            dst_ref=block,
            send_sem=self.send_sem.at[slot, stage],
            recv_sem=self.recv_sem.at[slot, stage],
            device_id=self.partner(("x", self.x_bits - 1 - count)),
            device_id_type=MESH_ID,
        )

    def out_block(self, k):
        number, start, column = self.chunks[k]
        return self.outs[number].at[
            pl.ds(start + (self.grp % 2) * self.half, self.half), pl.ds(column, PANEL)
        ]

    def out_copies(self, k, slot):
        stage = self.stages - 2
        remote = pltpu.make_async_remote_copy(
            src_ref=self.fin.at[slot],
            dst_ref=self.out_block(k),
            send_sem=self.send_sem.at[slot, stage],
            recv_sem=self.recv_sem.at[slot, stage],
            device_id=self.sibling(),
            device_id_type=MESH_ID,
        )
        local = pltpu.make_async_copy(self.fin.at[slot], self.out_block(k), self.out_sem.at[slot])
        return remote, local

    def later(self, k):
        return k + 3 * self.slots < len(self.chunks)

    def give(self, k, slot, stage, device):
        if self.later(k):
            pl.semaphore_signal(
                self.credit.at[slot, stage], inc=1, device_id=device, device_id_type=MESH_ID
            )

    def take(self, k, slot, stage):
        if k >= 3 * self.slots:
            pl.semaphore_wait(self.credit.at[slot, stage], 1)

    def add(self, slot, order, count, target=None):
        done = order[:count]
        place, column, width = self.region(done, False)
        free = [number for number, value in enumerate(place) if isinstance(value, slice)]
        cols = pl.ds(column, width)
        if not isinstance(column, int):
            cols = pl.ds(pl.multiple_of(column, width), width)

        def one(index, carry):
            where = list(place)
            lead = []
            for position, axis in enumerate(free):
                value = (index >> (len(free) - 1 - position)) & 1
                where[axis] = value
                lead.append(value)
            if count == 0:
                arrived = self.rc[(slot, *lead)]
            else:
                arrived = self.rd[slot % 3][count - 1][(slot // 3, *lead)]
            here = (slot, *where, slice(None), cols)
            if target is None:
                self.acc[here] = self.acc[here] + arrived
            else:
                self.fin[slot, :, self.x_columns(0)] = self.acc[here] + arrived
            return carry

        total = 2 ** len(free)
        if total == 1:
            one(0, 0)
        else:
            lax.fori_loop(0, total, one, 0)

    def run(self, k, stage):
        slot = k % (3 * self.slots)
        order = self.orders[k % 3]
        steps = self.steps
        if stage == 0:
            self.load(k, slot).start()
            self.take(k, slot, 0)
            self.c_copy(k, slot).start()
        elif stage <= steps + 1:
            count = stage - 1
            if count == 0:
                self.load(k, slot).wait()
                self.c_copy(k, slot).wait()
            else:
                self.d_copy(k, slot, count).wait()
            self.add(slot, order, count, None if count < steps else True)
            device = self.sibling() if count == 0 else self.partner(order[count - 1])
            self.give(k, slot, count, device)
            self.take(k, slot, count + 1)
            if count < steps:
                self.d_copy(k, slot, count + 1).start()
            else:
                self.ag_copy(k, slot, 0).start()
        elif stage <= steps + self.x_bits:
            count = stage - steps - 1
            self.ag_copy(k, slot, count - 1).wait()
            self.take(k, slot, stage)
            self.ag_copy(k, slot, count).start()
        elif stage == self.stages - 2:
            self.ag_copy(k, slot, self.x_bits - 1).wait()
            remote, local = self.out_copies(k, slot)
            remote.start()
            local.start()
        else:
            remote, local = self.out_copies(k, slot)
            remote.wait()
            local.wait()
            for count in range(self.x_bits):
                device = self.partner(("x", self.x_bits - 1 - count))
                self.give(k, slot, steps + 1 + count, device)

    def step(self, time):
        for stage in reversed(range(self.stages)):
            group = time - stage
            if 0 <= group < self.groups:
                for k in range(3 * group, min(3 * group + 3, len(self.chunks))):
                    self.run(k, stage)

    def barrier(self):
        semaphore = pltpu.get_barrier_semaphore()
        devices = [self.sibling()] + [self.partner(step) for step in self.orders[0]]
        for device in devices:
            pl.semaphore_signal(semaphore, inc=1, device_id=device, device_id_type=MESH_ID)
        pl.semaphore_wait(semaphore, len(devices))


def bit_counts(sizes):
    dp_size, grp_size = sizes
    x_bits = (grp_size // 2).bit_length() - 1
    dp_bits = dp_size.bit_length() - 1
    return x_bits, dp_bits, x_bits


def axis_orders(sizes):
    x_bits, dp_bits, y_bits = bit_counts(sizes)
    xs = [("x", i) for i in range(x_bits)]
    ys = [("d", i) for i in range(y_bits)]
    zs = [("d", i) for i in range(y_bits, dp_bits)]
    return [xs + ys + zs, ys + zs[:1] + xs + zs[1:], zs[:1] + ys + xs + zs[1:]]


def reducer_scratch(sizes, half):
    x_bits, dp_bits, _ = bit_counts(sizes)
    steps = x_bits + dp_bits
    groups = steps + 2
    slots = 3 * groups
    stages = steps + x_bits + 3
    landings = []
    for order in axis_orders(sizes):
        for count in range(1, steps + 1):
            done = [step[0] for step in order[:count]]
            lead = (2,) * (dp_bits - done.count("d"))
            width = PANEL >> done.count("x")
            landings.append(pltpu.VMEM((groups,) + lead + (half, width), jnp.float32))
    block = (slots,) + (2,) * dp_bits + (half, PANEL)
    return [
        pltpu.VMEM(block, jnp.float32),
        pltpu.VMEM(block, jnp.float32),
        *landings,
        pltpu.VMEM((slots, half, PANEL), jnp.float32),
        pltpu.SemaphoreType.DMA((slots,)),
        pltpu.SemaphoreType.DMA((slots,)),
        pltpu.SemaphoreType.DMA((slots, stages)),
        pltpu.SemaphoreType.DMA((slots, stages)),
        pltpu.SemaphoreType.REGULAR((slots, stages)),
    ]


def reduce_kernel(sizes, shapes, half, *refs):
    count = len(shapes)
    x_bits, dp_bits, _ = bit_counts(sizes)
    weights = refs[:count]
    outs = refs[count : 2 * count]
    rest = refs[2 * count :]
    steps = x_bits + dp_bits
    landings = [rest[2 + steps * i : 2 + steps * (i + 1)] for i in range(3)]
    scratch = (rest[0], rest[1], landings) + tuple(rest[2 + 3 * steps :])
    reducer = Reducer(sizes, shapes, half, weights, outs, scratch)
    reducer.barrier()
    for time in range(reducer.groups + reducer.stages - 1):
        reducer.step(time)


def reduce_weights(grads):
    sizes = (lax.axis_size("dp"), lax.axis_size("grp"))
    dp_size = sizes[0]
    dp_bits = dp_size.bit_length() - 1
    shapes = [grad.shape for grad in grads]
    half = 256 // dp_size
    views = [
        grad.reshape((2,) * dp_bits + (grad.shape[0] // dp_size, grad.shape[1])) for grad in grads
    ]
    anywhere = pl.BlockSpec(memory_space=pl.ANY)
    return pl.pallas_call(
        functools.partial(reduce_kernel, sizes, shapes, half),
        out_shape=[
            jax.ShapeDtypeStruct((shape[0] // dp_size, shape[1]), jnp.float32) for shape in shapes
        ],
        in_specs=[anywhere] * len(grads),
        out_specs=[anywhere] * len(grads),
        scratch_shapes=reducer_scratch(sizes, half),
        compiler_params=pltpu.CompilerParams(
            collective_id=4, has_side_effects=True, vmem_limit_bytes=58 * 2**20
        ),
    )(*views)


def mix(value, weight):
    return jnp.einsum("nhwc,cd->nhwd", value, weight, preferred_element_type=jnp.float32)


def mix_back(grad, weight):
    return jnp.einsum("nhwd,cd->nhwc", grad, weight, preferred_element_type=jnp.float32)


def weight_term(values, grads):
    total = None
    for value, grad in zip(values, grads):
        term = jnp.einsum("nhwc,nhwd->cd", value, grad, preferred_element_type=jnp.float32)
        total = term if total is None else total + term
    return total


def spatial(value, weight, stride):
    kernel = weight.reshape(3, 3, value.shape[3], weight.shape[1])
    return lax.conv_general_dilated(
        value,
        kernel,
        (stride, stride),
        ((1, 1), (1, 1)),
        dimension_numbers=("NHWC", "HWIO", "NHWC"),
        preferred_element_type=jnp.float32,
    )


def spatial_back(grad, weight, stride):
    kernel = weight.reshape(3, 3, -1, weight.shape[1])[::-1, ::-1]
    return lax.conv_general_dilated(
        grad,
        kernel,
        (1, 1),
        ((1, stride), (1, stride)),
        lhs_dilation=(stride, stride),
        dimension_numbers=("NHWC", "HWOI", "NHWC"),
        preferred_element_type=jnp.float32,
    )


def spatial_weight(values, grads, stride):
    total = None
    for value, grad in zip(values, grads):
        high = 2 - stride
        term = lax.conv_general_dilated(
            value,
            grad,
            (1, 1),
            ((1, high), (1, high)),
            rhs_dilation=(stride, stride),
            dimension_numbers=("CHWN", "IHWO", "HWNC"),
            preferred_element_type=jnp.float32,
        )
        total = term if total is None else total + term
    return total.reshape(-1, total.shape[3])


def fresh_moments(pairs):
    rows = []
    for group in range(2):
        rows.append(jnp.concatenate([jnp.sum(pair[group], axis=(0, 1, 2)) for pair in pairs]))
        rows.append(
            jnp.concatenate([jnp.sum(pair[group] * pair[group], axis=(0, 1, 2)) for pair in pairs])
        )
    sums = spread_sum(rows, len(pairs))
    devices = lax.axis_size(("dp", "grp"))
    result = []
    start = 0
    for pair in pairs:
        width = pair[0].shape[3]
        moments = []
        for group in range(2):
            count = pair[group].shape[0] * pair[group].shape[1] * pair[group].shape[2] * devices
            mean = sums[2 * group][start : start + width] / count
            spread = sums[2 * group + 1][start : start + width] / count - mean * mean
            moments.append((mean, lax.rsqrt(spread + EPS)))
        result.append(moments)
        start = start + width
    return result


def spread_sum(rows, parts):
    stacked = jnp.stack(rows)
    width = stacked.shape[1] // parts
    stacked = stacked.reshape(4 * parts, width)
    return all_sum(stacked).reshape(4, parts * width)


def standard(value, moment):
    return (value - moment[0]) * moment[1]


def norm_back(items):
    rows = []
    for group in range(2):
        rows.append(jnp.concatenate([jnp.sum(item[0][group], axis=(0, 1, 2)) for item in items]))
        rows.append(
            jnp.concatenate(
                [jnp.sum(item[0][group] * item[1][group], axis=(0, 1, 2)) for item in items]
            )
        )
    sums = spread_sum(rows, len(items))
    devices = lax.axis_size(("dp", "grp"))
    results = []
    start = 0
    for grads, scaled, moments, gain in items:
        width = grads[0].shape[3]
        shift_grad = sums[0][start : start + width] + sums[2][start : start + width]
        gain_grad = sums[1][start : start + width] + sums[3][start : start + width]
        backs = []
        for group in range(2):
            count = grads[group].shape[0] * grads[group].shape[1] * grads[group].shape[2] * devices
            mean_grad = sums[2 * group][start : start + width] / count
            mean_cross = sums[2 * group + 1][start : start + width] / count
            value = (
                gain * moments[group][1] * (grads[group] - mean_grad - scaled[group] * mean_cross)
            )
            backs.append(value.astype(jnp.bfloat16))
        results.append((backs, gain_grad, shift_grad))
        start = start + width
    return results


def norm_section(hidden, moments, gain, shift):
    scaled = [standard(value, moment) for value, moment in zip(hidden, moments)]
    before = [value * gain + shift for value in scaled]
    return (scaled, before)


def rounded(values):
    return [value.astype(jnp.bfloat16) for value in values]


def body(
    image_global,
    image_local,
    w_reduce,
    w_spatial,
    w_expand,
    w_short,
    w_reduce2,
    w_spatial2,
    w_expand2,
    gain_mid,
    shift_mid,
    gain_wide,
    shift_wide,
    cotangent_global,
    cotangent_local,
):
    images = [image_global, image_local]
    first = [mix(value, w_reduce) for value in images]
    moments1 = fresh_moments([first])[0]
    scaled1, before1 = norm_section(first, moments1, gain_mid[0], shift_mid[0])
    inner1 = rounded([gelu(value) for value in before1])
    second = [spatial(value, w_spatial, 2) for value in inner1]
    moments2 = fresh_moments([second])[0]
    scaled2, before2 = norm_section(second, moments2, gain_mid[1], shift_mid[1])
    inner2 = rounded([gelu(value) for value in before2])
    third = [mix(value, w_expand) for value in inner2]
    strided = [value[:, ::2, ::2, :] for value in images]
    side = [mix(value, w_short) for value in strided]
    moments3, moments_side = fresh_moments([third, side])
    scaled3, main_part = norm_section(third, moments3, gain_wide[0], shift_wide[0])
    scaled_side, side_part = norm_section(side, moments_side, gain_wide[1], shift_wide[1])
    before_mid = [main + branch for main, branch in zip(main_part, side_part)]
    middle = rounded([gelu(value) for value in before_mid])
    fourth = [mix(value, w_reduce2) for value in middle]
    moments4 = fresh_moments([fourth])[0]
    scaled4, before4 = norm_section(fourth, moments4, gain_mid[2], shift_mid[2])
    inner4 = rounded([gelu(value) for value in before4])
    fifth = [spatial(value, w_spatial2, 1) for value in inner4]
    moments5 = fresh_moments([fifth])[0]
    scaled5, before5 = norm_section(fifth, moments5, gain_mid[3], shift_mid[3])
    inner5 = rounded([gelu(value) for value in before5])
    sixth = [mix(value, w_expand2) for value in inner5]
    moments6 = fresh_moments([sixth])[0]
    scaled6, main_part = norm_section(sixth, moments6, gain_wide[2], shift_wide[2])
    before_out = [main + residual.astype(jnp.float32) for main, residual in zip(main_part, middle)]
    final = rounded([gelu(value) for value in before_out])

    incoming = [cotangent_global.astype(jnp.float32), cotangent_local.astype(jnp.float32)]
    grad_out = [gelu_back(value, grad) for value, grad in zip(before_out, incoming)]
    back6, gain6, shift6 = norm_back([(grad_out, scaled6, moments6, gain_wide[2])])[0]
    grad_expand2 = weight_term(inner5, back6)
    grad5 = [gelu_back(u, mix_back(grad, w_expand2)) for u, grad in zip(before5, back6)]
    back5, gain5, shift5 = norm_back([(grad5, scaled5, moments5, gain_mid[3])])[0]
    grad_spatial2 = spatial_weight(inner4, back5, 1)
    grad4 = [gelu_back(u, spatial_back(grad, w_spatial2, 1)) for u, grad in zip(before4, back5)]
    back4, gain4, shift4 = norm_back([(grad4, scaled4, moments4, gain_mid[2])])[0]
    grad_reduce2 = weight_term(middle, back4)
    grad_middle = [mix_back(grad, w_reduce2) + rest for grad, rest in zip(back4, grad_out)]
    grad_join = [gelu_back(u, grad) for u, grad in zip(before_mid, grad_middle)]
    (back3, gain3, shift3), (back_side, gain_side, shift_side) = norm_back(
        [
            (grad_join, scaled3, moments3, gain_wide[0]),
            (grad_join, scaled_side, moments_side, gain_wide[1]),
        ]
    )
    grad_expand = weight_term(inner2, back3)
    grad_short = weight_term(strided, back_side)
    grad2 = [gelu_back(u, mix_back(grad, w_expand)) for u, grad in zip(before2, back3)]
    back2, gain2, shift2 = norm_back([(grad2, scaled2, moments2, gain_mid[1])])[0]
    grad_spatial = spatial_weight(inner1, back2, 2)
    grad1 = [gelu_back(u, spatial_back(grad, w_spatial, 2)) for u, grad in zip(before1, back2)]
    back1, gain1, shift1 = norm_back([(grad1, scaled1, moments1, gain_mid[0])])[0]
    grad_reduce = weight_term(images, back1)
    grad_images = []
    for grad_first, grad_side in zip(back1, back_side):
        direct = mix_back(grad_first, w_reduce)
        across = mix_back(grad_side, w_short)
        spread = lax.pad(across, jnp.float32(0), ((0, 0, 0), (0, 1, 1), (0, 1, 1), (0, 0, 0)))
        grad_images.append((direct + spread).astype(jnp.bfloat16))
    totals = reduce_weights(
        [
            grad_expand2,
            grad_spatial2,
            grad_reduce2,
            grad_expand,
            grad_short,
            grad_spatial,
            grad_reduce,
        ]
    )
    return (
        final[0],
        final[1],
        grad_images[0],
        grad_images[1],
        totals[6],
        totals[5],
        totals[3],
        totals[4],
        totals[2],
        totals[1],
        totals[0],
        jnp.stack([gain1, gain2, gain4, gain5]),
        jnp.stack([shift1, shift2, shift4, shift5]),
        jnp.stack([gain3, gain_side, gain6]),
        jnp.stack([shift3, shift_side, shift6]),
    )


def solution(mesh):
    crops = P(("dp", "grp"), None, None, None)
    in_specs = (crops, crops) + (P(),) * 11 + (crops, crops)
    out_specs = (crops,) * 4 + (P("dp", None),) * 7 + (P(),) * 4
    return jax.shard_map(body, mesh=mesh, in_specs=in_specs, out_specs=out_specs, check_vma=False)
```

```python
import functools
import math

import jax
import jax.numpy as jnp
from jax import lax
from jax.experimental import pallas as pl
from jax.experimental.pallas import tpu as pltpu
from jax.sharding import PartitionSpec as P

EPS = 1e-05
MESH_ID = pl.DeviceIdType.MESH


PANEL = 512
DEPTH = 8


def chunk_list(shapes, dp_size, half):
    chunks = []
    for number, (rows, columns) in enumerate(shapes):
        own = rows // dp_size
        for panel in range(columns // PANEL):
            for start in range(0, own, 2 * half):
                chunks.append((number, start, panel * PANEL))
    return chunks


class Reducer:
    def __init__(self, sizes, shapes, half, weights, outs, scratch):
        dp_size, grp_size = sizes
        self.half = half
        self.weights = weights
        self.outs = outs
        (
            self.acc,
            self.rc,
            self.rd,
            self.fin,
            self.load_sem,
            self.out_sem,
            self.send_sem,
            self.recv_sem,
            self.credit,
        ) = scratch
        self.chunks = chunk_list(shapes, dp_size, half)
        self.dp = lax.axis_index("dp")
        self.grp = lax.axis_index("grp")
        x_bits, dp_bits, y_bits = bit_counts(sizes)
        self.x_bits, self.dp_bits = x_bits, dp_bits
        self.orders = axis_orders(sizes)
        self.steps = x_bits + dp_bits
        self.lanes = len(self.orders)
        self.groups = -(-len(self.chunks) // self.lanes)
        self.stages = self.steps + x_bits + 3
        self.slots = self.lanes * (self.steps + 2)

    def bit(self, step):
        kind, index = step
        return ((self.grp >> (index + 1)) & 1) if kind == "x" else ((self.dp >> index) & 1)

    def partner(self, step):
        kind, index = step
        if kind == "x":
            return (self.dp, self.grp ^ (2 << index))
        return (self.dp ^ (1 << index), self.grp)

    def sibling(self):
        return (self.dp, self.grp ^ 1)

    def region(self, done, last_flip):
        place = [slice(None)] * self.dp_bits
        width = PANEL
        column = 0
        for number, step in enumerate(done):
            bit = self.bit(step)
            if last_flip and number == len(done) - 1:
                bit = 1 - bit
            if step[0] == "d":
                place[self.dp_bits - 1 - step[1]] = bit
            else:
                width = width // 2
                column = column + bit * width
        return place, column, width

    def view(self, ref, slot, done, flip=False):
        place, column, width = self.region(done, flip)
        if isinstance(column, int):
            cols = pl.ds(column, width)
        else:
            cols = pl.ds(pl.multiple_of(column, width), width)
        return ref.at[(slot, *place, slice(None), cols)]

    def landing(self, k, order, count):
        return self.rd[k % self.lanes][count - 1].at[(k // self.lanes) % 2]

    def c_copy(self, k, slot):
        number, start, column = self.chunks[k]
        source = self.weights[number].at[
            (slice(None),) * self.dp_bits
            + (
                pl.ds(start + (1 - self.grp % 2) * self.half, self.half),
                pl.ds(column, PANEL),
            )
        ]
        return pltpu.make_async_remote_copy(
            src_ref=source,
            dst_ref=self.rc.at[k % (2 * self.lanes)],
            send_sem=self.send_sem.at[slot, 0],
            recv_sem=self.recv_sem.at[slot, 0],
            device_id=self.sibling(),
            device_id_type=MESH_ID,
        )

    def load(self, k, slot):
        number, start, column = self.chunks[k]
        source = self.weights[number].at[
            (slice(None),) * self.dp_bits
            + (pl.ds(start + (self.grp % 2) * self.half, self.half), pl.ds(column, PANEL))
        ]
        return pltpu.make_async_copy(source, self.acc.at[slot], self.load_sem.at[slot])

    def d_copy(self, k, slot, count):
        order = self.orders[k % self.lanes]
        return pltpu.make_async_remote_copy(
            src_ref=self.view(self.acc, slot, order[:count], True),
            dst_ref=self.landing(k, order, count),
            send_sem=self.send_sem.at[slot, count],
            recv_sem=self.recv_sem.at[slot, count],
            device_id=self.partner(order[count - 1]),
            device_id_type=MESH_ID,
        )

    def x_columns(self, count):
        steps = [("x", i) for i in range(self.x_bits - count)]
        place, column, width = self.region(steps, False)
        if isinstance(column, int):
            return pl.ds(column, width)
        return pl.ds(pl.multiple_of(column, width), width)

    def ag_copy(self, k, slot, count):
        columns = self.x_columns(count)
        block = self.fin.at[slot, :, columns]
        stage = self.steps + 1 + count
        return pltpu.make_async_remote_copy(
            src_ref=block,
            dst_ref=block,
            send_sem=self.send_sem.at[slot, stage],
            recv_sem=self.recv_sem.at[slot, stage],
            device_id=self.partner(("x", self.x_bits - 1 - count)),
            device_id_type=MESH_ID,
        )

    def out_block(self, k):
        number, start, column = self.chunks[k]
        return self.outs[number].at[
            pl.ds(start + (self.grp % 2) * self.half, self.half), pl.ds(column, PANEL)
        ]

    def out_copies(self, k, slot):
        stage = self.stages - 2
        remote = pltpu.make_async_remote_copy(
            src_ref=self.fin.at[slot],
            dst_ref=self.out_block(k),
            send_sem=self.send_sem.at[slot, stage],
            recv_sem=self.recv_sem.at[slot, stage],
            device_id=self.sibling(),
            device_id_type=MESH_ID,
        )
        local = pltpu.make_async_copy(self.fin.at[slot], self.out_block(k), self.out_sem.at[slot])
        return remote, local

    def period(self, stage):
        return 2 * self.lanes if stage <= self.steps else self.slots

    def give(self, k, stage, device):
        period = self.period(stage)
        if k + period < len(self.chunks):
            pl.semaphore_signal(
                self.credit.at[k % period, stage],
                inc=1,
                device_id=device,
                device_id_type=MESH_ID,
            )

    def take(self, k, stage):
        period = self.period(stage)
        if k >= period:
            pl.semaphore_wait(self.credit.at[k % period, stage], 1)

    def add(self, k, slot, order, count, target=None):
        done = order[:count]
        place, column, width = self.region(done, False)
        free = [number for number, value in enumerate(place) if isinstance(value, slice)]
        cols = pl.ds(column, width)
        if not isinstance(column, int):
            cols = pl.ds(pl.multiple_of(column, width), width)

        def one(index, carry):
            where = list(place)
            lead = []
            for position, axis in enumerate(free):
                value = (index >> (len(free) - 1 - position)) & 1
                where[axis] = value
                lead.append(value)
            if count == 0:
                arrived = self.rc[(k % (2 * self.lanes), *lead)]
            else:
                arrived = self.rd[k % self.lanes][count - 1][((k // self.lanes) % 2, *lead)]
            here = (slot, *where, slice(None), cols)
            if target is None:
                self.acc[here] = self.acc[here] + arrived
            else:
                self.fin[slot, :, self.x_columns(0)] = self.acc[here] + arrived
            return carry

        total = 2 ** len(free)
        if total == 1:
            one(0, 0)
        else:
            lax.fori_loop(0, total, one, 0)

    def run(self, k, stage):
        slot = k % self.slots
        order = self.orders[k % self.lanes]
        steps = self.steps
        if stage == 0:
            self.load(k, slot).start()
            self.take(k, 0)
            self.c_copy(k, slot).start()
        elif stage <= steps + 1:
            count = stage - 1
            if count == 0:
                self.load(k, slot).wait()
                self.c_copy(k, slot).wait()
            else:
                self.d_copy(k, slot, count).wait()
            self.add(k, slot, order, count, None if count < steps else True)
            device = self.sibling() if count == 0 else self.partner(order[count - 1])
            self.give(k, count, device)
            self.take(k, count + 1)
            if count < steps:
                self.d_copy(k, slot, count + 1).start()
            else:
                self.ag_copy(k, slot, 0).start()
        elif stage <= steps + self.x_bits:
            count = stage - steps - 1
            self.ag_copy(k, slot, count - 1).wait()
            self.take(k, stage)
            self.ag_copy(k, slot, count).start()
        elif stage == self.stages - 2:
            self.ag_copy(k, slot, self.x_bits - 1).wait()
            remote, local = self.out_copies(k, slot)
            remote.start()
            local.start()
        else:
            remote, local = self.out_copies(k, slot)
            remote.wait()
            local.wait()
            for count in range(self.x_bits):
                device = self.partner(("x", self.x_bits - 1 - count))
                self.give(k, steps + 1 + count, device)

    def step(self, time):
        for stage in reversed(range(self.stages)):
            group = time - stage
            if 0 <= group < self.groups:
                for k in range(
                    self.lanes * group, min(self.lanes * (group + 1), len(self.chunks))
                ):
                    self.run(k, stage)


def bit_counts(sizes):
    dp_size, grp_size = sizes
    x_bits = (grp_size // 2).bit_length() - 1
    dp_bits = dp_size.bit_length() - 1
    return x_bits, dp_bits, x_bits


def axis_orders(sizes):
    x_bits, dp_bits, y_bits = bit_counts(sizes)
    xs = [("x", i) for i in range(x_bits)]
    ys = [("d", i) for i in range(y_bits)]
    zs = [("d", i) for i in range(y_bits, dp_bits)]
    orders = [xs + ys + zs, ys + zs[:1] + xs + zs[1:], zs[:1] + ys + xs + zs[1:]]
    return orders if x_bits + dp_bits < 5 else orders[:2]


def reducer_scratch(sizes, half):
    x_bits, dp_bits, _ = bit_counts(sizes)
    steps = x_bits + dp_bits
    groups = steps + 2
    orders = axis_orders(sizes)
    slots = len(orders) * groups
    stages = steps + x_bits + 3
    landings = []
    for order in orders:
        for count in range(1, steps + 1):
            done = [step[0] for step in order[:count]]
            lead = (2,) * (dp_bits - done.count("d"))
            width = PANEL >> done.count("x")
            landings.append(pltpu.VMEM((2,) + lead + (half, width), jnp.float32))
    block = (slots,) + (2,) * dp_bits + (half, PANEL)
    return [
        pltpu.VMEM(block, jnp.float32),
        pltpu.VMEM((2 * len(orders),) + block[1:], jnp.float32),
        *landings,
        pltpu.VMEM((slots, half, PANEL), jnp.float32),
        pltpu.SemaphoreType.DMA((slots,)),
        pltpu.SemaphoreType.DMA((slots,)),
        pltpu.SemaphoreType.DMA((slots, stages)),
        pltpu.SemaphoreType.DMA((slots, stages)),
        pltpu.SemaphoreType.REGULAR((slots, stages)),
    ]


C0 = math.sqrt(2.0 / math.pi)
C1 = C0 * 0.044715
W = 512
BLK = 16
FIRST, SECOND, THIRD, SIDE, FOURTH, FIFTH, SIXTH = 0, 1, 2, 6, 10, 11, 12


def gelu(u):
    t = jnp.tanh(u * (C0 + C1 * u * u))
    return u * (0.5 + 0.5 * t)


def gelu_both(u):
    square = u * u
    t = jnp.tanh(u * (C0 + C1 * square))
    half = 0.5 + 0.5 * t
    slope = half + 0.5 * u * (1.0 - t * t) * (C0 + 3.0 * C1 * square)
    return u * half, slope


def dot(a, b):
    return lax.dot_general(a, b, (((1,), (0,)), ((), ())), preferred_element_type=jnp.float32)


def dot_t(a, b):
    return lax.dot_general(a, b, (((1,), (1,)), ((), ())), preferred_element_type=jnp.float32)


def dot_rows(a, b):
    return lax.dot_general(a, b, (((0,), (0,)), ((), ())), preferred_element_type=jnp.float32)


class Exchange:
    def __init__(self, sizes, refs):
        self.dp_size, self.grp_size = sizes
        self.msg, self.gbuf, self.part, self.dbuf, self.tot, self.send, self.recv = refs
        self.dp = lax.axis_index("dp")
        self.grp = lax.axis_index("grp")
        self.turn = 1

    def copy(self, phase, k, source, target, device):
        result = pltpu.make_async_remote_copy(
            src_ref=source,
            dst_ref=target,
            send_sem=self.send.at[self.turn, phase, k],
            recv_sem=self.recv.at[self.turn, phase, k],
            device_id=device,
            device_id_type=MESH_ID,
        )
        result.start()
        self.copies.append(result)

    def begin(self):
        self.turn = 1 - self.turn
        return self.msg.at[self.turn]

    def start(self, pieces):
        turn = self.turn
        self.cut = pieces % self.grp_size == 0
        self.own = pieces // self.grp_size if self.cut else pieces
        own = self.own
        self.copies = []
        for k in range(1, self.grp_size):
            peer = self.grp ^ k
            first = peer * own if self.cut else 0
            self.copy(
                0,
                k,
                self.msg.at[turn, pl.ds(first, own)],
                self.gbuf.at[turn, self.grp, pl.ds(0, own)],
                (self.dp, peer),
            )
        for q in range(own):
            here = self.grp * own + q if self.cut else q
            self.gbuf[turn, self.grp, q] = self.msg[turn, here]

    def wait(self):
        for copy in self.copies:
            copy.wait()
        self.copies = []

    def middle(self):
        turn = self.turn
        self.wait()
        for q in range(self.own):
            total = self.gbuf[turn, 0, q]
            for k in range(1, self.grp_size):
                total = total + self.gbuf[turn, k, q]
            self.part[turn, q] = total
            self.dbuf[turn, self.dp, q] = total
        for k in range(1, self.dp_size):
            self.copy(
                1,
                k,
                self.part.at[turn, pl.ds(0, self.own)],
                self.dbuf.at[turn, self.dp, pl.ds(0, self.own)],
                (self.dp ^ k, self.grp),
            )

    def last(self):
        turn = self.turn
        self.wait()
        for q in range(self.own):
            total = self.dbuf[turn, 0, q]
            for k in range(1, self.dp_size):
                total = total + self.dbuf[turn, k, q]
            here = self.grp * self.own + q if self.cut else q
            self.tot[turn, here] = total
        if self.cut:
            block = self.tot.at[turn, pl.ds(self.grp * self.own, self.own)]
            for k in range(1, self.grp_size):
                self.copy(2, k, block, block, (self.dp, self.grp ^ k))

    def finish(self):
        self.wait()
        return self.tot.at[self.turn]


class Net:
    def __init__(self, sizes, geometry, refs):
        self.sizes = sizes
        self.devices = sizes[0] * sizes[1]
        self.crops, self.per = geometry
        self.top = self.crops * 64
        self.rows = self.top + 9 * self.per
        self.top_blocks = self.top // BLK
        self.blocks = self.rows // BLK
        for name, ref in refs.items():
            setattr(self, name, ref)
        self.slot = 0
        self.pending = [[], []]


    def load(self, number, source, target):
        copy = pltpu.make_async_copy(source, target, self.load_sem.at[number])
        copy.start()
        return copy


    def sweep(self, body, init):
        results = []
        for group in range(2):
            low, high = (0, self.top_blocks) if group == 0 else (self.top_blocks, self.blocks)

            def one(index, carry, group=group):
                rows = pl.ds(pl.multiple_of(index * BLK, BLK), BLK)
                return body(group, index, rows, self.keeper(group, index), carry)

            results.append(lax.fori_loop(low, high, one, init))
        return results

    def keeper(self, group, index):
        if group == 1:
            return lambda value: value
        row = index * BLK + lax.broadcasted_iota(jnp.int32, (BLK, 128), 0)
        valid = ((row & 7) != 7) & ((row & 63) < 56)
        valid = jnp.concatenate([valid.astype(jnp.float32)] * (W // 128), axis=1)
        return lambda value: value * valid

    def zeros(self):
        return jnp.zeros((8, W), jnp.float32)

    @staticmethod
    def fold(value):
        return value[0:8] + value[8:16]

    def put(self, msg, piece, results, second=0):
        for group in range(2):
            first, other = results[group][0], results[group][1 + second]
            msg[piece, pl.ds(2 * group, 1)] = jnp.sum(first, axis=0, keepdims=True)
            msg[piece, pl.ds(2 * group + 1, 1)] = jnp.sum(other, axis=0, keepdims=True)

    def count(self, group, scale):
        pixels = (49 * self.crops, 9 * self.per)[group]
        return float(pixels * scale * self.devices)

    def moments(self, total, piece, norm, scale=1):
        for group in range(2):
            count = self.count(group, scale)
            mean = total[piece, pl.ds(2 * group, 1)] / count
            square = total[piece, pl.ds(2 * group + 1, 1)] / count
            self.mom[norm, pl.ds(2 * group, 1)] = mean
            self.mom[norm, pl.ds(2 * group + 1, 1)] = lax.rsqrt(square - mean * mean + EPS)

    def affine(self, norm, group):
        mean = self.mom[norm, pl.ds(2 * group, 1)]
        scale = self.mom[norm, pl.ds(2 * group + 1, 1)] * self.gain[norm]
        return scale, self.shift[norm] - mean * scale

    def standard(self, norm, group):
        mean = self.mom[norm, pl.ds(2 * group, 1)]
        deviation = self.mom[norm, pl.ds(2 * group + 1, 1)]
        return deviation, -mean * deviation

    def measure(self, msg, piece, source, masked, store=None):
        def body(group, index, rows, keep, carry):
            value = source[rows, :]
            if store is not None:
                store[rows, :] = value.astype(store.dtype)
            if masked:
                value = keep(value)
            total, square = carry
            return total + self.fold(value), square + self.fold(value * value)

        results = self.sweep(body, (self.zeros(), self.zeros()))
        if piece is not None:
            self.put(msg, piece, results)
        return results

    def activate(self, source, norm, target):
        params = [self.affine(norm, group) for group in range(2)]

        def body(group, index, rows, keep, carry):
            scale, offset = params[group]
            target(group, index, rows, keep(gelu(source[rows, :] * scale + offset)))
            return carry

        self.sweep(body, 0)


    def shifted(self, source, target, offset):
        start = BLK + offset
        aligned = start // 8 * 8
        skip = start - aligned

        def one(index, carry):
            rows = pl.ds(pl.multiple_of(index * BLK, BLK), BLK)
            if skip:
                value = source[pl.ds(pl.multiple_of(index * BLK + aligned, 8), 24), :]
                value = value[skip : skip + BLK]
            else:
                value = source[pl.ds(pl.multiple_of(index * BLK + aligned, 8), BLK), :]
            target[rows, :] = value.astype(jnp.bfloat16)
            return carry

        lax.fori_loop(0, self.top_blocks, one, 0)

    def moved(self, source, first, target, down, across):
        per = self.per
        for a in range(3):
            for b in range(3):
                here = pl.ds(self.top + (3 * a + b) * per, per)
                if 0 <= a + down < 3 and 0 <= b + across < 3:
                    there = pl.ds(first + (3 * (a + down) + b + across) * per, per)
                    target[here, :] = source[there, :]
                else:
                    target[here, :] = jnp.zeros((per, W), jnp.bfloat16)

    def clear_margins(self, ref):
        zero = jnp.zeros((BLK, W), jnp.float32)
        ref[pl.ds(0, BLK), :] = zero
        ref[pl.ds(BLK + self.top, BLK), :] = zero


    def norm_sums(self, msg, piece, results, norm):
        self.put(msg, piece, results)

    def back(self, norm, total, piece, second=1):
        self.dshift[norm] = total[piece, pl.ds(0, 1)] + total[piece, pl.ds(2, 1)]
        self.dgain[norm] = total[piece, pl.ds(1, 1)] + total[piece, pl.ds(3, 1)]

    def back_params(self, norm, group, total, piece, scale=1):
        count = self.count(group, scale)
        mean_grad = total[piece, pl.ds(2 * group, 1)] / count
        mean_cross = total[piece, pl.ds(2 * group + 1, 1)] / count
        factor = self.gain[norm] * self.mom[norm, pl.ds(2 * group + 1, 1)]
        return factor, mean_grad, mean_cross

    def back_sweep(self, norm, total, piece, grad, hidden, target, scale=1):
        self.back(norm, total, piece)
        params = [
            self.back_params(norm, group, total, piece, scale) + self.standard(norm, group)
            for group in range(2)
        ]

        def body(group, index, rows, keep, carry):
            factor, mean_grad, mean_cross, a, b = params[group]
            scaled = hidden[rows, :].astype(jnp.float32) * a + b
            value = factor * (grad[rows, :] - mean_grad - scaled * mean_cross)
            target(group, index, rows, keep(value))
            return carry

        self.sweep(body, 0)

    def through(self, msg, piece, norm, grad, hidden, masked):
        params = [self.affine(norm, group) + self.standard(norm, group) for group in range(2)]

        def body(group, index, rows, keep, carry):
            scale, offset, a, b = params[group]
            value = hidden[rows, :].astype(jnp.float32)
            slope = gelu_both(value * scale + offset)[1]
            result = grad[rows, :] * slope
            if masked:
                result = keep(result)
            grad[rows, :] = result
            first, cross = carry
            return first + self.fold(result), cross + self.fold(result * (value * a + b))

        results = self.sweep(body, (self.zeros(), self.zeros()))
        if piece is not None:
            self.put(msg, piece, results)
        return results


    def emit(self, number, row, column, value):
        slot = self.slot
        self.slot = 1 - slot
        self.drain(slot)
        self.stage[slot] = value
        grads = self.grads[number]
        own = grads.shape[-2]
        bits = len(grads.shape) - 2
        place = row
        while place < row + W:
            owner = place // own
            size = min(own - place % own, row + W - place)
            index = tuple((owner >> (bits - 1 - i)) & 1 for i in range(bits))
            copy = pltpu.make_async_copy(
                self.stage.at[slot, pl.ds(place - row, size)],
                grads.at[index + (pl.ds(place % own, size), pl.ds(column, W))],
                self.stage_sem.at[slot, len(self.pending[slot])],
            )
            copy.start()
            self.pending[slot].append(copy)
            place += size

    def drain(self, slot):
        for copy in self.pending[slot]:
            copy.wait()
        self.pending[slot] = []

    def flush(self):
        self.drain(0)
        self.drain(1)


def network(net, exchange, reducer):
    rows = net.rows
    top = net.top
    reducer_time = [0]

    def reduce_step():
        reducer.step(reducer_time[0])
        reducer_time[0] += 1

    hbm = net.hbm
    loads = {}
    for plane in range(4):
        loads["img", plane] = net.load(
            plane, hbm["image"].at[pl.ds(plane * rows, rows)], net.img.at[plane]
        )
    loads["wr"] = net.load(4, hbm["w_reduce"], net.wr)
    loads["gain"] = net.load(5, hbm["gain"], net.gain)
    loads["shift"] = net.load(6, hbm["shift"], net.shift)
    loads["ws"] = net.load(7, hbm["w_spatial"], net.wa)
    for k in range(2):
        for p in range(4):
            loads["short", 4 * k + p] = net.load(
                8 + 4 * k + p,
                hbm["w_short"].at[pl.ds(k * W, W), pl.ds(p * W, W)],
                net.wb.at[4 * k + p],
            )
    loads["we"] = net.load(16, hbm["w_expand"], net.we)
    loads["wr2"] = net.load(17, hbm["w_reduce2"], net.wr2)
    loads["we2"] = net.load(18, hbm["w_expand2"], net.we2)
    for p in range(4):
        loads["cot", p] = net.load(19 + p, hbm["cot"].at[:, pl.ds(p * W, W)], net.gh.at[p])
    net.entry()
    for plane in range(4):
        net.clear_margins(net.gz.at[plane])
    net.clear_margins(net.t4)

    loads["wr"].wait()
    msg = exchange.begin()
    results = None
    for plane in range(4):
        loads["img", plane].wait()
        net.f1[plane] = dot(net.img[plane], net.wr[...])
        new = net.measure(msg, None, net.f1.at[plane], False, net.h1.at[plane])
        results = new if results is None else jax.tree.map(jnp.add, results, new)
    net.put(msg, 0, results)
    exchange.start(1)
    side_sums = []

    def side(p):
        for k in range(2):
            loads["short", 4 * k + p].wait()
        net.f3[...] = dot(net.img[0, :, 0:W], net.wb[p]) + dot(net.img[0, :, W:], net.wb[4 + p])
        side_sums.append(net.measure(msg, None, net.f3, False, net.hs.at[p]))

    side(0)
    side(1)
    exchange.middle()
    side(2)
    side(3)
    exchange.last()
    total = exchange.finish()
    loads["gain"].wait()
    loads["shift"].wait()
    net.moments(total, 0, FIRST, 4)
    for plane in range(4):

        def keep_first(group, index, where, value, plane=plane):
            if group == 0:
                net.gz[plane, pl.ds(pl.multiple_of(index * BLK + BLK, BLK), BLK), :] = value
            else:
                there = pl.ds(pl.multiple_of((index - net.top_blocks) * BLK, BLK), BLK)
                net.nl[plane, there, :] = value.astype(jnp.bfloat16)

        net.activate(net.f1.at[plane], FIRST, keep_first)
    for tap in range(9):
        i, j = divmod(tap, 3)
        plane = 2 * (i != 1) + (j != 1)
        net.shifted(net.gz.at[plane], net.x.at[tap], -8 * (i == 0) - (j == 0))
        net.moved(net.nl.at[plane], 0, net.x.at[tap], -(i == 0), -(j == 0))
    save = pltpu.make_async_copy(net.x, hbm["x_keep"], net.load_sem.at[23])
    save.start()
    loads["ws"].wait()
    msg = exchange.begin()

    def conv(weights):
        total = dot(net.x[0], weights[0])
        for tap in range(1, 9):
            total = total + dot(net.x[tap], weights[tap])
        return total

    net.f3[...] = conv(net.wa)
    net.measure(msg, 0, net.f3, True, net.h2)
    loads["ws2"] = net.load(7, hbm["w_spatial2"], net.wa)
    exchange.start(1)
    exchange.middle()
    exchange.last()
    total = exchange.finish()
    net.moments(total, 0, SECOND)

    def plain(ref):
        def keep(group, index, where, value):
            ref[where, :] = value.astype(ref.dtype)

        return keep

    net.activate(net.f3, SECOND, plain(net.n2))
    loads["we"].wait()
    msg = exchange.begin()
    for p in range(4):
        net.f1[p] = dot(net.n2[...], net.we[:, p * W : (p + 1) * W])
        net.measure(msg, p, net.f1.at[p], False, net.h3.at[p])
        net.put(msg, 4 + p, side_sums[p])
    exchange.start(8)
    exchange.middle()
    exchange.last()
    total = exchange.finish()
    for p in range(8):
        net.moments(total, p, THIRD + p)

    def join(p, group):
        a3, b3 = net.affine(THIRD + p, group)
        a4, b4 = net.affine(SIDE + p, group)
        return a3, a4, b3 + b4

    for p in range(4):
        params = [join(p, group) for group in range(2)]

        def join_body(group, index, where, keep, carry, p=p, params=params):
            a3, a4, b = params[group]
            u = net.f1[p, where, :] * a3 + net.hs[p, where, :].astype(jnp.float32) * a4 + b
            net.o1[p, where, :] = keep(gelu(u)).astype(jnp.bfloat16)
            return carry

        net.sweep(join_body, 0)
    loads["wr2"].wait()
    msg = exchange.begin()
    value = dot(net.o1[0], net.wr2[0])
    for p in range(1, 4):
        value = value + dot(net.o1[p], net.wr2[p])
    net.f3[...] = value
    net.measure(msg, 0, net.f3, False, net.h4)
    exchange.start(1)
    exchange.middle()
    exchange.last()
    total = exchange.finish()
    net.moments(total, 0, FOURTH)

    def around(ref):
        def keep(group, index, where, value):
            if group == 0:
                net.t4[pl.ds(pl.multiple_of(index * BLK + BLK, BLK), BLK), :] = value
            ref[where, :] = value.astype(jnp.bfloat16)

        return keep

    net.activate(net.f3, FOURTH, around(net.small))
    save.wait()
    for tap in range(9):
        i, j = divmod(tap, 3)
        net.shifted(net.t4, net.x.at[tap], 8 * (i - 1) + j - 1)
        net.moved(net.small, top, net.x.at[tap], i - 1, j - 1)
    loads["ws2"].wait()
    msg = exchange.begin()
    net.f3[...] = conv(net.wa)
    net.measure(msg, 0, net.f3, True, net.h5)
    exchange.start(1)
    exchange.middle()
    exchange.last()
    total = exchange.finish()
    net.moments(total, 0, FIFTH)
    net.activate(net.f3, FIFTH, plain(net.n5))
    loads["we2"].wait()
    msg = exchange.begin()
    for p in range(4):
        net.f1[p] = dot(net.n5[...], net.we2[:, p * W : (p + 1) * W])
        net.measure(msg, p, net.f1.at[p], False)
    exchange.start(4)
    exchange.middle()
    exchange.last()
    total = exchange.finish()
    for p in range(4):
        net.moments(total, p, SIXTH + p)
        loads["cot", p].wait()
    msg = exchange.begin()
    outs = []
    for p in range(4):
        params = [
            net.affine(SIXTH + p, group) + net.standard(SIXTH + p, group) for group in range(2)
        ]

        def out_body(group, index, where, keep, carry, p=p, params=params):
            scale, offset, a, b = params[group]
            h = net.f1[p, where, :]
            u = h * scale + offset + net.o1[p, where, :].astype(jnp.float32)
            y, slope = gelu_both(u)
            grad = net.gh[p, where, :].astype(jnp.float32) * slope
            net.gh[p, where, :] = y.astype(jnp.bfloat16)
            net.gz[p, where, :] = grad
            first, cross = carry
            return first + net.fold(grad), cross + net.fold(grad * (h * a + b))

        net.put(msg, p, net.sweep(out_body, (net.zeros(), net.zeros())))
        out = pltpu.make_async_copy(
            net.gh.at[p], hbm["y"].at[:, pl.ds(p * W, W)], net.load_sem.at[p]
        )
        out.start()
        outs.append(out)
    exchange.start(4)
    exchange.middle()
    exchange.last()
    total = exchange.finish()
    for out in outs:
        out.wait()
    for p in range(4):
        net.back_sweep(
            SIXTH + p, total, p, net.gz.at[p], net.f1.at[p], plain(net.gh.at[p])
        )
    value = dot_t(net.gh[0], net.we2[:, 0:W])
    for p in range(1, 4):
        value = value + dot_t(net.gh[p], net.we2[:, p * W : (p + 1) * W])
    net.f3[...] = value
    msg = exchange.begin()
    net.through(msg, 0, FIFTH, net.f3, net.h5, False)
    exchange.start(1)
    for p in range(2):
        net.emit(0, 0, p * W, dot_rows(net.n5[...], net.gh[p]))
    exchange.middle()
    for p in range(2, 4):
        net.emit(0, 0, p * W, dot_rows(net.n5[...], net.gh[p]))
    net.flush()
    reduce_step()
    exchange.last()
    total = exchange.finish()
    net.back_sweep(FIFTH, total, 0, net.f3, net.h5, around(net.small))
    for p in range(8):
        loads["short", p] = None
    for tap in range(9):
        i, j = divmod(tap, 3)
        net.shifted(net.t4, net.wb.at[tap], 8 * (1 - i) + 1 - j)
        net.moved(net.small, top, net.wb.at[tap], 1 - i, 1 - j)
    where = pl.ds(0, rows)
    value = dot_t(net.wb[0, where, :], net.wa[0])
    for tap in range(1, 9):
        value = value + dot_t(net.wb[tap, where, :], net.wa[tap])
    net.f3[...] = value
    loads["ws"] = net.load(7, hbm["w_spatial"], net.wa)
    msg = exchange.begin()
    net.through(msg, 0, FOURTH, net.f3, net.h4, True)
    exchange.start(1)
    for tap in range(5):
        net.emit(1, tap * W, 0, dot_rows(net.x[tap], net.small[...]))
    exchange.middle()
    for tap in range(5, 9):
        net.emit(1, tap * W, 0, dot_rows(net.x[tap], net.small[...]))
    net.flush()
    reduce_step()
    loads["x"] = pltpu.make_async_copy(hbm["x_keep"], net.x, net.load_sem.at[23])
    loads["x"].start()
    exchange.last()
    total = exchange.finish()
    net.back_sweep(FOURTH, total, 0, net.f3, net.h4, plain(net.small))
    msg = exchange.begin()
    for p in range(4):
        net.gz[p] = net.gz[p] + dot_t(net.small[...], net.wr2[p])
        params = [
            join(p, group)
            + net.standard(THIRD + p, group)
            + net.standard(SIDE + p, group)
            for group in range(2)
        ]

        def join_back(group, index, where, keep, carry, p=p, params=params):
            a3, a4, b, sa3, sb3, sa4, sb4 = params[group]
            h3 = net.h3[p, where, :].astype(jnp.float32)
            hs = net.hs[p, where, :].astype(jnp.float32)
            slope = gelu_both(h3 * a3 + hs * a4 + b)[1]
            grad = net.gz[p, where, :] * slope
            net.gz[p, where, :] = grad
            first, cross3, cross4 = carry
            return (
                first + net.fold(grad),
                cross3 + net.fold(grad * (h3 * sa3 + sb3)),
                cross4 + net.fold(grad * (hs * sa4 + sb4)),
            )

        results = net.sweep(join_back, (net.zeros(), net.zeros(), net.zeros()))
        net.put(msg, p, results)
        net.put(msg, 4 + p, results, 1)
    exchange.start(8)
    for p in range(2):
        net.emit(2, p * W, 0, dot_rows(net.o1[p], net.small[...]))
    exchange.middle()
    for p in range(2, 4):
        net.emit(2, p * W, 0, dot_rows(net.o1[p], net.small[...]))
    exchange.last()
    net.flush()
    reduce_step()
    total = exchange.finish()
    for p in range(4):
        net.back_sweep(THIRD + p, total, p, net.gz.at[p], net.h3.at[p], plain(net.h3.at[p]))
        net.back_sweep(SIDE + p, total, 4 + p, net.gz.at[p], net.hs.at[p], plain(net.hs.at[p]))
    value = dot_t(net.h3[0], net.we[:, 0:W])
    for p in range(1, 4):
        value = value + dot_t(net.h3[p], net.we[:, p * W : (p + 1) * W])
    net.f3[...] = value
    msg = exchange.begin()
    net.through(msg, 0, SECOND, net.f3, net.h2, False)
    exchange.start(1)
    for p in range(4):
        net.emit(3, 0, p * W, dot_rows(net.n2[...], net.h3[p]))
    exchange.middle()
    for k in range(2):
        for p in range(4):
            net.emit(4, k * W, p * W, dot_rows(net.img[0, :, k * W : (k + 1) * W], net.hs[p]))
    exchange.last()
    net.flush()
    reduce_step()
    total = exchange.finish()
    net.back_sweep(SECOND, total, 0, net.f3, net.h2, around(net.small))
    for s in range(4):
        net.shifted(net.t4, net.wb.at[s], 8 * (s // 2) + s % 2)
        net.moved(net.small, top, net.wb.at[s], s // 2, s % 2)
    loads["ws"].wait()
    msg = exchange.begin()
    results = None
    for plane in range(4):
        value = None
        for tap in range(9):
            i, j = divmod(tap, 3)
            if 2 * (i != 1) + (j != 1) == plane:
                term = dot_t(net.wb[2 * (i == 0) + (j == 0), where, :], net.wa[tap])
                value = term if value is None else value + term
        net.f1[plane] = value
        new = net.through(msg, None, FIRST, net.f1.at[plane], net.h1.at[plane], True)
        results = new if results is None else jax.tree.map(jnp.add, results, new)
    net.put(msg, 0, results)
    for k in range(2):
        for p in range(4):
            loads["short", 4 * k + p] = net.load(
                8 + 4 * k + p,
                hbm["w_short"].at[pl.ds(k * W, W), pl.ds(p * W, W)],
                net.wb.at[4 * k + p],
            )
    exchange.start(1)
    loads["x"].wait()
    for tap in range(5):
        net.emit(5, tap * W, 0, dot_rows(net.x[tap], net.small[...]))
    exchange.middle()
    for tap in range(5, 9):
        net.emit(5, tap * W, 0, dot_rows(net.x[tap], net.small[...]))
    exchange.last()
    net.flush()
    reduce_step()
    total = exchange.finish()
    for plane in range(4):
        net.back_sweep(
            FIRST, total, 0, net.f1.at[plane], net.h1.at[plane], plain(net.h1.at[plane]), 4
        )
    for k in range(2):
        value = dot_rows(net.img[0, :, k * W : (k + 1) * W], net.h1[0])
        for plane in range(1, 4):
            value = value + dot_rows(net.img[plane, :, k * W : (k + 1) * W], net.h1[plane])
        net.emit(6, k * W, 0, value)
    net.flush()
    reduce_step()
    outs = []
    for plane in range(4):
        for k in range(2):
            value = dot_t(net.h1[plane], net.wr[k * W : (k + 1) * W, :])
            if plane == 0:
                for p in range(4):
                    if k == 0:
                        loads["short", p].wait()
                        loads["short", 4 + p].wait()
                    value = value + dot_t(net.hs[p], net.wb[4 * k + p])
            net.img[plane, :, k * W : (k + 1) * W] = value.astype(jnp.bfloat16)
        out = pltpu.make_async_copy(
            net.img.at[plane], hbm["grad_image"].at[pl.ds(plane * rows, rows)], net.load_sem.at[plane]
        )
        out.start()
        outs.append(out)
    while reducer_time[0] < reducer.groups + reducer.stages - 1:
        reduce_step()
    for out in outs:
        out.wait()


HBM_IN = (
    "image",
    "cot",
    "w_reduce",
    "w_spatial",
    "w_expand",
    "w_short",
    "w_reduce2",
    "w_spatial2",
    "w_expand2",
    "gain",
    "shift",
)
SHAPES = ((512, 2048), (4608, 512), (2048, 512), (512, 2048), (1024, 2048), (4608, 512), (1024, 512))


def whole_kernel(sizes, geometry, names, half, *refs):
    x_bits, dp_bits, _ = bit_counts(sizes)
    steps = x_bits + dp_bits
    place = [0]

    def some(number):
        start = place[0]
        place[0] += number
        return refs[start : place[0]]

    hbm = dict(zip(HBM_IN, some(len(HBM_IN))))
    hbm["y"], hbm["grad_image"] = some(2)
    outs = some(7)
    dgain, dshift = some(2)
    grads = some(7)
    (hbm["x_keep"],) = some(1)
    parts = dict(zip(names, some(len(names))))
    exchange = Exchange(sizes, some(7))
    lanes = len(axis_orders(sizes))
    rest = some(2 + lanes * steps + 6)
    landings = [rest[2 + steps * i : 2 + steps * (i + 1)] for i in range(lanes)]
    scratch = (rest[0], rest[1], landings) + tuple(rest[2 + lanes * steps :])
    reducer = Reducer(sizes, SHAPES, half, grads, outs, scratch)
    net = Net(sizes, geometry, parts)
    net.hbm, net.grads, net.dgain, net.dshift = hbm, grads, dgain, dshift

    def entry():
        semaphore = pltpu.get_barrier_semaphore()
        dp_size, grp_size = sizes
        for k in range(1, grp_size):
            pl.semaphore_signal(
                semaphore, inc=1, device_id=(reducer.dp, reducer.grp ^ k), device_id_type=MESH_ID
            )
        for k in range(1, dp_size):
            pl.semaphore_signal(
                semaphore, inc=1, device_id=(reducer.dp ^ k, reducer.grp), device_id_type=MESH_ID
            )
        pl.semaphore_wait(semaphore, dp_size + grp_size - 2)

    net.entry = entry
    network(net, exchange, reducer)


def run_network(image, cot, weights, gain, shift, crops, per):
    sizes = (lax.axis_size("dp"), lax.axis_size("grp"))
    dp_size, grp_size = sizes
    dp_bits = dp_size.bit_length() - 1
    half = 256 // dp_size
    rows = crops * 64 + 9 * per
    bf16, f32 = jnp.bfloat16, jnp.float32
    scratch = {
        "img": pltpu.VMEM((4, rows, 1024), bf16),
        "h1": pltpu.VMEM((4, rows, W), bf16),
        "x": pltpu.VMEM((9, rows, W), bf16),
        "f1": pltpu.VMEM((4, rows, W), f32),
        "h3": pltpu.VMEM((4, rows, W), bf16),
        "hs": pltpu.VMEM((4, rows, W), bf16),
        "o1": pltpu.VMEM((4, rows, W), bf16),
        "h2": pltpu.VMEM((rows, W), bf16),
        "h4": pltpu.VMEM((rows, W), bf16),
        "h5": pltpu.VMEM((rows, W), bf16),
        "n2": pltpu.VMEM((rows, W), bf16),
        "n5": pltpu.VMEM((rows, W), bf16),
        "small": pltpu.VMEM((rows, W), bf16),
        "gz": pltpu.VMEM((4, rows, W), f32),
        "gh": pltpu.VMEM((4, rows, W), bf16),
        "t4": pltpu.VMEM((crops * 64 + 2 * BLK, W), f32),
        "nl": pltpu.VMEM((4, 9 * per, W), bf16),
        "f3": pltpu.VMEM((rows, W), f32),
        "stage": pltpu.VMEM((2, W, W), f32),
        "wr": pltpu.VMEM((1024, W), bf16),
        "we": pltpu.VMEM((W, 2048), bf16),
        "wr2": pltpu.VMEM((4, W, W), bf16),
        "we2": pltpu.VMEM((W, 2048), bf16),
        "wa": pltpu.VMEM((9, W, W), bf16),
        "wb": pltpu.VMEM((9, W, W), bf16),
        "gain": pltpu.VMEM((16, 1, W), f32),
        "shift": pltpu.VMEM((16, 1, W), f32),
        "mom": pltpu.VMEM((16, 4, W), f32),
        "load_sem": pltpu.SemaphoreType.DMA((24,)),
        "stage_sem": pltpu.SemaphoreType.DMA((2, 32)),
    }
    own = 8 if 8 % grp_size else max(8 // grp_size, 4 if 4 % grp_size else 4 // grp_size)
    peers = max(sizes)
    exchange = [
        pltpu.VMEM((2, 8, 4, W), f32),
        pltpu.VMEM((2, grp_size, own, 4, W), f32),
        pltpu.VMEM((2, own, 4, W), f32),
        pltpu.VMEM((2, dp_size, own, 4, W), f32),
        pltpu.VMEM((2, 8, 4, W), f32),
        pltpu.SemaphoreType.DMA((2, 3, peers)),
        pltpu.SemaphoreType.DMA((2, 3, peers)),
    ]
    anywhere = pl.BlockSpec(memory_space=pl.ANY)
    inside = pl.BlockSpec(memory_space=pltpu.VMEM)
    shape = jax.ShapeDtypeStruct
    out_shape = (
        [shape((rows, 2048), bf16), shape((4 * rows, 1024), bf16)]
        + [shape((r // dp_size, c), f32) for r, c in SHAPES]
        + [shape((16, 1, W), f32)] * 2
        + [shape((2,) * dp_bits + (r // dp_size, c), f32) for r, c in SHAPES]
        + [shape((9, rows, W), bf16)]
    )
    return pl.pallas_call(
        functools.partial(whole_kernel, sizes, (crops, per), tuple(scratch), half),
        out_shape=out_shape,
        in_specs=[anywhere] * len(HBM_IN),
        out_specs=[anywhere] * 9 + [inside] * 2 + [anywhere] * 8,
        scratch_shapes=list(scratch.values()) + exchange + reducer_scratch(sizes, half),
        compiler_params=pltpu.CompilerParams(
            collective_id=1, has_side_effects=True, vmem_limit_bytes=VMEM_LIMIT
        ),
    )(image, cot, *weights, gain, shift)


VMEM_LIMIT = 64 * 2**20 - 2**16


def global_rows(value):
    crops, _, _, width = value.shape
    padded = jnp.pad(value, ((0, 0), (0, 1), (0, 1), (0, 0)))
    return padded.reshape(crops * 64, width)


def local_rows(value):
    return value.transpose(1, 2, 0, 3).reshape(-1, value.shape[3])


def global_back(value, crops):
    return value.reshape(crops, 8, 8, -1)[:, :7, :7]


def local_back(value, per):
    return value.reshape(3, 3, per, -1).transpose(2, 0, 1, 3)


def body(
    image_global,
    image_local,
    w_reduce,
    w_spatial,
    w_expand,
    w_short,
    w_reduce2,
    w_spatial2,
    w_expand2,
    gain_mid,
    shift_mid,
    gain_wide,
    shift_wide,
    cotangent_global,
    cotangent_local,
):
    crops, per = image_global.shape[0], image_local.shape[0]
    top = crops * 64
    rows = top + 9 * per
    planes = []
    for a in range(2):
        for b in range(2):
            planes.append(global_rows(image_global[:, a::2, b::2]))
            planes.append(local_rows(image_local[:, a::2, b::2]))
    image = jnp.concatenate(planes)
    cot = jnp.concatenate([global_rows(cotangent_global), local_rows(cotangent_local)])

    def pieces(mid, wide):
        parts = [mid[0:2], wide[0:2].reshape(8, W), mid[2:4], wide[2].reshape(4, W)]
        return jnp.concatenate(parts).reshape(16, 1, W)

    results = run_network(
        image,
        cot,
        [
            w_reduce,
            w_spatial.reshape(9, W, W),
            w_expand,
            w_short,
            w_reduce2.reshape(4, W, W),
            w_spatial2.reshape(9, W, W),
            w_expand2,
        ],
        pieces(gain_mid, gain_wide),
        pieces(shift_mid, shift_wide),
        crops,
        per,
    )
    y, grad_image = results[:2]
    expand2, spatial2, reduce2, expand, short, spatial, reduce = results[2:9]
    planes = grad_image.reshape(2, 2, rows, 1024)
    big = planes[:, :, :top].reshape(2, 2, crops, 8, 8, 1024)[:, :, :, :7, :7]
    big = big.transpose(2, 3, 0, 4, 1, 5).reshape(crops, 14, 14, 1024)
    little = planes[:, :, top:].reshape(2, 2, 3, 3, per, 1024)
    little = little.transpose(4, 2, 0, 3, 1, 5).reshape(per, 6, 6, 1024)

    def split(value):
        value = value.reshape(16, W)
        mid = jnp.concatenate([value[0:2], value[10:12]])
        wide = jnp.concatenate([value[2:10], value[12:16]]).reshape(3, 2048)
        return mid, wide

    gain_grads = split(results[9])
    shift_grads = split(results[10])
    return (
        global_back(y[:top], crops),
        local_back(y[top:], per),
        big,
        little,
        reduce,
        spatial,
        expand,
        short,
        reduce2,
        spatial2,
        expand2,
        gain_grads[0],
        shift_grads[0],
        gain_grads[1],
        shift_grads[1],
    )


def solution(mesh):
    crops = P(("dp", "grp"), None, None, None)
    in_specs = (crops, crops) + (P(),) * 11 + (crops, crops)
    out_specs = (crops,) * 4 + (P("dp", None),) * 7 + (P(),) * 4
    return jax.shard_map(body, mesh=mesh, in_specs=in_specs, out_specs=out_specs, check_vma=False)
```

```python
import functools
import math

import jax
import jax.numpy as jnp
from jax import lax
from jax.experimental import pallas as pl
from jax.experimental.pallas import tpu as pltpu
from jax.sharding import PartitionSpec as P

EPS = 1e-05
MESH_ID = pl.DeviceIdType.MESH


PANEL = 512
DEPTH = 8


def chunk_list(shapes, dp_size, half):
    chunks = []
    for number, (rows, columns) in enumerate(shapes):
        own = rows // dp_size
        for panel in range(columns // PANEL):
            for start in range(0, own, 2 * half):
                chunks.append((number, start, panel * PANEL))
    return chunks


class Reducer:
    def __init__(self, sizes, shapes, half, weights, outs, scratch):
        dp_size, grp_size = sizes
        self.half = half
        self.weights = weights
        self.outs = outs
        (
            self.acc,
            self.rc,
            self.rd,
            self.fin,
            self.load_sem,
            self.out_sem,
            self.send_sem,
            self.recv_sem,
            self.credit,
        ) = scratch
        self.chunks = chunk_list(shapes, dp_size, half)
        self.dp = lax.axis_index("dp")
        self.grp = lax.axis_index("grp")
        x_bits, dp_bits, y_bits = bit_counts(sizes)
        self.x_bits, self.dp_bits = x_bits, dp_bits
        self.orders = axis_orders(sizes)
        self.steps = x_bits + dp_bits
        self.lanes = len(self.orders) // 2
        self.plan = []
        self.entered = 0
        self.stages = self.steps + x_bits + 3
        self.slots = self.lanes * (self.steps + 2)

    def bit(self, step):
        kind, index = step
        return ((self.grp >> (index + 1)) & 1) if kind == "x" else ((self.dp >> index) & 1)

    def partner(self, step):
        kind, index = step
        if kind == "x":
            return (self.dp, self.grp ^ (2 << index))
        return (self.dp ^ (1 << index), self.grp)

    def sibling(self):
        return (self.dp, self.grp ^ 1)

    def region(self, done, last_flip):
        place = [slice(None)] * self.dp_bits
        width = PANEL
        column = 0
        for number, step in enumerate(done):
            bit = self.bit(step)
            if last_flip and number == len(done) - 1:
                bit = 1 - bit
            if step[0] == "d":
                place[self.dp_bits - 1 - step[1]] = bit
            else:
                width = width // 2
                column = column + bit * width
        return place, column, width

    def view(self, ref, slot, done, flip=False):
        place, column, width = self.region(done, flip)
        if isinstance(column, int):
            cols = pl.ds(column, width)
        else:
            cols = pl.ds(pl.multiple_of(column, width), width)
        return ref.at[(slot, *place, slice(None), cols)]

    def landing(self, k, order, count):
        return self.rd[k % len(self.orders)][count - 1]

    def c_copy(self, k, slot):
        number, start, column = self.chunks[k]
        source = self.weights[number].at[
            (slice(None),) * self.dp_bits
            + (
                pl.ds(start + (1 - self.grp % 2) * self.half, self.half),
                pl.ds(column, PANEL),
            )
        ]
        return pltpu.make_async_remote_copy(
            src_ref=source,
            dst_ref=self.rc.at[k % (2 * self.lanes)],
            send_sem=self.send_sem.at[slot, 0],
            recv_sem=self.recv_sem.at[slot, 0],
            device_id=self.sibling(),
            device_id_type=MESH_ID,
        )

    def load(self, k, slot):
        number, start, column = self.chunks[k]
        source = self.weights[number].at[
            (slice(None),) * self.dp_bits
            + (pl.ds(start + (self.grp % 2) * self.half, self.half), pl.ds(column, PANEL))
        ]
        return pltpu.make_async_copy(source, self.acc.at[slot], self.load_sem.at[slot])

    def d_copy(self, k, slot, count):
        order = self.orders[k % len(self.orders)]
        return pltpu.make_async_remote_copy(
            src_ref=self.view(self.acc, slot, order[:count], True),
            dst_ref=self.landing(k, order, count),
            send_sem=self.send_sem.at[slot, count],
            recv_sem=self.recv_sem.at[slot, count],
            device_id=self.partner(order[count - 1]),
            device_id_type=MESH_ID,
        )

    def x_columns(self, count):
        steps = [("x", i) for i in range(self.x_bits - count)]
        place, column, width = self.region(steps, False)
        if isinstance(column, int):
            return pl.ds(column, width)
        return pl.ds(pl.multiple_of(column, width), width)

    def ag_copy(self, k, slot, count):
        columns = self.x_columns(count)
        block = self.fin.at[slot, :, columns]
        stage = self.steps + 1 + count
        return pltpu.make_async_remote_copy(
            src_ref=block,
            dst_ref=block,
            send_sem=self.send_sem.at[slot, stage],
            recv_sem=self.recv_sem.at[slot, stage],
            device_id=self.partner(("x", self.x_bits - 1 - count)),
            device_id_type=MESH_ID,
        )

    def out_block(self, k):
        number, start, column = self.chunks[k]
        return self.outs[number].at[
            pl.ds(start + (self.grp % 2) * self.half, self.half), pl.ds(column, PANEL)
        ]

    def out_copies(self, k, slot):
        stage = self.stages - 2
        remote = pltpu.make_async_remote_copy(
            src_ref=self.fin.at[slot],
            dst_ref=self.out_block(k),
            send_sem=self.send_sem.at[slot, stage],
            recv_sem=self.recv_sem.at[slot, stage],
            device_id=self.sibling(),
            device_id_type=MESH_ID,
        )
        local = pltpu.make_async_copy(self.fin.at[slot], self.out_block(k), self.out_sem.at[slot])
        return remote, local

    def period(self, stage):
        return 2 * self.lanes if stage <= self.steps else self.slots

    def give(self, k, stage, device):
        period = self.period(stage)
        if k + period < len(self.chunks):
            pl.semaphore_signal(
                self.credit.at[k % period, stage],
                inc=1,
                device_id=device,
                device_id_type=MESH_ID,
            )

    def take(self, k, stage):
        period = self.period(stage)
        if k >= period:
            pl.semaphore_wait(self.credit.at[k % period, stage], 1)

    def add(self, k, slot, order, count, target=None):
        done = order[:count]
        place, column, width = self.region(done, False)
        free = [number for number, value in enumerate(place) if isinstance(value, slice)]
        cols = pl.ds(column, width)
        if not isinstance(column, int):
            cols = pl.ds(pl.multiple_of(column, width), width)

        def one(index, carry):
            where = list(place)
            lead = []
            for position, axis in enumerate(free):
                value = (index >> (len(free) - 1 - position)) & 1
                where[axis] = value
                lead.append(value)
            if count == 0:
                arrived = self.rc[(k % (2 * self.lanes), *lead)]
            else:
                arrived = self.rd[k % len(self.orders)][count - 1][(*lead, slice(None), slice(None))]
            here = (slot, *where, slice(None), cols)
            if target is None:
                self.acc[here] = self.acc[here] + arrived
            else:
                self.fin[slot, :, self.x_columns(0)] = self.acc[here] + arrived
            return carry

        total = 2 ** len(free)
        if total == 1:
            one(0, 0)
        else:
            lax.fori_loop(0, total, one, 0)

    def run(self, k, stage):
        slot = k % self.slots
        order = self.orders[k % len(self.orders)]
        steps = self.steps
        if stage == 0:
            self.load(k, slot).start()
            self.take(k, 0)
            self.c_copy(k, slot).start()
        elif stage <= steps + 1:
            count = stage - 1
            if count == 0:
                self.load(k, slot).wait()
                self.c_copy(k, slot).wait()
            else:
                self.d_copy(k, slot, count).wait()
            self.add(k, slot, order, count, None if count < steps else True)
            device = self.sibling() if count == 0 else self.partner(order[count - 1])
            self.give(k, count, device)
            self.take(k, count + 1)
            if count < steps:
                self.d_copy(k, slot, count + 1).start()
            else:
                self.ag_copy(k, slot, 0).start()
        elif stage <= steps + self.x_bits:
            count = stage - steps - 1
            self.ag_copy(k, slot, count - 1).wait()
            self.take(k, stage)
            self.ag_copy(k, slot, count).start()
        elif stage == self.stages - 2:
            self.ag_copy(k, slot, self.x_bits - 1).wait()
            remote, local = self.out_copies(k, slot)
            remote.start()
            local.start()
        else:
            remote, local = self.out_copies(k, slot)
            remote.wait()
            local.wait()
            for count in range(self.x_bits):
                device = self.partner(("x", self.x_bits - 1 - count))
                self.give(k, steps + 1 + count, device)

    def step(self, weights):
        ready = sum(1 for chunk in self.chunks if chunk[0] < weights)
        after = min(ready, self.entered + self.lanes)
        self.plan.append(list(range(self.entered, after)))
        self.entered = after
        time = len(self.plan) - 1
        for stage in (1, 2, 0, *reversed(range(3, self.stages))):
            if stage <= time:
                for k in self.plan[time - stage]:
                    self.run(k, stage)

    def busy(self):
        recent = self.plan[1 - self.stages :]
        return self.entered < len(self.chunks) or any(recent)


def bit_counts(sizes):
    dp_size, grp_size = sizes
    x_bits = (grp_size // 2).bit_length() - 1
    dp_bits = dp_size.bit_length() - 1
    return x_bits, dp_bits, x_bits


def axis_orders(sizes):
    x_bits, dp_bits, y_bits = bit_counts(sizes)
    xs = [("x", i) for i in range(x_bits)]
    ys = [("d", i) for i in range(y_bits)]
    zs = [("d", i) for i in range(y_bits, dp_bits)]
    first = [xs + ys + zs, ys + zs[:1] + xs + zs[1:], zs[:1] + ys + xs + zs[1:]]
    second = [first[0], ys + xs + zs, first[2]]
    lanes = 3 if x_bits + dp_bits < 5 else 2
    return first[:lanes] + second[:lanes]


def reducer_scratch(sizes, half):
    x_bits, dp_bits, _ = bit_counts(sizes)
    steps = x_bits + dp_bits
    groups = steps + 2
    orders = axis_orders(sizes)
    slots = len(orders) // 2 * groups
    stages = steps + x_bits + 3
    landings = []
    for order in orders:
        for count in range(1, steps + 1):
            done = [step[0] for step in order[:count]]
            lead = (2,) * (dp_bits - done.count("d"))
            width = PANEL >> done.count("x")
            landings.append(pltpu.VMEM(lead + (half, width), jnp.float32))
    block = (slots,) + (2,) * dp_bits + (half, PANEL)
    return [
        pltpu.VMEM(block, jnp.float32),
        pltpu.VMEM((len(orders),) + block[1:], jnp.float32),
        *landings,
        pltpu.VMEM((slots, half, PANEL), jnp.float32),
        pltpu.SemaphoreType.DMA((slots,)),
        pltpu.SemaphoreType.DMA((slots,)),
        pltpu.SemaphoreType.DMA((slots, stages)),
        pltpu.SemaphoreType.DMA((slots, stages)),
        pltpu.SemaphoreType.REGULAR((slots, stages)),
    ]


C0 = math.sqrt(2.0 / math.pi)
C1 = C0 * 0.044715
W = 512
BLK = 16
FIRST, SECOND, THIRD, SIDE, FOURTH, FIFTH, SIXTH = 0, 1, 2, 6, 10, 11, 12


def gelu(u):
    t = jnp.tanh(u * (C0 + C1 * u * u))
    return u * (0.5 + 0.5 * t)


def gelu_both(u):
    square = u * u
    t = jnp.tanh(u * (C0 + C1 * square))
    half = 0.5 + 0.5 * t
    slope = half + 0.5 * u * (1.0 - t * t) * (C0 + 3.0 * C1 * square)
    return u * half, slope


def dot(a, b):
    return lax.dot_general(a, b, (((1,), (0,)), ((), ())), preferred_element_type=jnp.float32)


def dot_t(a, b):
    return lax.dot_general(a, b, (((1,), (1,)), ((), ())), preferred_element_type=jnp.float32)


def dot_rows(a, b):
    return lax.dot_general(a, b, (((0,), (0,)), ((), ())), preferred_element_type=jnp.float32)


class Exchange:
    def __init__(self, sizes, refs):
        self.dp_size, self.grp_size = sizes
        self.msg, self.gbuf, self.part, self.dbuf, self.tot, self.send, self.recv = refs
        self.dp = lax.axis_index("dp")
        self.grp = lax.axis_index("grp")
        self.turn = 1

    def copy(self, phase, k, source, target, device):
        result = pltpu.make_async_remote_copy(
            src_ref=source,
            dst_ref=target,
            send_sem=self.send.at[self.turn, phase, k],
            recv_sem=self.recv.at[self.turn, phase, k],
            device_id=device,
            device_id_type=MESH_ID,
        )
        result.start()
        self.copies.append(result)

    def begin(self):
        self.turn = 1 - self.turn
        return self.msg.at[self.turn]

    def start(self, pieces):
        turn = self.turn
        self.cut = pieces % self.grp_size == 0
        self.own = pieces // self.grp_size if self.cut else pieces
        own = self.own
        self.copies = []
        for k in range(1, self.grp_size):
            peer = self.grp ^ k
            first = peer * own if self.cut else 0
            self.copy(
                0,
                k,
                self.msg.at[turn, pl.ds(first, own)],
                self.gbuf.at[turn, self.grp, pl.ds(0, own)],
                (self.dp, peer),
            )
        for q in range(own):
            here = self.grp * own + q if self.cut else q
            self.gbuf[turn, self.grp, q] = self.msg[turn, here]

    def wait(self):
        for copy in self.copies:
            copy.wait()
        self.copies = []

    def middle(self):
        turn = self.turn
        self.wait()
        for q in range(self.own):
            total = self.gbuf[turn, 0, q]
            for k in range(1, self.grp_size):
                total = total + self.gbuf[turn, k, q]
            self.part[turn, q] = total
            self.dbuf[turn, self.dp, q] = total
        for k in range(1, self.dp_size):
            self.copy(
                1,
                k,
                self.part.at[turn, pl.ds(0, self.own)],
                self.dbuf.at[turn, self.dp, pl.ds(0, self.own)],
                (self.dp ^ k, self.grp),
            )

    def last(self):
        turn = self.turn
        self.wait()
        for q in range(self.own):
            total = self.dbuf[turn, 0, q]
            for k in range(1, self.dp_size):
                total = total + self.dbuf[turn, k, q]
            here = self.grp * self.own + q if self.cut else q
            self.tot[turn, here] = total
        if self.cut:
            block = self.tot.at[turn, pl.ds(self.grp * self.own, self.own)]
            for k in range(1, self.grp_size):
                self.copy(2, k, block, block, (self.dp, self.grp ^ k))

    def finish(self):
        self.wait()
        return self.tot.at[self.turn]


class Net:
    def __init__(self, sizes, geometry, refs):
        self.sizes = sizes
        self.devices = sizes[0] * sizes[1]
        self.crops, self.per = geometry
        self.top = self.crops * 56
        self.margin = -(-9 * self.crops // BLK) * BLK
        self.rows = self.top + 9 * self.per
        self.top_blocks = self.top // BLK
        self.blocks = self.rows // BLK
        for name, ref in refs.items():
            setattr(self, name, ref)
        self.slot = 0
        self.done = 0
        self.pending = [[], []]


    def load(self, number, source, target):
        copy = pltpu.make_async_copy(source, target, self.load_sem.at[number])
        copy.start()
        return copy


    def pixels(self, plane, half=None):
        columns = slice(None) if half is None else slice(half * W, (half + 1) * W)
        value = self.img[plane, :, :, columns]
        return value.reshape(self.rows, value.shape[2])

    def spread_image(self, a):
        crops = self.crops

        def one(row, carry):
            for b in range(2):
                for column in range(7):
                    value = self.raw[a, row, 2 * column + b]
                    self.turn[b, pl.ds(crops * column, crops), :] = value.astype(jnp.float32)
                block = self.turn[b].astype(jnp.bfloat16).reshape(-1, BLK, 1024)
                where = pl.ds(row * (8 * crops // BLK), 8 * crops // BLK)
                self.img[2 * a + b, where] = block
            return carry

        lax.fori_loop(0, 7, one, 0)

    def gather_image(self, a):
        crops = self.crops

        def one(row, carry):
            for b in range(2):
                where = pl.ds(row * (8 * crops // BLK), 8 * crops // BLK)
                block = self.img[2 * a + b, where].reshape(8 * crops, 1024)
                self.turn[b] = block.astype(jnp.float32)
                for column in range(7):
                    value = self.turn[b, pl.ds(crops * column, crops), :]
                    self.raw[a, row, 2 * column + b] = value.astype(jnp.bfloat16)
            return carry

        lax.fori_loop(0, 7, one, 0)

    def spread_wide(self, source, target):
        crops = self.crops

        def one(row, carry):
            for half in range(2):
                for column in range(7):
                    value = source[row, column, :, half * 1024 : (half + 1) * 1024]
                    self.turn[half, pl.ds(crops * column, crops), :] = value.astype(jnp.float32)
                for p in range(2):
                    value = self.turn[half, :, p * W : (p + 1) * W].astype(jnp.bfloat16)
                    where = pl.ds(pl.multiple_of(row * 8 * crops, BLK), 8 * crops)
                    target[2 * half + p, where, :] = value
            return carry

        lax.fori_loop(0, 7, one, 0)

    def gather_wide(self, source, target):
        crops = self.crops

        def one(row, carry):
            for half in range(2):
                for p in range(2):
                    where = pl.ds(pl.multiple_of(row * 8 * crops, BLK), 8 * crops)
                    value = source[2 * half + p, where, :].astype(jnp.float32)
                    self.turn[half, :, p * W : (p + 1) * W] = value
                for column in range(7):
                    value = self.turn[half, pl.ds(crops * column, crops), :]
                    target[row, column, :, half * 1024 : (half + 1) * 1024] = value.astype(
                        jnp.bfloat16
                    )
            return carry

        lax.fori_loop(0, 7, one, 0)


    def sweep(self, body, init):
        results = []
        for group in range(2):
            low, high = (0, self.top_blocks) if group == 0 else (self.top_blocks, self.blocks)

            def one(index, carry, group=group):
                rows = pl.ds(pl.multiple_of(index * BLK, BLK), BLK)
                return body(group, index, rows, self.keeper(group, index), carry)

            results.append(lax.fori_loop(low, high, one, init))
        return results

    def keeper(self, group, index):
        if group == 1:
            return lambda value: value
        row = index * BLK + lax.broadcasted_iota(jnp.int32, (BLK, 128), 0)
        valid = row % (8 * self.crops) < 7 * self.crops
        valid = jnp.concatenate([valid.astype(jnp.float32)] * (W // 128), axis=1)
        return lambda value: value * valid

    def zeros(self):
        return jnp.zeros((8, W), jnp.float32)

    @staticmethod
    def fold(value):
        return value[0:8] + value[8:16]

    def put(self, msg, piece, results, second=0):
        for group in range(2):
            first, other = results[group][0], results[group][1 + second]
            msg[piece, pl.ds(2 * group, 1)] = jnp.sum(first, axis=0, keepdims=True)
            msg[piece, pl.ds(2 * group + 1, 1)] = jnp.sum(other, axis=0, keepdims=True)

    def count(self, group, scale):
        pixels = (49 * self.crops, 9 * self.per)[group]
        return float(pixels * scale * self.devices)

    def moments(self, total, piece, norm, scale=1):
        for group in range(2):
            count = self.count(group, scale)
            mean = total[piece, pl.ds(2 * group, 1)] / count
            square = total[piece, pl.ds(2 * group + 1, 1)] / count
            self.mom[norm, pl.ds(2 * group, 1)] = mean
            self.mom[norm, pl.ds(2 * group + 1, 1)] = lax.rsqrt(square - mean * mean + EPS)

    def affine(self, norm, group):
        mean = self.mom[norm, pl.ds(2 * group, 1)]
        scale = self.mom[norm, pl.ds(2 * group + 1, 1)] * self.gain[norm]
        return scale, self.shift[norm] - mean * scale

    def standard(self, norm, group):
        mean = self.mom[norm, pl.ds(2 * group, 1)]
        deviation = self.mom[norm, pl.ds(2 * group + 1, 1)]
        return deviation, -mean * deviation

    def measure(self, msg, piece, source, masked, store=None):
        def body(group, index, rows, keep, carry):
            value = source[rows, :]
            if store is not None:
                store[rows, :] = value.astype(store.dtype)
            if masked:
                value = keep(value)
            total, square = carry
            return total + self.fold(value), square + self.fold(value * value)

        results = self.sweep(body, (self.zeros(), self.zeros()))
        if piece is not None:
            self.put(msg, piece, results)
        return results

    def activate(self, source, norm, target):
        params = [self.affine(norm, group) for group in range(2)]

        def body(group, index, rows, keep, carry):
            scale, offset = params[group]
            target(group, index, rows, keep(gelu(source[rows, :] * scale + offset)))
            return carry

        self.sweep(body, 0)


    def shifted(self, source, target, down, across):
        offset = (8 * down + across) * self.crops
        start = self.margin + offset
        aligned = start // 8 * 8
        skip = start - aligned

        def one(index, carry):
            rows = pl.ds(pl.multiple_of(index * BLK, BLK), BLK)
            if skip:
                value = source[pl.ds(pl.multiple_of(index * BLK + aligned, 8), 24), :]
                value = value[skip : skip + BLK]
            else:
                value = source[pl.ds(pl.multiple_of(index * BLK + aligned, 8), BLK), :]
            target[rows, :] = value.astype(jnp.bfloat16)
            return carry

        lax.fori_loop(0, self.top_blocks, one, 0)

    def moved(self, source, first, target, down, across):
        per = self.per
        for a in range(3):
            for b in range(3):
                here = pl.ds(self.top + (3 * a + b) * per, per)
                if 0 <= a + down < 3 and 0 <= b + across < 3:
                    there = pl.ds(first + (3 * (a + down) + b + across) * per, per)
                    target[here, :] = source[there, :]
                else:
                    target[here, :] = jnp.zeros((per, W), jnp.bfloat16)

    def clear_margins(self, ref):
        zero = jnp.zeros((self.margin, W), jnp.float32)
        ref[pl.ds(0, self.margin), :] = zero
        ref[pl.ds(self.margin + self.top, self.margin), :] = zero

    @staticmethod
    def parameter(norm):
        if norm in (FIRST, SECOND):
            return 0, norm, slice(0, W)
        if norm in (FOURTH, FIFTH):
            return 0, norm - FOURTH + 2, slice(0, W)
        row, panel = (2, norm - SIXTH) if norm >= SIXTH else divmod(norm - THIRD, 4)
        return 1, row, slice(panel * W, (panel + 1) * W)


    def norm_sums(self, msg, piece, results, norm):
        self.put(msg, piece, results)

    def back(self, norm, total, piece, second=1):
        kind, row, columns = self.parameter(norm)
        where = (slice(row, row + 1), columns)
        self.dshift[kind][where] = total[piece, pl.ds(0, 1)] + total[piece, pl.ds(2, 1)]
        self.dgain[kind][where] = total[piece, pl.ds(1, 1)] + total[piece, pl.ds(3, 1)]

    def back_params(self, norm, group, total, piece, scale=1):
        count = self.count(group, scale)
        mean_grad = total[piece, pl.ds(2 * group, 1)] / count
        mean_cross = total[piece, pl.ds(2 * group + 1, 1)] / count
        factor = self.gain[norm] * self.mom[norm, pl.ds(2 * group + 1, 1)]
        return factor, mean_grad, mean_cross

    def back_sweep(self, norm, total, piece, grad, hidden, target, scale=1):
        self.back(norm, total, piece)
        params = [
            self.back_params(norm, group, total, piece, scale) + self.standard(norm, group)
            for group in range(2)
        ]

        def body(group, index, rows, keep, carry):
            factor, mean_grad, mean_cross, a, b = params[group]
            scaled = hidden[rows, :].astype(jnp.float32) * a + b
            value = factor * (grad[rows, :] - mean_grad - scaled * mean_cross)
            target(group, index, rows, keep(value))
            return carry

        self.sweep(body, 0)

    def through(self, msg, piece, norm, grad, hidden, masked):
        params = [self.affine(norm, group) + self.standard(norm, group) for group in range(2)]

        def body(group, index, rows, keep, carry):
            scale, offset, a, b = params[group]
            value = hidden[rows, :].astype(jnp.float32)
            slope = gelu_both(value * scale + offset)[1]
            result = grad[rows, :] * slope
            if masked:
                result = keep(result)
            grad[rows, :] = result
            first, cross = carry
            return first + self.fold(result), cross + self.fold(result * (value * a + b))

        results = self.sweep(body, (self.zeros(), self.zeros()))
        if piece is not None:
            self.put(msg, piece, results)
        return results


    def emit(self, number, row, column, value):
        slot = self.slot
        self.slot = 1 - slot
        self.drain(slot)
        self.stage[slot] = value
        grads = self.grads[number]
        own = grads.shape[-2]
        bits = len(grads.shape) - 2
        place = row
        while place < row + W:
            owner = place // own
            size = min(own - place % own, row + W - place)
            index = tuple((owner >> (bits - 1 - i)) & 1 for i in range(bits))
            copy = pltpu.make_async_copy(
                self.stage.at[slot, pl.ds(place - row, size)],
                grads.at[index + (pl.ds(place % own, size), pl.ds(column, W))],
                self.stage_sem.at[slot, len(self.pending[slot])],
            )
            copy.start()
            self.pending[slot].append(copy)
            place += size

    def drain(self, slot):
        for copy in self.pending[slot]:
            copy.wait()
        self.pending[slot] = []

    def flush(self, weights):
        self.drain(0)
        self.drain(1)
        self.done = weights


def network(net, exchange, reducer):
    rows = net.rows
    top = net.top

    def reduce_step():
        reducer.step(net.done)

    hbm = net.hbm
    loads = {}
    for a in range(2):
        loads["img", a] = net.load(a, hbm["image_global"].at[:, a], net.raw.at[a])
    edge, wide = net.top_blocks, net.per // BLK
    for plane in range(4):
        for row in range(3):
            loads["img", plane, row] = net.load(
                24 + 3 * plane + row,
                hbm["image_local"].at[row, plane // 2, :, plane % 2],
                net.img.at[plane, pl.ds(edge + 3 * wide * row, 3 * wide)],
            )
    loads["wr"] = net.load(4, hbm["w_reduce"], net.wr)
    loads["ws"] = net.load(7, hbm["w_spatial"], net.wa)
    for k in range(2):
        for p in range(4):
            loads["short", 4 * k + p] = net.load(
                8 + 4 * k + p,
                hbm["w_short"].at[pl.ds(k * W, W), pl.ds(p * W, W)],
                net.wb.at[4 * k + p],
            )
    loads["we"] = net.load(16, hbm["w_expand"], net.we)
    loads["wr2"] = net.load(17, hbm["w_reduce2"], net.wr2)
    loads["we2"] = net.load(18, hbm["w_expand2"], net.we2)
    net.entry()
    for plane in range(4):
        net.clear_margins(net.gz.at[plane])
    net.clear_margins(net.t4)
    net.turn[...] = jnp.zeros(net.turn.shape, jnp.float32)
    for norm in range(16):
        kind, row, columns = net.parameter(norm)
        net.gain[norm] = hbm[("gain_mid", "gain_wide")[kind]][row : row + 1, columns]
        net.shift[norm] = hbm[("shift_mid", "shift_wide")[kind]][row : row + 1, columns]

    loads["wr"].wait()
    msg = exchange.begin()
    results = None
    for plane in range(4):
        if plane % 2 == 0:
            loads["img", plane // 2].wait()
            net.spread_image(plane // 2)
        for row in range(3):
            loads["img", plane, row].wait()
        net.f1[plane] = dot(net.pixels(plane), net.wr[...])
        new = net.measure(msg, None, net.f1.at[plane], False, net.h1.at[plane])
        results = new if results is None else jax.tree.map(jnp.add, results, new)
    net.put(msg, 0, results)
    exchange.start(1)
    side_sums = []

    def side(p):
        for k in range(2):
            loads["short", 4 * k + p].wait()
        net.f3[...] = dot(net.pixels(0, 0), net.wb[p]) + dot(net.pixels(0, 1), net.wb[4 + p])
        side_sums.append(net.measure(msg, None, net.f3, False, net.hs.at[p]))

    side(0)
    side(1)
    loads["cot"] = net.load(2, hbm["cot_global"], net.wide)
    for p in range(4):
        for place in range(9):
            loads["cot", p, place] = net.load(
                40 + 9 * p + place,
                hbm["cot_local"].at[place, :, pl.ds(p * W, W)],
                net.gh.at[p, pl.ds(top + place * net.per, net.per)],
            )
    exchange.middle()
    side(2)
    side(3)
    exchange.last()
    total = exchange.finish()
    net.moments(total, 0, FIRST, 4)
    for plane in range(4):

        def keep_first(group, index, where, value, plane=plane):
            if group == 0:
                net.gz[plane, pl.ds(pl.multiple_of(index * BLK + net.margin, BLK), BLK), :] = value
            else:
                there = pl.ds(pl.multiple_of((index - net.top_blocks) * BLK, BLK), BLK)
                net.nl[plane, there, :] = value.astype(jnp.bfloat16)

        net.activate(net.f1.at[plane], FIRST, keep_first)
    for tap in range(9):
        i, j = divmod(tap, 3)
        plane = 2 * (i != 1) + (j != 1)
        net.shifted(net.gz.at[plane], net.x.at[tap], -(i == 0), -(j == 0))
        net.moved(net.nl.at[plane], 0, net.x.at[tap], -(i == 0), -(j == 0))
    save = pltpu.make_async_copy(net.x, hbm["x_keep"], net.load_sem.at[23])
    save.start()
    loads["ws"].wait()
    msg = exchange.begin()

    def conv(weights):
        total = dot(net.x[0], weights[0])
        for tap in range(1, 9):
            total = total + dot(net.x[tap], weights[tap])
        return total

    net.f3[...] = conv(net.wa)
    net.measure(msg, 0, net.f3, True, net.h2)
    loads["ws2"] = net.load(7, hbm["w_spatial2"], net.wa)
    exchange.start(1)
    loads["cot"].wait()
    net.spread_wide(net.wide, net.gh)
    exchange.middle()
    exchange.last()
    total = exchange.finish()
    net.moments(total, 0, SECOND)

    def plain(ref):
        def keep(group, index, where, value):
            ref[where, :] = value.astype(ref.dtype)

        return keep

    net.activate(net.f3, SECOND, plain(net.n2))
    loads["we"].wait()
    msg = exchange.begin()
    for p in range(4):
        net.f1[p] = dot(net.n2[...], net.we[:, p * W : (p + 1) * W])
        net.measure(msg, p, net.f1.at[p], False, net.h3.at[p])
        net.put(msg, 4 + p, side_sums[p])
    exchange.start(8)
    exchange.middle()
    exchange.last()
    total = exchange.finish()
    for p in range(8):
        net.moments(total, p, THIRD + p)

    def join(p, group):
        a3, b3 = net.affine(THIRD + p, group)
        a4, b4 = net.affine(SIDE + p, group)
        return a3, a4, b3 + b4

    for p in range(4):
        params = [join(p, group) for group in range(2)]

        def join_body(group, index, where, keep, carry, p=p, params=params):
            a3, a4, b = params[group]
            u = net.f1[p, where, :] * a3 + net.hs[p, where, :].astype(jnp.float32) * a4 + b
            net.o1[p, where, :] = keep(gelu(u)).astype(jnp.bfloat16)
            return carry

        net.sweep(join_body, 0)
    loads["wr2"].wait()
    msg = exchange.begin()
    value = dot(net.o1[0], net.wr2[0])
    for p in range(1, 4):
        value = value + dot(net.o1[p], net.wr2[p])
    net.f3[...] = value
    net.measure(msg, 0, net.f3, False, net.h4)
    exchange.start(1)
    exchange.middle()
    exchange.last()
    total = exchange.finish()
    net.moments(total, 0, FOURTH)

    def around(ref):
        def keep(group, index, where, value):
            if group == 0:
                net.t4[pl.ds(pl.multiple_of(index * BLK + net.margin, BLK), BLK), :] = value
            ref[where, :] = value.astype(jnp.bfloat16)

        return keep

    net.activate(net.f3, FOURTH, around(net.small))
    save.wait()
    for tap in range(9):
        i, j = divmod(tap, 3)
        net.shifted(net.t4, net.x.at[tap], i - 1, j - 1)
        net.moved(net.small, top, net.x.at[tap], i - 1, j - 1)
    loads["ws2"].wait()
    msg = exchange.begin()
    net.f3[...] = conv(net.wa)
    net.measure(msg, 0, net.f3, True, net.h5)
    exchange.start(1)
    exchange.middle()
    exchange.last()
    total = exchange.finish()
    net.moments(total, 0, FIFTH)
    net.activate(net.f3, FIFTH, plain(net.n5))
    loads["we2"].wait()
    msg = exchange.begin()
    for p in range(4):
        net.f1[p] = dot(net.n5[...], net.we2[:, p * W : (p + 1) * W])
        net.measure(msg, p, net.f1.at[p], False)
    exchange.start(4)
    exchange.middle()
    exchange.last()
    total = exchange.finish()
    for p in range(4):
        net.moments(total, p, SIXTH + p)
        for place in range(9):
            loads["cot", p, place].wait()
    msg = exchange.begin()
    outs = []
    for p in range(4):
        params = [
            net.affine(SIXTH + p, group) + net.standard(SIXTH + p, group) for group in range(2)
        ]

        def out_body(group, index, where, keep, carry, p=p, params=params):
            scale, offset, a, b = params[group]
            h = net.f1[p, where, :]
            u = h * scale + offset + net.o1[p, where, :].astype(jnp.float32)
            y, slope = gelu_both(u)
            grad = net.gh[p, where, :].astype(jnp.float32) * slope
            net.gh[p, where, :] = y.astype(jnp.bfloat16)
            net.gz[p, where, :] = grad
            first, cross = carry
            return first + net.fold(grad), cross + net.fold(grad * (h * a + b))

        net.put(msg, p, net.sweep(out_body, (net.zeros(), net.zeros())))
        for place in range(9):
            out = pltpu.make_async_copy(
                net.gh.at[p, pl.ds(top + place * net.per, net.per)],
                hbm["y_local"].at[place, :, pl.ds(p * W, W)],
                net.load_sem.at[40 + 9 * p + place],
            )
            out.start()
            outs.append(out)
    exchange.start(4)
    net.gather_wide(net.gh, net.wide)
    out = pltpu.make_async_copy(net.wide, hbm["y_global"], net.load_sem.at[2])
    out.start()
    outs.append(out)
    exchange.middle()
    exchange.last()
    total = exchange.finish()
    for out in outs:
        out.wait()
    for p in range(4):
        net.back_sweep(
            SIXTH + p, total, p, net.gz.at[p], net.f1.at[p], plain(net.gh.at[p])
        )
    value = dot_t(net.gh[0], net.we2[:, 0:W])
    for p in range(1, 4):
        value = value + dot_t(net.gh[p], net.we2[:, p * W : (p + 1) * W])
    net.f3[...] = value
    msg = exchange.begin()
    net.through(msg, 0, FIFTH, net.f3, net.h5, False)
    exchange.start(1)
    for p in range(2):
        net.emit(0, 0, p * W, dot_rows(net.n5[...], net.gh[p]))
    exchange.middle()
    for p in range(2, 4):
        net.emit(0, 0, p * W, dot_rows(net.n5[...], net.gh[p]))
    net.flush(1)
    reduce_step()
    exchange.last()
    total = exchange.finish()
    net.back_sweep(FIFTH, total, 0, net.f3, net.h5, around(net.small))
    for p in range(8):
        loads["short", p] = None
    for tap in range(9):
        i, j = divmod(tap, 3)
        net.shifted(net.t4, net.wb.at[tap], 1 - i, 1 - j)
        net.moved(net.small, top, net.wb.at[tap], 1 - i, 1 - j)
    where = pl.ds(0, rows)
    value = dot_t(net.wb[0, where, :], net.wa[0])
    for tap in range(1, 9):
        value = value + dot_t(net.wb[tap, where, :], net.wa[tap])
    reduce_step()
    net.f3[...] = value
    loads["ws"] = net.load(7, hbm["w_spatial"], net.wa)
    msg = exchange.begin()
    net.through(msg, 0, FOURTH, net.f3, net.h4, True)
    exchange.start(1)
    for tap in range(5):
        net.emit(1, tap * W, 0, dot_rows(net.x[tap], net.small[...]))
    exchange.middle()
    for tap in range(5, 9):
        net.emit(1, tap * W, 0, dot_rows(net.x[tap], net.small[...]))
    net.flush(2)
    reduce_step()
    loads["x"] = pltpu.make_async_copy(hbm["x_keep"], net.x, net.load_sem.at[23])
    loads["x"].start()
    exchange.last()
    total = exchange.finish()
    reduce_step()
    net.back_sweep(FOURTH, total, 0, net.f3, net.h4, plain(net.small))
    msg = exchange.begin()
    for p in range(4):
        net.gz[p] = net.gz[p] + dot_t(net.small[...], net.wr2[p])
        params = [
            join(p, group)
            + net.standard(THIRD + p, group)
            + net.standard(SIDE + p, group)
            for group in range(2)
        ]

        def join_back(group, index, where, keep, carry, p=p, params=params):
            a3, a4, b, sa3, sb3, sa4, sb4 = params[group]
            h3 = net.h3[p, where, :].astype(jnp.float32)
            hs = net.hs[p, where, :].astype(jnp.float32)
            slope = gelu_both(h3 * a3 + hs * a4 + b)[1]
            grad = net.gz[p, where, :] * slope
            net.gz[p, where, :] = grad
            first, cross3, cross4 = carry
            return (
                first + net.fold(grad),
                cross3 + net.fold(grad * (h3 * sa3 + sb3)),
                cross4 + net.fold(grad * (hs * sa4 + sb4)),
            )

        results = net.sweep(join_back, (net.zeros(), net.zeros(), net.zeros()))
        net.put(msg, p, results)
        net.put(msg, 4 + p, results, 1)
    reduce_step()
    exchange.start(8)
    for p in range(2):
        net.emit(2, p * W, 0, dot_rows(net.o1[p], net.small[...]))
    exchange.middle()
    for p in range(2, 4):
        net.emit(2, p * W, 0, dot_rows(net.o1[p], net.small[...]))
    exchange.last()
    net.flush(3)
    reduce_step()
    total = exchange.finish()
    for p in range(4):
        net.back_sweep(THIRD + p, total, p, net.gz.at[p], net.h3.at[p], plain(net.h3.at[p]))
        net.back_sweep(SIDE + p, total, 4 + p, net.gz.at[p], net.hs.at[p], plain(net.hs.at[p]))
    value = dot_t(net.h3[0], net.we[:, 0:W])
    for p in range(1, 4):
        value = value + dot_t(net.h3[p], net.we[:, p * W : (p + 1) * W])
    net.f3[...] = value
    reduce_step()
    msg = exchange.begin()
    net.through(msg, 0, SECOND, net.f3, net.h2, False)
    exchange.start(1)
    for p in range(4):
        net.emit(3, 0, p * W, dot_rows(net.n2[...], net.h3[p]))
    exchange.middle()
    reduce_step()
    for k in range(2):
        for p in range(4):
            net.emit(4, k * W, p * W, dot_rows(net.pixels(0, k), net.hs[p]))
    exchange.last()
    net.flush(5)
    reduce_step()
    total = exchange.finish()
    reduce_step()
    net.back_sweep(SECOND, total, 0, net.f3, net.h2, around(net.small))
    for s in range(4):
        net.shifted(net.t4, net.wb.at[s], s // 2, s % 2)
        net.moved(net.small, top, net.wb.at[s], s // 2, s % 2)
    loads["ws"].wait()
    msg = exchange.begin()
    results = None
    for plane in range(4):
        value = None
        for tap in range(9):
            i, j = divmod(tap, 3)
            if 2 * (i != 1) + (j != 1) == plane:
                term = dot_t(net.wb[2 * (i == 0) + (j == 0), where, :], net.wa[tap])
                value = term if value is None else value + term
        net.f1[plane] = value
        new = net.through(msg, None, FIRST, net.f1.at[plane], net.h1.at[plane], True)
        results = new if results is None else jax.tree.map(jnp.add, results, new)
    reduce_step()
    net.put(msg, 0, results)
    for k in range(2):
        for p in range(4):
            loads["short", 4 * k + p] = net.load(
                8 + 4 * k + p,
                hbm["w_short"].at[pl.ds(k * W, W), pl.ds(p * W, W)],
                net.wb.at[4 * k + p],
            )
    exchange.start(1)
    loads["x"].wait()
    for tap in range(5):
        net.emit(5, tap * W, 0, dot_rows(net.x[tap], net.small[...]))
    exchange.middle()
    for tap in range(5, 9):
        net.emit(5, tap * W, 0, dot_rows(net.x[tap], net.small[...]))
    exchange.last()
    net.flush(6)
    reduce_step()
    total = exchange.finish()
    reduce_step()
    for plane in range(4):
        net.back_sweep(
            FIRST, total, 0, net.f1.at[plane], net.h1.at[plane], plain(net.h1.at[plane]), 4
        )
    for k in range(2):
        value = dot_rows(net.pixels(0, k), net.h1[0])
        for plane in range(1, 4):
            value = value + dot_rows(net.pixels(plane, k), net.h1[plane])
        net.emit(6, k * W, 0, value)
    net.flush(7)
    reduce_step()
    outs = []
    for plane in range(4):
        for k in range(2):
            value = dot_t(net.h1[plane], net.wr[k * W : (k + 1) * W, :])
            if plane == 0:
                for p in range(4):
                    if k == 0:
                        loads["short", p].wait()
                        loads["short", 4 + p].wait()
                    value = value + dot_t(net.hs[p], net.wb[4 * k + p])
            value = value.astype(jnp.bfloat16).reshape(rows // BLK, BLK, W)
            net.img[plane, :, :, k * W : (k + 1) * W] = value
        for row in range(3):
            out = pltpu.make_async_copy(
                net.img.at[plane, pl.ds(edge + 3 * wide * row, 3 * wide)],
                hbm["grad_local"].at[row, plane // 2, :, plane % 2],
                net.load_sem.at[24 + 3 * plane + row],
            )
            out.start()
            outs.append(out)
        if plane % 2:
            net.gather_image(plane // 2)
            out = pltpu.make_async_copy(
                net.raw.at[plane // 2],
                hbm["grad_global"].at[:, plane // 2],
                net.load_sem.at[plane // 2],
            )
            out.start()
            outs.append(out)
            reduce_step()
    while reducer.busy():
        reduce_step()
    for out in outs:
        out.wait()


HBM_IN = (
    "image_global",
    "image_local",
    "cot_global",
    "cot_local",
    "w_reduce",
    "w_spatial",
    "w_expand",
    "w_short",
    "w_reduce2",
    "w_spatial2",
    "w_expand2",
    "gain_mid",
    "shift_mid",
    "gain_wide",
    "shift_wide",
)
HBM_OUT = ("y_global", "y_local", "grad_global", "grad_local")
SHAPES = ((512, 2048), (4608, 512), (2048, 512), (512, 2048), (1024, 2048), (4608, 512), (1024, 512))


def whole_kernel(sizes, geometry, names, half, *refs):
    x_bits, dp_bits, _ = bit_counts(sizes)
    steps = x_bits + dp_bits
    place = [0]

    def some(number):
        start = place[0]
        place[0] += number
        return refs[start : place[0]]

    hbm = dict(zip(HBM_IN, some(len(HBM_IN))))
    hbm.update(zip(HBM_OUT, some(len(HBM_OUT))))
    outs = some(7)
    small = some(4)
    grads = some(7)
    (hbm["x_keep"],) = some(1)
    parts = dict(zip(names, some(len(names))))
    exchange = Exchange(sizes, some(7))
    lanes = len(axis_orders(sizes))
    rest = some(2 + lanes * steps + 6)
    landings = [rest[2 + steps * i : 2 + steps * (i + 1)] for i in range(lanes)]
    scratch = (rest[0], rest[1], landings) + tuple(rest[2 + lanes * steps :])
    reducer = Reducer(sizes, SHAPES, half, grads, outs, scratch)
    net = Net(sizes, geometry, parts)
    net.hbm, net.grads = hbm, grads
    net.dgain, net.dshift = (small[0], small[2]), (small[1], small[3])

    def entry():
        semaphore = pltpu.get_barrier_semaphore()
        dp_size, grp_size = sizes
        for k in range(1, grp_size):
            pl.semaphore_signal(
                semaphore, inc=1, device_id=(reducer.dp, reducer.grp ^ k), device_id_type=MESH_ID
            )
        for k in range(1, dp_size):
            pl.semaphore_signal(
                semaphore, inc=1, device_id=(reducer.dp ^ k, reducer.grp), device_id_type=MESH_ID
            )
        pl.semaphore_wait(semaphore, dp_size + grp_size - 2)

    net.entry = entry
    network(net, exchange, reducer)


def run_network(arrays, weights, norms, crops, per):
    sizes = (lax.axis_size("dp"), lax.axis_size("grp"))
    dp_size, grp_size = sizes
    dp_bits = dp_size.bit_length() - 1
    half = 256 // dp_size
    rows = crops * 56 + 9 * per
    margin = -(-9 * crops // BLK) * BLK
    bf16, f32 = jnp.bfloat16, jnp.float32
    scratch = {
        "img": pltpu.VMEM((4, rows // BLK, BLK, 1024), bf16),
        "h1": pltpu.VMEM((4, rows, W), bf16),
        "x": pltpu.VMEM((9, rows, W), bf16),
        "f1": pltpu.VMEM((4, rows, W), f32),
        "h3": pltpu.VMEM((4, rows, W), bf16),
        "hs": pltpu.VMEM((4, rows, W), bf16),
        "o1": pltpu.VMEM((4, rows, W), bf16),
        "h2": pltpu.VMEM((rows, W), bf16),
        "h4": pltpu.VMEM((rows, W), bf16),
        "h5": pltpu.VMEM((rows, W), bf16),
        "n2": pltpu.VMEM((rows, W), bf16),
        "n5": pltpu.VMEM((rows, W), bf16),
        "small": pltpu.VMEM((rows, W), bf16),
        "gz": pltpu.VMEM((4, rows, W), f32),
        "gh": pltpu.VMEM((4, rows, W), bf16),
        "t4": pltpu.VMEM((crops * 56 + 2 * margin, W), f32),
        "nl": pltpu.VMEM((4, 9 * per, W), bf16),
        "f3": pltpu.VMEM((rows, W), f32),
        "stage": pltpu.VMEM((2, W, W), f32),
        "wr": pltpu.VMEM((1024, W), bf16),
        "we": pltpu.VMEM((W, 2048), bf16),
        "wr2": pltpu.VMEM((4, W, W), bf16),
        "we2": pltpu.VMEM((W, 2048), bf16),
        "wa": pltpu.VMEM((9, W, W), bf16),
        "wb": pltpu.VMEM((9, W, W), bf16),
        "gain": pltpu.VMEM((16, 1, W), f32),
        "shift": pltpu.VMEM((16, 1, W), f32),
        "mom": pltpu.VMEM((16, 4, W), f32),
        "raw": pltpu.VMEM((2, 7, 14, crops, 1024), bf16),
        "wide": pltpu.VMEM((7, 7, crops, 2048), bf16),
        "turn": pltpu.VMEM((2, 8 * crops, 1024), f32),
        "load_sem": pltpu.SemaphoreType.DMA((76,)),
        "stage_sem": pltpu.SemaphoreType.DMA((2, 32)),
    }
    own = 8 if 8 % grp_size else max(8 // grp_size, 4 if 4 % grp_size else 4 // grp_size)
    peers = max(sizes)
    exchange = [
        pltpu.VMEM((2, 8, 4, W), f32),
        pltpu.VMEM((2, grp_size, own, 4, W), f32),
        pltpu.VMEM((2, own, 4, W), f32),
        pltpu.VMEM((2, dp_size, own, 4, W), f32),
        pltpu.VMEM((2, 8, 4, W), f32),
        pltpu.SemaphoreType.DMA((2, 3, peers)),
        pltpu.SemaphoreType.DMA((2, 3, peers)),
    ]
    anywhere = pl.BlockSpec(memory_space=pl.ANY)
    inside = pl.BlockSpec(memory_space=pltpu.VMEM)
    shape = jax.ShapeDtypeStruct
    out_shape = (
        [
            shape((7, 7, crops, 2048), bf16),
            shape((9, per, 2048), bf16),
            shape((7, 2, 14, crops, 1024), bf16),
            shape((3, 2, 3, 2, per, 1024), bf16),
        ]
        + [shape((r // dp_size, c), f32) for r, c in SHAPES]
        + [shape((4, W), f32)] * 2
        + [shape((3, 2048), f32)] * 2
        + [shape((2,) * dp_bits + (r // dp_size, c), f32) for r, c in SHAPES]
        + [shape((9, rows, W), bf16)]
    )
    return pl.pallas_call(
        functools.partial(whole_kernel, sizes, (crops, per), tuple(scratch), half),
        out_shape=out_shape,
        in_specs=[anywhere] * (len(HBM_IN) - 4) + [inside] * 4,
        out_specs=[anywhere] * 11 + [inside] * 4 + [anywhere] * 8,
        scratch_shapes=list(scratch.values()) + exchange + reducer_scratch(sizes, half),
        compiler_params=pltpu.CompilerParams(
            collective_id=1, has_side_effects=True, vmem_limit_bytes=VMEM_LIMIT
        ),
    )(*arrays, *weights, *norms)


VMEM_LIMIT = 64 * 2**20 - 2**16


def body(
    image_global,
    image_local,
    w_reduce,
    w_spatial,
    w_expand,
    w_short,
    w_reduce2,
    w_spatial2,
    w_expand2,
    gain_mid,
    shift_mid,
    gain_wide,
    shift_wide,
    cotangent_global,
    cotangent_local,
):
    crops, per = image_global.shape[0], image_local.shape[0]
    results = run_network(
        [
            image_global.transpose(1, 2, 0, 3).reshape(7, 2, 14, crops, 1024),
            image_local.transpose(1, 2, 0, 3).reshape(3, 2, 3, 2, per, 1024),
            cotangent_global.transpose(1, 2, 0, 3),
            cotangent_local.transpose(1, 2, 0, 3).reshape(9, per, 2048),
        ],
        [
            w_reduce,
            w_spatial.reshape(9, W, W),
            w_expand,
            w_short,
            w_reduce2.reshape(4, W, W),
            w_spatial2.reshape(9, W, W),
            w_expand2,
        ],
        [gain_mid, shift_mid, gain_wide, shift_wide],
        crops,
        per,
    )
    y_global, y_local, grad_global, grad_local = results[:4]
    expand2, spatial2, reduce2, expand, short, spatial, reduce = results[4:11]
    return (
        y_global.transpose(2, 0, 1, 3),
        y_local.reshape(3, 3, per, 2048).transpose(2, 0, 1, 3),
        grad_global.reshape(14, 14, crops, 1024).transpose(2, 0, 1, 3),
        grad_local.reshape(6, 6, per, 1024).transpose(2, 0, 1, 3),
        reduce,
        spatial,
        expand,
        short,
        reduce2,
        spatial2,
        expand2,
        *results[11:15],
    )


def solution(mesh):
    crops = P(("dp", "grp"), None, None, None)
    in_specs = (crops, crops) + (P(),) * 11 + (crops, crops)
    out_specs = (crops,) * 4 + (P("dp", None),) * 7 + (P(),) * 4
    return jax.shard_map(body, mesh=mesh, in_specs=in_specs, out_specs=out_specs, check_vma=False)
```

```python
import functools
import math

import jax
import jax.numpy as jnp
from jax import lax
from jax.experimental import pallas as pl
from jax.experimental.pallas import tpu as pltpu
from jax.sharding import PartitionSpec as P

EPS = 1e-05
MESH_ID = pl.DeviceIdType.MESH


PANEL = 512
DEPTH = 8


def chunk_list(shapes, dp_size, half):
    chunks = []
    for number, (rows, columns) in enumerate(shapes):
        own = rows // dp_size
        for panel in range(columns // PANEL):
            for start in range(0, own, 2 * half):
                chunks.append((number, start, panel * PANEL))
    return chunks


class Reducer:
    def __init__(self, sizes, shapes, half, weights, outs, scratch):
        dp_size, grp_size = sizes
        self.half = half
        self.weights = weights
        self.outs = outs
        (
            self.acc,
            self.rc,
            self.rd,
            self.fin,
            self.load_sem,
            self.out_sem,
            self.send_sem,
            self.recv_sem,
            self.credit,
        ) = scratch
        self.chunks = chunk_list(shapes, dp_size, half)
        self.dp = lax.axis_index("dp")
        self.grp = lax.axis_index("grp")
        x_bits, dp_bits, y_bits = bit_counts(sizes)
        self.x_bits, self.dp_bits = x_bits, dp_bits
        self.orders = axis_orders(sizes)
        self.steps = x_bits + dp_bits
        self.lanes = len(self.orders) // 2
        self.plan = []
        self.entered = 0
        self.stages = self.steps + x_bits + 3
        self.slots = self.lanes * (self.steps + 2)

    def bit(self, step):
        kind, index = step
        return ((self.grp >> (index + 1)) & 1) if kind == "x" else ((self.dp >> index) & 1)

    def partner(self, step):
        kind, index = step
        if kind == "x":
            return (self.dp, self.grp ^ (2 << index))
        return (self.dp ^ (1 << index), self.grp)

    def sibling(self):
        return (self.dp, self.grp ^ 1)

    def region(self, done, last_flip):
        place = [slice(None)] * self.dp_bits
        width = PANEL
        column = 0
        for number, step in enumerate(done):
            bit = self.bit(step)
            if last_flip and number == len(done) - 1:
                bit = 1 - bit
            if step[0] == "d":
                place[self.dp_bits - 1 - step[1]] = bit
            else:
                width = width // 2
                column = column + bit * width
        return place, column, width

    def view(self, ref, slot, done, flip=False):
        place, column, width = self.region(done, flip)
        if isinstance(column, int):
            cols = pl.ds(column, width)
        else:
            cols = pl.ds(pl.multiple_of(column, width), width)
        return ref.at[(slot, *place, slice(None), cols)]

    def landing(self, k, order, count):
        return self.rd[k % len(self.orders)][count - 1]

    def c_copy(self, k, slot):
        number, start, column = self.chunks[k]
        source = self.weights[number].at[
            (slice(None),) * self.dp_bits
            + (
                pl.ds(start + (1 - self.grp % 2) * self.half, self.half),
                pl.ds(column, PANEL),
            )
        ]
        return pltpu.make_async_remote_copy(
            src_ref=source,
            dst_ref=self.rc.at[k % (2 * self.lanes)],
            send_sem=self.send_sem.at[slot, 0],
            recv_sem=self.recv_sem.at[slot, 0],
            device_id=self.sibling(),
            device_id_type=MESH_ID,
        )

    def load(self, k, slot):
        number, start, column = self.chunks[k]
        source = self.weights[number].at[
            (slice(None),) * self.dp_bits
            + (pl.ds(start + (self.grp % 2) * self.half, self.half), pl.ds(column, PANEL))
        ]
        return pltpu.make_async_copy(source, self.acc.at[slot], self.load_sem.at[slot])

    def d_copy(self, k, slot, count):
        order = self.orders[k % len(self.orders)]
        return pltpu.make_async_remote_copy(
            src_ref=self.view(self.acc, slot, order[:count], True),
            dst_ref=self.landing(k, order, count),
            send_sem=self.send_sem.at[slot, count],
            recv_sem=self.recv_sem.at[slot, count],
            device_id=self.partner(order[count - 1]),
            device_id_type=MESH_ID,
        )

    def x_columns(self, count):
        steps = [("x", i) for i in range(self.x_bits - count)]
        place, column, width = self.region(steps, False)
        if isinstance(column, int):
            return pl.ds(column, width)
        return pl.ds(pl.multiple_of(column, width), width)

    def ag_copy(self, k, slot, count):
        columns = self.x_columns(count)
        block = self.fin.at[slot, :, columns]
        stage = self.steps + 1 + count
        return pltpu.make_async_remote_copy(
            src_ref=block,
            dst_ref=block,
            send_sem=self.send_sem.at[slot, stage],
            recv_sem=self.recv_sem.at[slot, stage],
            device_id=self.partner(("x", self.x_bits - 1 - count)),
            device_id_type=MESH_ID,
        )

    def out_block(self, k):
        number, start, column = self.chunks[k]
        return self.outs[number].at[
            pl.ds(start + (self.grp % 2) * self.half, self.half), pl.ds(column, PANEL)
        ]

    def out_copies(self, k, slot):
        stage = self.stages - 2
        remote = pltpu.make_async_remote_copy(
            src_ref=self.fin.at[slot],
            dst_ref=self.out_block(k),
            send_sem=self.send_sem.at[slot, stage],
            recv_sem=self.recv_sem.at[slot, stage],
            device_id=self.sibling(),
            device_id_type=MESH_ID,
        )
        local = pltpu.make_async_copy(self.fin.at[slot], self.out_block(k), self.out_sem.at[slot])
        return remote, local

    def period(self, stage):
        return 2 * self.lanes if stage <= self.steps else self.slots

    def give(self, k, stage, device):
        period = self.period(stage)
        if k + period < len(self.chunks):
            pl.semaphore_signal(
                self.credit.at[k % period, stage],
                inc=1,
                device_id=device,
                device_id_type=MESH_ID,
            )

    def take(self, k, stage):
        period = self.period(stage)
        if k >= period:
            pl.semaphore_wait(self.credit.at[k % period, stage], 1)

    def add(self, k, slot, order, count, target=None):
        done = order[:count]
        place, column, width = self.region(done, False)
        free = [number for number, value in enumerate(place) if isinstance(value, slice)]
        cols = pl.ds(column, width)
        if not isinstance(column, int):
            cols = pl.ds(pl.multiple_of(column, width), width)

        def one(index, carry):
            where = list(place)
            lead = []
            for position, axis in enumerate(free):
                value = (index >> (len(free) - 1 - position)) & 1
                where[axis] = value
                lead.append(value)
            if count == 0:
                arrived = self.rc[(k % (2 * self.lanes), *lead)]
            else:
                arrived = self.rd[k % len(self.orders)][count - 1][(*lead, slice(None), slice(None))]
            here = (slot, *where, slice(None), cols)
            if target is None:
                self.acc[here] = self.acc[here] + arrived
            else:
                self.fin[slot, :, self.x_columns(0)] = self.acc[here] + arrived
            return carry

        total = 2 ** len(free)
        if total == 1:
            one(0, 0)
        else:
            lax.fori_loop(0, total, one, 0)

    def run(self, k, stage):
        slot = k % self.slots
        order = self.orders[k % len(self.orders)]
        steps = self.steps
        if stage == 0:
            self.load(k, slot).start()
            self.take(k, 0)
            self.c_copy(k, slot).start()
        elif stage <= steps + 1:
            count = stage - 1
            if count == 0:
                self.load(k, slot).wait()
                self.c_copy(k, slot).wait()
            else:
                self.d_copy(k, slot, count).wait()
            self.add(k, slot, order, count, None if count < steps else True)
            device = self.sibling() if count == 0 else self.partner(order[count - 1])
            self.give(k, count, device)
            self.take(k, count + 1)
            if count < steps:
                self.d_copy(k, slot, count + 1).start()
            else:
                self.ag_copy(k, slot, 0).start()
        elif stage <= steps + self.x_bits:
            count = stage - steps - 1
            self.ag_copy(k, slot, count - 1).wait()
            self.take(k, stage)
            self.ag_copy(k, slot, count).start()
        elif stage == self.stages - 2:
            self.ag_copy(k, slot, self.x_bits - 1).wait()
            remote, local = self.out_copies(k, slot)
            remote.start()
            local.start()
        else:
            remote, local = self.out_copies(k, slot)
            remote.wait()
            local.wait()
            for count in range(self.x_bits):
                device = self.partner(("x", self.x_bits - 1 - count))
                self.give(k, steps + 1 + count, device)

    def step(self, weights):
        ready = sum(1 for chunk in self.chunks if chunk[0] < weights)
        after = min(ready, self.entered + self.lanes)
        self.plan.append(list(range(self.entered, after)))
        self.entered = after
        time = len(self.plan) - 1
        for stage in (1, 2, 0, *reversed(range(3, self.stages))):
            if stage <= time:
                for k in self.plan[time - stage]:
                    self.run(k, stage)

    def busy(self):
        recent = self.plan[1 - self.stages :]
        return self.entered < len(self.chunks) or any(recent)


def bit_counts(sizes):
    dp_size, grp_size = sizes
    x_bits = (grp_size // 2).bit_length() - 1
    dp_bits = dp_size.bit_length() - 1
    return x_bits, dp_bits, x_bits


def axis_orders(sizes):
    x_bits, dp_bits, y_bits = bit_counts(sizes)
    xs = [("x", i) for i in range(x_bits)]
    ys = [("d", i) for i in range(y_bits)]
    zs = [("d", i) for i in range(y_bits, dp_bits)]
    first = [xs + ys + zs, ys + zs[:1] + xs + zs[1:], zs[:1] + ys + xs + zs[1:]]
    second = [first[0], ys + xs + zs, first[2]]
    lanes = 3 if x_bits + dp_bits < 5 else 2
    return first[:lanes] + second[:lanes]


def reducer_scratch(sizes, half):
    x_bits, dp_bits, _ = bit_counts(sizes)
    steps = x_bits + dp_bits
    groups = steps + 2
    orders = axis_orders(sizes)
    slots = len(orders) // 2 * groups
    stages = steps + x_bits + 3
    landings = []
    for order in orders:
        for count in range(1, steps + 1):
            done = [step[0] for step in order[:count]]
            lead = (2,) * (dp_bits - done.count("d"))
            width = PANEL >> done.count("x")
            landings.append(pltpu.VMEM(lead + (half, width), jnp.float32))
    block = (slots,) + (2,) * dp_bits + (half, PANEL)
    return [
        pltpu.VMEM(block, jnp.float32),
        pltpu.VMEM((len(orders),) + block[1:], jnp.float32),
        *landings,
        pltpu.VMEM((slots, half, PANEL), jnp.float32),
        pltpu.SemaphoreType.DMA((slots,)),
        pltpu.SemaphoreType.DMA((slots,)),
        pltpu.SemaphoreType.DMA((slots, stages)),
        pltpu.SemaphoreType.DMA((slots, stages)),
        pltpu.SemaphoreType.REGULAR((slots, stages)),
    ]


C0 = math.sqrt(2.0 / math.pi)
C1 = C0 * 0.044715
W = 512
BLK = 16
FIRST, SECOND, THIRD, SIDE, FOURTH, FIFTH, SIXTH = 0, 1, 2, 6, 10, 11, 12


def gelu(u):
    t = jnp.tanh(u * (C0 + C1 * u * u))
    return u * (0.5 + 0.5 * t)


def gelu_both(u):
    square = u * u
    t = jnp.tanh(u * (C0 + C1 * square))
    half = 0.5 + 0.5 * t
    slope = half + 0.5 * u * (1.0 - t * t) * (C0 + 3.0 * C1 * square)
    return u * half, slope


def dot(a, b):
    return lax.dot_general(a, b, (((1,), (0,)), ((), ())), preferred_element_type=jnp.float32)


def dot_t(a, b):
    return lax.dot_general(a, b, (((1,), (1,)), ((), ())), preferred_element_type=jnp.float32)


def dot_rows(a, b):
    return lax.dot_general(a, b, (((0,), (0,)), ((), ())), preferred_element_type=jnp.float32)


H = W // 2


def chip_groups(sizes):
    dp_size, grp_size = sizes
    chips = grp_size // 2
    if dp_size * chips <= 16:
        flips = [(k // chips, 2 * (k % chips)) for k in range(1, dp_size * chips)]
        return [(lambda dp, grp: dp * chips + (grp >> 1), flips)]
    return [
        (lambda dp, grp: grp >> 1, [(0, 2 * k) for k in range(1, chips)]),
        (lambda dp, grp: dp, [(k, 0) for k in range(1, dp_size)]),
    ]


class Totals:
    def __init__(self, ref):
        self.ref = ref

    def row(self, piece, row):
        parts = [self.ref[half, piece, pl.ds(row, 1)] for half in range(2)]
        return jnp.concatenate(parts, axis=1)


class Exchange:
    def __init__(self, sizes, refs):
        self.msg, self.cbuf, self.part, self.bufs, self.tot, self.send, self.recv = refs
        self.dp = lax.axis_index("dp")
        self.grp = lax.axis_index("grp")
        self.core = self.grp % 2
        self.groups = chip_groups(sizes)
        self.halves = self.cbuf.shape[1]
        self.turn = -1
        self.copies = []

    def copy(self, place, source, target, flip):
        result = pltpu.make_async_remote_copy(
            src_ref=source,
            dst_ref=target,
            send_sem=self.send.at[self.turn, place],
            recv_sem=self.recv.at[self.turn, place],
            device_id=(self.dp ^ flip[0], self.grp ^ flip[1]),
            device_id_type=MESH_ID,
        )
        result.start()
        self.copies.append(result)

    def begin(self):
        self.turn = (self.turn + 1) % self.msg.shape[0]
        return self

    def write(self, piece, row, value):
        for half in range(2):
            self.msg[self.turn, half, piece, pl.ds(row, 1)] = value[:, half * H : (half + 1) * H]

    def start(self, pieces, cut=True):
        self.cut = cut
        self.pieces = pl.ds(0, pieces)
        self.number = pieces
        self.taken = range(1 if cut else 2)
        turn = self.turn
        if cut:
            source, target = self.msg.at[turn, 1 - self.core], self.cbuf.at[turn, 0]
            self.copy(0, source.at[self.pieces], target.at[self.pieces], (0, 1))
        else:
            source, target = self.msg.at[turn], self.cbuf.at[turn]
            self.copy(0, source.at[:, self.pieces], target.at[:, self.pieces], (0, 1))

    def wait(self):
        for copy in self.copies:
            copy.wait()
        self.copies = []

    def spread(self, number, read):
        turn = self.turn
        index, flips = self.groups[number]
        mine = index(self.dp, self.grp)
        for half in self.taken:
            for piece in range(self.number):
                value = read(half, piece)
                self.part[turn, number, half, piece] = value
                self.bufs[number][turn, mine, half, piece] = value
        first = 2 + sum(len(group[1]) for group in self.groups[:number])
        halves = pl.ds(0, len(self.taken))
        for k, flip in enumerate(flips):
            self.copy(
                first + k,
                self.part.at[turn, number, halves, self.pieces],
                self.bufs[number].at[turn, mine, halves, self.pieces],
                flip,
            )

    def gathered(self, number):
        count = len(self.groups[number][1]) + 1

        def read(half, piece):
            total = self.bufs[number][self.turn, 0, half, piece]
            for k in range(1, count):
                total = total + self.bufs[number][self.turn, k, half, piece]
            return total

        return read

    def middle(self):
        turn = self.turn
        self.wait()

        def read(half, piece):
            place = self.core if self.cut else half
            return self.msg[turn, place, piece] + self.cbuf[turn, half, piece]

        self.spread(0, read)

    def last(self):
        turn = self.turn
        self.wait()
        for number in range(1, len(self.groups)):
            self.spread(number, self.gathered(number - 1))
            self.wait()
        read = self.gathered(len(self.groups) - 1)
        for half in self.taken:
            for piece in range(self.number):
                self.tot[turn, self.core if self.cut else half, piece] = read(half, piece)
        if self.cut:
            block = self.tot.at[turn, self.core, self.pieces]
            self.copy(1, block, block, (0, 1))

    def finish(self):
        self.wait()
        return Totals(self.tot.at[self.turn])


def exchange_scratch(sizes, pieces, rows, halves, turns):
    groups = chip_groups(sizes)
    copies = 2 + sum(len(group[1]) for group in groups)
    block = (pieces, rows, H)
    return [
        pltpu.VMEM((turns, 2) + block, jnp.float32),
        pltpu.VMEM((turns, halves) + block, jnp.float32),
        pltpu.VMEM((turns, len(groups), halves) + block, jnp.float32),
        *[pltpu.VMEM((turns, len(group[1]) + 1, halves) + block, jnp.float32) for group in groups],
        pltpu.VMEM((turns, 2) + block, jnp.float32),
        pltpu.SemaphoreType.DMA((turns, copies)),
        pltpu.SemaphoreType.DMA((turns, copies)),
    ]


BOTH = (0, 1)


def first_row(group, groups):
    return 2 * group if len(groups) == 2 else 0


class Net:
    def __init__(self, sizes, geometry, refs):
        self.sizes = sizes
        self.devices = sizes[0] * sizes[1]
        self.crops, self.per = geometry
        self.top = self.crops * 56
        self.margin = -(-9 * self.crops // BLK) * BLK
        self.rows = self.top + 9 * self.per
        self.top_blocks = self.top // BLK
        self.blocks = self.rows // BLK
        for name, ref in refs.items():
            setattr(self, name, ref)
        self.slot = 0
        self.done = 0
        self.pending = [[], []]


    def load(self, number, source, target):
        copy = pltpu.make_async_copy(source, target, self.load_sem.at[number])
        copy.start()
        return copy


    def pixels(self, plane, half=None, group=None):
        columns = slice(None) if half is None else slice(half * W, (half + 1) * W)
        low, high = (0, self.rows) if group is None else self.span(group)
        value = self.img[plane, pl.ds(low // BLK, (high - low) // BLK), :, columns]
        return value.reshape(high - low, value.shape[2])

    def spread_image(self, a):
        crops = self.crops

        def one(row, carry):
            for b in range(2):
                for column in range(7):
                    value = self.raw[a, row, 2 * column + b]
                    self.turn[b, pl.ds(crops * column, crops), :] = value.astype(jnp.float32)
                block = self.turn[b].astype(jnp.bfloat16).reshape(-1, BLK, 1024)
                where = pl.ds(row * (8 * crops // BLK), 8 * crops // BLK)
                self.img[2 * a + b, where] = block
            return carry

        lax.fori_loop(0, 7, one, 0)

    def gather_image(self, a):
        crops = self.crops

        def one(row, carry):
            for b in range(2):
                where = pl.ds(row * (8 * crops // BLK), 8 * crops // BLK)
                block = self.img[2 * a + b, where].reshape(8 * crops, 1024)
                self.turn[b] = block.astype(jnp.float32)
                for column in range(7):
                    value = self.turn[b, pl.ds(crops * column, crops), :]
                    self.raw[a, row, 2 * column + b] = value.astype(jnp.bfloat16)
            return carry

        lax.fori_loop(0, 7, one, 0)

    def spread_wide(self, source, target):
        crops = self.crops

        def one(row, carry):
            for half in range(2):
                for column in range(7):
                    value = source[row, column, :, half * 1024 : (half + 1) * 1024]
                    self.turn[half, pl.ds(crops * column, crops), :] = value.astype(jnp.float32)
                for p in range(2):
                    value = self.turn[half, :, p * W : (p + 1) * W].astype(jnp.bfloat16)
                    where = pl.ds(pl.multiple_of(row * 8 * crops, BLK), 8 * crops)
                    target[2 * half + p, where, :] = value
            return carry

        lax.fori_loop(0, 7, one, 0)

    def gather_wide(self, source, target):
        crops = self.crops

        def one(row, carry):
            for half in range(2):
                for p in range(2):
                    where = pl.ds(pl.multiple_of(row * 8 * crops, BLK), 8 * crops)
                    value = source[2 * half + p, where, :].astype(jnp.float32)
                    self.turn[half, :, p * W : (p + 1) * W] = value
                for column in range(7):
                    value = self.turn[half, pl.ds(crops * column, crops), :]
                    target[row, column, :, half * 1024 : (half + 1) * 1024] = value.astype(
                        jnp.bfloat16
                    )
            return carry

        lax.fori_loop(0, 7, one, 0)


    def span(self, group):
        return (0, self.top) if group == 0 else (self.top, self.rows)

    def sweep(self, body, init, groups=BOTH):
        results = {}
        for group in groups:
            low, high = (0, self.top_blocks) if group == 0 else (self.top_blocks, self.blocks)

            def one(index, carry, group=group):
                rows = pl.ds(pl.multiple_of(index * BLK, BLK), BLK)
                return body(group, index, rows, self.keeper(group, index), carry)

            results[group] = lax.fori_loop(low, high, one, init)
        return results

    def keeper(self, group, index):
        if group == 1:
            return lambda value: value
        row = index * BLK + lax.broadcasted_iota(jnp.int32, (BLK, 128), 0)
        valid = row % (8 * self.crops) < 7 * self.crops
        valid = jnp.concatenate([valid.astype(jnp.float32)] * (W // 128), axis=1)
        return lambda value: value * valid

    def zeros(self):
        return jnp.zeros((8, W), jnp.float32)

    @staticmethod
    def fold(value):
        return value[0:8] + value[8:16]

    def put(self, msg, piece, results):
        for group in results:
            row = first_row(group, results)
            first, other = results[group][:2]
            msg.write(piece, row, jnp.sum(first, axis=0, keepdims=True))
            msg.write(piece, row + 1, jnp.sum(other, axis=0, keepdims=True))

    def count(self, group, scale):
        pixels = (49 * self.crops, 9 * self.per)[group]
        return float(pixels * scale * self.devices)

    def moments(self, total, piece, norm, group, scale=1):
        count = self.count(group, scale)
        mean = total.row(piece, 0) / count
        square = total.row(piece, 1) / count
        self.mom[norm, pl.ds(2 * group, 1)] = mean
        self.mom[norm, pl.ds(2 * group + 1, 1)] = lax.rsqrt(square - mean * mean + EPS)

    def affine(self, norm, group):
        mean = self.mom[norm, pl.ds(2 * group, 1)]
        scale = self.mom[norm, pl.ds(2 * group + 1, 1)] * self.gain[norm]
        return scale, self.shift[norm] - mean * scale

    def standard(self, norm, group):
        mean = self.mom[norm, pl.ds(2 * group, 1)]
        deviation = self.mom[norm, pl.ds(2 * group + 1, 1)]
        return deviation, -mean * deviation

    def measure(self, source, masked, groups, store=None):
        def body(group, index, rows, keep, carry):
            value = source[rows, :]
            if store is not None:
                store[rows, :] = value.astype(store.dtype)
            if masked:
                value = keep(value)
            total, square = carry
            return total + self.fold(value), square + self.fold(value * value)

        return self.sweep(body, (self.zeros(), self.zeros()), groups)

    def activate(self, source, norm, target, groups):
        params = {group: self.affine(norm, group) for group in groups}

        def body(group, index, rows, keep, carry):
            scale, offset = params[group]
            target(group, index, rows, keep(gelu(source[rows, :] * scale + offset)))
            return carry

        self.sweep(body, 0, groups)


    def shifted(self, source, target, down, across):
        offset = (8 * down + across) * self.crops
        start = self.margin + offset
        aligned = start // 8 * 8
        skip = start - aligned

        def one(index, carry):
            rows = pl.ds(pl.multiple_of(index * BLK, BLK), BLK)
            if skip:
                value = source[pl.ds(pl.multiple_of(index * BLK + aligned, 8), 24), :]
                value = value[skip : skip + BLK]
            else:
                value = source[pl.ds(pl.multiple_of(index * BLK + aligned, 8), BLK), :]
            target[rows, :] = value.astype(jnp.bfloat16)
            return carry

        lax.fori_loop(0, self.top_blocks, one, 0)

    def moved(self, source, first, target, down, across):
        per = self.per
        for a in range(3):
            for b in range(3):
                here = pl.ds(self.top + (3 * a + b) * per, per)
                if 0 <= a + down < 3 and 0 <= b + across < 3:
                    there = pl.ds(first + (3 * (a + down) + b + across) * per, per)
                    target[here, :] = source[there, :]
                else:
                    target[here, :] = jnp.zeros((per, W), jnp.bfloat16)

    def clear_margins(self, ref):
        zero = jnp.zeros((self.margin, W), jnp.float32)
        ref[pl.ds(0, self.margin), :] = zero
        ref[pl.ds(self.margin + self.top, self.margin), :] = zero

    @staticmethod
    def parameter(norm):
        if norm in (FIRST, SECOND):
            return 0, norm, slice(0, W)
        if norm in (FOURTH, FIFTH):
            return 0, norm - FOURTH + 2, slice(0, W)
        row, panel = (2, norm - SIXTH) if norm >= SIXTH else divmod(norm - THIRD, 4)
        return 1, row, slice(panel * W, (panel + 1) * W)


    def back(self, norm, total, piece, cross):
        kind, row, columns = self.parameter(norm)
        where = (slice(row, row + 1), columns)
        self.dshift[kind][where] = total.row(piece, 0) + total.row(piece, 2)
        self.dgain[kind][where] = total.row(*cross[0]) + total.row(*cross[1])

    def back_params(self, norm, group, total, piece, row, cross, scale):
        count = self.count(group, scale)
        mean_grad = total.row(piece, row) / count
        mean_cross = total.row(*cross) / count
        factor = self.gain[norm] * self.mom[norm, pl.ds(2 * group + 1, 1)]
        return factor, mean_grad, mean_cross

    def back_sweep(
        self, norm, total, piece, grad, hidden, target, scale=1, cross=None, groups=BOTH
    ):
        cross = cross or {group: (piece, first_row(group, groups) + 1) for group in groups}
        if len(groups) == 2:
            self.back(norm, total, piece, cross)
        params = {}
        for group in groups:
            row = first_row(group, groups)
            params[group] = self.back_params(norm, group, total, piece, row, cross[group], scale)
            params[group] += self.standard(norm, group)

        def body(group, index, rows, keep, carry):
            factor, mean_grad, mean_cross, a, b = params[group]
            scaled = hidden[rows, :].astype(jnp.float32) * a + b
            value = factor * (grad[rows, :] - mean_grad - scaled * mean_cross)
            target(group, index, rows, keep(value))
            return carry

        self.sweep(body, 0, groups)

    def through(self, msg, piece, norm, grad, hidden, masked):
        params = [self.affine(norm, group) + self.standard(norm, group) for group in range(2)]

        def body(group, index, rows, keep, carry):
            scale, offset, a, b = params[group]
            value = hidden[rows, :].astype(jnp.float32)
            slope = gelu_both(value * scale + offset)[1]
            result = grad[rows, :] * slope
            if masked:
                result = keep(result)
            grad[rows, :] = result
            first, cross = carry
            return first + self.fold(result), cross + self.fold(result * (value * a + b))

        results = self.sweep(body, (self.zeros(), self.zeros()))
        if piece is not None:
            self.put(msg, piece, results)
        return results


    def emit(self, number, row, column, value):
        slot = self.slot
        self.slot = 1 - slot
        self.drain(slot)
        self.stage[slot] = value
        grads = self.grads[number]
        own = grads.shape[-2]
        bits = len(grads.shape) - 2
        place = row
        while place < row + W:
            owner = place // own
            size = min(own - place % own, row + W - place)
            index = tuple((owner >> (bits - 1 - i)) & 1 for i in range(bits))
            copy = pltpu.make_async_copy(
                self.stage.at[slot, pl.ds(place - row, size)],
                grads.at[index + (pl.ds(place % own, size), pl.ds(column, W))],
                self.stage_sem.at[slot, len(self.pending[slot])],
            )
            copy.start()
            self.pending[slot].append(copy)
            place += size

    def drain(self, slot):
        for copy in self.pending[slot]:
            copy.wait()
        self.pending[slot] = []

    def flush(self, weights):
        self.drain(0)
        self.drain(1)
        self.done = weights


def network(net, exchange, exchanges, sides, reducer):
    rows = net.rows
    top = net.top

    def reduce_step():
        reducer.step(net.done)

    hbm = net.hbm
    loads = {}
    for a in range(2):
        loads["img", a] = net.load(a, hbm["image_global"].at[:, a], net.raw.at[a])
    edge, wide = net.top_blocks, net.per // BLK
    for plane in range(4):
        for row in range(3):
            loads["img", plane, row] = net.load(
                24 + 3 * plane + row,
                hbm["image_local"].at[row, plane // 2, :, plane % 2],
                net.img.at[plane, pl.ds(edge + 3 * wide * row, 3 * wide)],
            )
    loads["wr"] = net.load(4, hbm["w_reduce"], net.wr)

    def load_short():
        for k in range(2):
            for p in range(4):
                loads["short", 4 * k + p] = net.load(
                    8 + 4 * k + p,
                    hbm["w_short"].at[pl.ds(k * W, W), pl.ds(p * W, W)],
                    net.wb.at[4 * k + p],
                )

    net.arrive()
    for plane in range(4):
        net.clear_margins(net.gz.at[plane])
    net.clear_margins(net.t4)
    net.turn[...] = jnp.zeros(net.turn.shape, jnp.float32)
    for norm in range(16):
        kind, row, columns = net.parameter(norm)
        net.gain[norm] = hbm[("gain_mid", "gain_wide")[kind]][row : row + 1, columns]
        net.shift[norm] = hbm[("shift_mid", "shift_wide")[kind]][row : row + 1, columns]

    loads["wr"].wait()

    def plain(ref):
        def keep(group, index, where, value):
            ref[where, :] = value.astype(ref.dtype)

        return keep

    def around(ref):
        def keep(group, index, where, value):
            if group == 0:
                net.t4[pl.ds(pl.multiple_of(index * BLK + net.margin, BLK), BLK), :] = value
            ref[where, :] = value.astype(jnp.bfloat16)

        return keep

    def join(p, group):
        a3, b3 = net.affine(THIRD + p, group)
        a4, b4 = net.affine(SIDE + p, group)
        return a3, a4, b3 + b4

    sixth_totals = {}
    outs = {0: [], 1: []}

    def load_more():
        loads["we"] = net.load(16, hbm["w_expand"], net.we)
        loads["wr2"] = net.load(17, hbm["w_reduce2"], net.wr2)
        loads["we2"] = net.load(18, hbm["w_expand2"], net.we2)
        loads["cot"] = net.load(2, hbm["cot_global"], net.wide)
        for p in range(4):
            for place in range(9):
                loads["cot", p, place] = net.load(
                    40 + 9 * p + place,
                    hbm["cot_local"].at[place, :, pl.ds(p * W, W)],
                    net.gh.at[p, pl.ds(top + place * net.per, net.per)],
                )

    def forward(group):
        exchange, side = exchanges[group], sides[group]
        only = (group,)
        low, high = net.span(group)
        here = pl.ds(low, high - low)
        results = None
        for plane in range(4):
            if group == 0:
                if plane % 2 == 0:
                    loads["img", plane // 2].wait()
                    net.spread_image(plane // 2)
                if plane == 0:
                    load_short()
                    loads["ws"] = net.load(7, hbm["w_spatial"], net.wa)
            else:
                for row in range(3):
                    loads["img", plane, row].wait()
            net.f1[plane, here] = dot(net.pixels(plane, None, group), net.wr[...])
            new = net.measure(net.f1.at[plane], False, only, net.h1.at[plane])
            results = new if results is None else jax.tree.map(jnp.add, results, new)
        net.put(exchange.begin(), 0, results)
        if group == 0:
            net.entered()
        exchange.start(1, False)
        exchange.middle()
        side.begin()
        for p in range(4):
            if group == 0:
                loads["short", p].wait()
                loads["short", 4 + p].wait()
            net.f3[here] = dot(net.pixels(0, 0, group), net.wb[p]) + dot(
                net.pixels(0, 1, group), net.wb[4 + p]
            )
            net.put(side, p, net.measure(net.f3, False, only, net.hs.at[p]))
        if group == 0:
            load_more()
        yield
        exchange.last()
        total = exchange.finish()
        side.start(4)
        net.moments(total, 0, FIRST, group, 4)
        for plane in range(4):

            def keep_first(group, index, where, value, plane=plane):
                if group == 0:
                    there = pl.ds(pl.multiple_of(index * BLK + net.margin, BLK), BLK)
                    net.gz[plane, there, :] = value
                else:
                    there = pl.ds(pl.multiple_of((index - net.top_blocks) * BLK, BLK), BLK)
                    net.nl[plane, there, :] = value.astype(jnp.bfloat16)

            net.activate(net.f1.at[plane], FIRST, keep_first, only)
        side.middle()
        for tap in range(9):
            i, j = divmod(tap, 3)
            plane = 2 * (i != 1) + (j != 1)
            if group == 0:
                net.shifted(net.gz.at[plane], net.x.at[tap], -(i == 0), -(j == 0))
            else:
                net.moved(net.nl.at[plane], 0, net.x.at[tap], -(i == 0), -(j == 0))
        if group == 0:
            loads["ws"].wait()

        def conv():
            total = dot(net.x[0, here], net.wa[0])
            for tap in range(1, 9):
                total = total + dot(net.x[tap, here], net.wa[tap])
            return total

        net.f3[here] = conv()
        net.put(exchange.begin(), 0, net.measure(net.f3, True, only, net.h2))
        exchange.start(1, False)
        exchange.middle()
        if group == 0:
            loads["cot"].wait()
            net.spread_wide(net.wide, net.gh)
        else:
            loads["ws2"] = net.load(7, hbm["w_spatial2"], net.wa)
            loads["x"] = pltpu.make_async_copy(net.x, hbm["x_keep"], net.load_sem.at[23])
            loads["x"].start()
        yield
        exchange.last()
        total = exchange.finish()
        side.last()
        net.moments(total, 0, SECOND, group)
        net.activate(net.f3, SECOND, plain(net.n2), only)
        if group == 0:
            loads["we"].wait()
        exchange.begin()
        for p in range(4):
            net.f1[p, here] = dot(net.n2[here], net.we[:, p * W : (p + 1) * W])
            net.put(exchange, p, net.measure(net.f1.at[p], False, only, net.h3.at[p]))
        exchange.start(4)
        exchange.middle()
        total_side = side.finish()
        for p in range(4):
            net.moments(total_side, p, SIDE + p, group)
        yield
        exchange.last()
        total = exchange.finish()
        for p in range(4):
            net.moments(total, p, THIRD + p, group)
        for p in range(4):
            params = join(p, group)

            def join_body(group, index, where, keep, carry, p=p, params=params):
                a3, a4, b = params
                u = net.f1[p, where, :] * a3 + net.hs[p, where, :].astype(jnp.float32) * a4 + b
                net.o1[p, where, :] = keep(gelu(u)).astype(jnp.bfloat16)
                return carry

            net.sweep(join_body, 0, only)
        if group == 0:
            loads["wr2"].wait()
        value = dot(net.o1[0, here], net.wr2[0])
        for p in range(1, 4):
            value = value + dot(net.o1[p, here], net.wr2[p])
        net.f3[here] = value
        net.put(exchange.begin(), 0, net.measure(net.f3, False, only, net.h4))
        exchange.start(1, False)
        exchange.middle()
        yield
        exchange.last()
        total = exchange.finish()
        net.moments(total, 0, FOURTH, group)
        net.activate(net.f3, FOURTH, around(net.small), only)
        if group == 0:
            loads["x"].wait()
        for tap in range(9):
            i, j = divmod(tap, 3)
            if group == 0:
                net.shifted(net.t4, net.x.at[tap], i - 1, j - 1)
            else:
                net.moved(net.small, top, net.x.at[tap], i - 1, j - 1)
        if group == 0:
            loads["ws2"].wait()
        net.f3[here] = conv()
        net.put(exchange.begin(), 0, net.measure(net.f3, True, only, net.h5))
        exchange.start(1, False)
        exchange.middle()
        yield
        exchange.last()
        total = exchange.finish()
        net.moments(total, 0, FIFTH, group)
        net.activate(net.f3, FIFTH, plain(net.n5), only)
        if group == 0:
            loads["we2"].wait()
        exchange.begin()
        for p in range(4):
            net.f1[p, here] = dot(net.n5[here], net.we2[:, p * W : (p + 1) * W])
            net.put(exchange, p, net.measure(net.f1.at[p], False, only))
        exchange.start(4)
        exchange.middle()
        yield
        exchange.last()
        total = exchange.finish()
        exchange.begin()
        for p in range(4):
            net.moments(total, p, SIXTH + p, group)
            if group == 1:
                for place in range(9):
                    loads["cot", p, place].wait()
            params = net.affine(SIXTH + p, group) + net.standard(SIXTH + p, group)

            def out_body(group, index, where, keep, carry, p=p, params=params):
                scale, offset, a, b = params
                h = net.f1[p, where, :]
                u = h * scale + offset + net.o1[p, where, :].astype(jnp.float32)
                y, slope = gelu_both(u)
                grad = net.gh[p, where, :].astype(jnp.float32) * slope
                net.gh[p, where, :] = y.astype(jnp.bfloat16)
                net.gz[p, where, :] = grad
                first, cross = carry
                return first + net.fold(grad), cross + net.fold(grad * (h * a + b))

            net.put(exchange, p, net.sweep(out_body, (net.zeros(), net.zeros()), only))
        exchange.start(4)
        exchange.middle()
        if group == 0:
            net.gather_wide(net.gh, net.wide)
            out = pltpu.make_async_copy(net.wide, hbm["y_global"], net.load_sem.at[2])
            out.start()
            outs[0].append(out)
        else:
            for p in range(4):
                for place in range(9):
                    out = pltpu.make_async_copy(
                        net.gh.at[p, pl.ds(top + place * net.per, net.per)],
                        hbm["y_local"].at[place, :, pl.ds(p * W, W)],
                        net.load_sem.at[40 + 9 * p + place],
                    )
                    out.start()
                    outs[1].append(out)
        yield
        exchange.last()
        total = exchange.finish()
        sixth_totals[group] = total
        if group == 1:
            for out in outs[1]:
                out.wait()
        for p in range(4):
            net.back_sweep(
                SIXTH + p, total, p, net.gz.at[p], net.f1.at[p], plain(net.gh.at[p]), groups=only
            )

    streams = [forward(0), forward(1)]
    running = True
    while running:
        running = [next(stream, stream) is not stream for stream in streams][1]
    for p in range(4):
        kind, row, columns = net.parameter(SIXTH + p)
        place = (slice(row, row + 1), columns)
        low, high = sixth_totals[0], sixth_totals[1]
        net.dshift[kind][place] = low.row(p, 0) + high.row(p, 0)
        net.dgain[kind][place] = low.row(p, 1) + high.row(p, 1)
    value = dot_t(net.gh[0], net.we2[:, 0:W])
    for p in range(1, 4):
        value = value + dot_t(net.gh[p], net.we2[:, p * W : (p + 1) * W])
    net.f3[...] = value
    msg = exchange.begin()
    net.through(msg, 0, FIFTH, net.f3, net.h5, False)
    exchange.start(1)
    exchange.middle()
    for p in range(2):
        net.emit(0, 0, p * W, dot_rows(net.n5[...], net.gh[p]))
    for p in range(2, 4):
        net.emit(0, 0, p * W, dot_rows(net.n5[...], net.gh[p]))
    net.flush(1)
    reduce_step()
    exchange.last()
    total = exchange.finish()
    net.back_sweep(FIFTH, total, 0, net.f3, net.h5, around(net.small))
    for tap in range(9):
        i, j = divmod(tap, 3)
        net.shifted(net.t4, net.wb.at[tap], 1 - i, 1 - j)
        net.moved(net.small, top, net.wb.at[tap], 1 - i, 1 - j)
    where = pl.ds(0, rows)
    value = dot_t(net.wb[0, where, :], net.wa[0])
    for tap in range(1, 9):
        value = value + dot_t(net.wb[tap, where, :], net.wa[tap])
    reduce_step()
    net.f3[...] = value
    loads["ws"] = net.load(7, hbm["w_spatial"], net.wa)
    msg = exchange.begin()
    net.through(msg, 0, FOURTH, net.f3, net.h4, True)
    exchange.start(1)
    exchange.middle()
    for tap in range(5):
        net.emit(1, tap * W, 0, dot_rows(net.x[tap], net.small[...]))
    for tap in range(5, 9):
        net.emit(1, tap * W, 0, dot_rows(net.x[tap], net.small[...]))
    net.flush(2)
    reduce_step()
    loads["x"] = pltpu.make_async_copy(hbm["x_keep"], net.x, net.load_sem.at[23])
    loads["x"].start()
    exchange.last()
    total = exchange.finish()
    reduce_step()
    net.back_sweep(FOURTH, total, 0, net.f3, net.h4, plain(net.small))
    msg = exchange.begin()
    for p in range(4):
        net.gz[p] = net.gz[p] + dot_t(net.small[...], net.wr2[p])
        params = [
            join(p, group)
            + net.standard(THIRD + p, group)
            + net.standard(SIDE + p, group)
            for group in range(2)
        ]

        def join_back(group, index, where, keep, carry, p=p, params=params):
            a3, a4, b, sa3, sb3, sa4, sb4 = params[group]
            h3 = net.h3[p, where, :].astype(jnp.float32)
            hs = net.hs[p, where, :].astype(jnp.float32)
            slope = gelu_both(h3 * a3 + hs * a4 + b)[1]
            grad = net.gz[p, where, :] * slope
            net.gz[p, where, :] = grad
            first, cross3, cross4 = carry
            return (
                first + net.fold(grad),
                cross3 + net.fold(grad * (h3 * sa3 + sb3)),
                cross4 + net.fold(grad * (hs * sa4 + sb4)),
            )

        results = net.sweep(join_back, (net.zeros(), net.zeros(), net.zeros()))
        net.put(msg, p, results)
        for group in range(2):
            value = jnp.sum(results[group][2], axis=0, keepdims=True)
            msg.write(4 + p // 2, 2 * (p % 2) + group, value)
    reduce_step()
    exchange.start(6)
    exchange.middle()
    for p in range(2):
        net.emit(2, p * W, 0, dot_rows(net.o1[p], net.small[...]))
    for p in range(2, 4):
        net.emit(2, p * W, 0, dot_rows(net.o1[p], net.small[...]))
    exchange.last()
    net.flush(3)
    reduce_step()
    total = exchange.finish()
    for p in range(4):
        net.back_sweep(THIRD + p, total, p, net.gz.at[p], net.h3.at[p], plain(net.h3.at[p]))
        cross = {group: (4 + p // 2, 2 * (p % 2) + group) for group in BOTH}
        net.back_sweep(
            SIDE + p, total, p, net.gz.at[p], net.hs.at[p], plain(net.hs.at[p]), cross=cross
        )
    value = dot_t(net.h3[0], net.we[:, 0:W])
    for p in range(1, 4):
        value = value + dot_t(net.h3[p], net.we[:, p * W : (p + 1) * W])
    net.f3[...] = value
    reduce_step()
    msg = exchange.begin()
    net.through(msg, 0, SECOND, net.f3, net.h2, False)
    exchange.start(1)
    exchange.middle()
    for p in range(4):
        net.emit(3, 0, p * W, dot_rows(net.n2[...], net.h3[p]))
    reduce_step()
    for k in range(2):
        for p in range(4):
            net.emit(4, k * W, p * W, dot_rows(net.pixels(0, k), net.hs[p]))
    exchange.last()
    net.flush(5)
    reduce_step()
    total = exchange.finish()
    reduce_step()
    net.back_sweep(SECOND, total, 0, net.f3, net.h2, around(net.small))
    for s in range(4):
        net.shifted(net.t4, net.wb.at[s], s // 2, s % 2)
        net.moved(net.small, top, net.wb.at[s], s // 2, s % 2)
    loads["ws"].wait()
    msg = exchange.begin()
    results = None
    for plane in range(4):
        value = None
        for tap in range(9):
            i, j = divmod(tap, 3)
            if 2 * (i != 1) + (j != 1) == plane:
                term = dot_t(net.wb[2 * (i == 0) + (j == 0), where, :], net.wa[tap])
                value = term if value is None else value + term
        net.f1[plane] = value
        new = net.through(msg, None, FIRST, net.f1.at[plane], net.h1.at[plane], True)
        results = new if results is None else jax.tree.map(jnp.add, results, new)
    reduce_step()
    net.put(msg, 0, results)
    for k in range(2):
        for p in range(4):
            loads["short", 4 * k + p] = net.load(
                8 + 4 * k + p,
                hbm["w_short"].at[pl.ds(k * W, W), pl.ds(p * W, W)],
                net.wb.at[4 * k + p],
            )
    exchange.start(1)
    exchange.middle()
    loads["x"].wait()
    for tap in range(5):
        net.emit(5, tap * W, 0, dot_rows(net.x[tap], net.small[...]))
    for tap in range(5, 9):
        net.emit(5, tap * W, 0, dot_rows(net.x[tap], net.small[...]))
    exchange.last()
    net.flush(6)
    reduce_step()
    total = exchange.finish()
    reduce_step()
    for plane in range(4):
        net.back_sweep(
            FIRST, total, 0, net.f1.at[plane], net.h1.at[plane], plain(net.h1.at[plane]), 4
        )
    for k in range(2):
        value = dot_rows(net.pixels(0, k), net.h1[0])
        for plane in range(1, 4):
            value = value + dot_rows(net.pixels(plane, k), net.h1[plane])
        net.emit(6, k * W, 0, value)
    net.flush(7)
    reduce_step()
    outs = outs[0]
    for plane in range(4):
        for k in range(2):
            value = dot_t(net.h1[plane], net.wr[k * W : (k + 1) * W, :])
            if plane == 0:
                for p in range(4):
                    if k == 0:
                        loads["short", p].wait()
                        loads["short", 4 + p].wait()
                    value = value + dot_t(net.hs[p], net.wb[4 * k + p])
            value = value.astype(jnp.bfloat16).reshape(rows // BLK, BLK, W)
            net.img[plane, :, :, k * W : (k + 1) * W] = value
        for row in range(3):
            out = pltpu.make_async_copy(
                net.img.at[plane, pl.ds(edge + 3 * wide * row, 3 * wide)],
                hbm["grad_local"].at[row, plane // 2, :, plane % 2],
                net.load_sem.at[24 + 3 * plane + row],
            )
            out.start()
            outs.append(out)
        if plane % 2:
            net.gather_image(plane // 2)
            out = pltpu.make_async_copy(
                net.raw.at[plane // 2],
                hbm["grad_global"].at[:, plane // 2],
                net.load_sem.at[plane // 2],
            )
            out.start()
            outs.append(out)
            reduce_step()
    while reducer.busy():
        reduce_step()
    for out in outs:
        out.wait()


HBM_IN = (
    "image_global",
    "image_local",
    "cot_global",
    "cot_local",
    "w_reduce",
    "w_spatial",
    "w_expand",
    "w_short",
    "w_reduce2",
    "w_spatial2",
    "w_expand2",
    "gain_mid",
    "shift_mid",
    "gain_wide",
    "shift_wide",
)
HBM_OUT = ("y_global", "y_local", "grad_global", "grad_local")
SHAPES = ((512, 2048), (4608, 512), (2048, 512), (512, 2048), (1024, 2048), (4608, 512), (1024, 512))


def whole_kernel(sizes, geometry, names, half, *refs):
    x_bits, dp_bits, _ = bit_counts(sizes)
    steps = x_bits + dp_bits
    place = [0]

    def some(number):
        start = place[0]
        place[0] += number
        return refs[start : place[0]]

    hbm = dict(zip(HBM_IN, some(len(HBM_IN))))
    hbm.update(zip(HBM_OUT, some(len(HBM_OUT))))
    outs = some(7)
    small = some(4)
    grads = some(7)
    (hbm["x_keep"],) = some(1)
    parts = dict(zip(names, some(len(names))))
    groups = len(chip_groups(sizes))

    def some_exchange():
        taken = some(6 + groups)
        return Exchange(sizes, (*taken[:3], taken[3 : 3 + groups], *taken[3 + groups :]))

    exchange, *others = [some_exchange() for _ in range(5)]
    lanes = len(axis_orders(sizes))
    rest = some(2 + lanes * steps + 6)
    landings = [rest[2 + steps * i : 2 + steps * (i + 1)] for i in range(lanes)]
    scratch = (rest[0], rest[1], landings) + tuple(rest[2 + lanes * steps :])
    reducer = Reducer(sizes, SHAPES, half, grads, outs, scratch)
    net = Net(sizes, geometry, parts)
    net.hbm, net.grads = hbm, grads
    net.dgain, net.dshift = (small[0], small[2]), (small[1], small[3])

    flips = [(0, 1)] + [flip for group in chip_groups(sizes) for flip in group[1]]
    semaphore = pltpu.get_barrier_semaphore()

    def arrive():
        for down, across in flips:
            device = (reducer.dp ^ down, reducer.grp ^ across)
            pl.semaphore_signal(semaphore, inc=1, device_id=device, device_id_type=MESH_ID)

    def entered():
        pl.semaphore_wait(semaphore, len(flips))

    net.arrive, net.entered = arrive, entered
    network(net, exchange, others[:2], others[2:], reducer)


def settle_kernel(*refs):
    count = (len(refs) - 2) // 3
    ins, outs, held = refs[:count], refs[count : 2 * count], refs[2 * count : 3 * count]
    first = [pltpu.make_async_copy(ins[i], held[i], refs[-2].at[i]) for i in range(count)]
    second = [pltpu.make_async_copy(held[i], outs[i], refs[-1].at[i]) for i in range(count)]
    for copy in first:
        copy.start()
    for i in range(count):
        first[i].wait()
        second[i].start()
    for copy in second:
        copy.wait()


def settle(values):
    anywhere = pl.BlockSpec(memory_space=pl.ANY)
    count = len(values)
    return pl.pallas_call(
        settle_kernel,
        out_shape=[jax.ShapeDtypeStruct(value.shape, value.dtype) for value in values],
        in_specs=[anywhere] * count,
        out_specs=[anywhere] * count,
        scratch_shapes=[pltpu.VMEM(value.shape, value.dtype) for value in values]
        + [pltpu.SemaphoreType.DMA((count,))] * 2,
        compiler_params=pltpu.CompilerParams(vmem_limit_bytes=VMEM_LIMIT),
    )(*values)


def run_network(arrays, weights, norms, crops, per):
    sizes = (lax.axis_size("dp"), lax.axis_size("grp"))
    dp_size, grp_size = sizes
    dp_bits = dp_size.bit_length() - 1
    half = 256 // dp_size
    rows = crops * 56 + 9 * per
    margin = -(-9 * crops // BLK) * BLK
    bf16, f32 = jnp.bfloat16, jnp.float32
    scratch = {
        "img": pltpu.VMEM((4, rows // BLK, BLK, 1024), bf16),
        "h1": pltpu.VMEM((4, rows, W), bf16),
        "x": pltpu.VMEM((9, rows, W), bf16),
        "f1": pltpu.VMEM((4, rows, W), f32),
        "h3": pltpu.VMEM((4, rows, W), bf16),
        "hs": pltpu.VMEM((4, rows, W), bf16),
        "o1": pltpu.VMEM((4, rows, W), bf16),
        "h2": pltpu.VMEM((rows, W), bf16),
        "h4": pltpu.VMEM((rows, W), bf16),
        "h5": pltpu.VMEM((rows, W), bf16),
        "n2": pltpu.VMEM((rows, W), bf16),
        "n5": pltpu.VMEM((rows, W), bf16),
        "small": pltpu.VMEM((rows, W), bf16),
        "gz": pltpu.VMEM((4, rows, W), f32),
        "gh": pltpu.VMEM((4, rows, W), bf16),
        "t4": pltpu.VMEM((crops * 56 + 2 * margin, W), f32),
        "nl": pltpu.VMEM((4, 9 * per, W), bf16),
        "f3": pltpu.VMEM((rows, W), f32),
        "stage": pltpu.VMEM((2, W, W), f32),
        "wr": pltpu.VMEM((1024, W), bf16),
        "we": pltpu.VMEM((W, 2048), bf16),
        "wr2": pltpu.VMEM((4, W, W), bf16),
        "we2": pltpu.VMEM((W, 2048), bf16),
        "wa": pltpu.VMEM((9, W, W), bf16),
        "wb": pltpu.VMEM((9, W, W), bf16),
        "gain": pltpu.VMEM((16, 1, W), f32),
        "shift": pltpu.VMEM((16, 1, W), f32),
        "mom": pltpu.VMEM((16, 4, W), f32),
        "raw": pltpu.VMEM((2, 7, 14, crops, 1024), bf16),
        "wide": pltpu.VMEM((7, 7, crops, 2048), bf16),
        "turn": pltpu.VMEM((2, 8 * crops, 1024), f32),
        "load_sem": pltpu.SemaphoreType.DMA((76,)),
        "stage_sem": pltpu.SemaphoreType.DMA((2, 32)),
    }
    exchange = exchange_scratch(sizes, 6, 4, 1, 2)
    for _ in range(2):
        exchange += exchange_scratch(sizes, 4, 2, 2, 2)
    for _ in range(2):
        exchange += exchange_scratch(sizes, 4, 2, 1, 1)
    anywhere = pl.BlockSpec(memory_space=pl.ANY)
    inside = pl.BlockSpec(memory_space=pltpu.VMEM)
    shape = jax.ShapeDtypeStruct
    out_shape = (
        [
            shape((7, 7, crops, 2048), bf16),
            shape((9, per, 2048), bf16),
            shape((7, 2, 14, crops, 1024), bf16),
            shape((3, 2, 3, 2, per, 1024), bf16),
        ]
        + [shape((r // dp_size, c), f32) for r, c in SHAPES]
        + [shape((4, W), f32)] * 2
        + [shape((3, 2048), f32)] * 2
        + [shape((2,) * dp_bits + (r // dp_size, c), f32) for r, c in SHAPES]
        + [shape((9, rows, W), bf16)]
    )
    return pl.pallas_call(
        functools.partial(whole_kernel, sizes, (crops, per), tuple(scratch), half),
        out_shape=out_shape,
        in_specs=[anywhere] * (len(HBM_IN) - 4) + [inside] * 4,
        out_specs=[anywhere] * 11 + [inside] * 4 + [anywhere] * 8,
        scratch_shapes=list(scratch.values()) + exchange + reducer_scratch(sizes, half),
        compiler_params=pltpu.CompilerParams(
            collective_id=1, has_side_effects=True, vmem_limit_bytes=VMEM_LIMIT
        ),
    )(*arrays, *weights, *norms)


VMEM_LIMIT = 64 * 2**20 - 2**16


def body(
    image_global,
    image_local,
    w_reduce,
    w_spatial,
    w_expand,
    w_short,
    w_reduce2,
    w_spatial2,
    w_expand2,
    gain_mid,
    shift_mid,
    gain_wide,
    shift_wide,
    cotangent_global,
    cotangent_local,
):
    crops, per = image_global.shape[0], image_local.shape[0]
    results = run_network(
        [
            image_global.transpose(1, 2, 0, 3).reshape(7, 2, 14, crops, 1024),
            image_local.transpose(1, 2, 0, 3).reshape(3, 2, 3, 2, per, 1024),
            cotangent_global.transpose(1, 2, 0, 3),
            cotangent_local.transpose(1, 2, 0, 3).reshape(9, per, 2048),
        ],
        [
            w_reduce,
            w_spatial.reshape(9, W, W),
            w_expand,
            w_short,
            w_reduce2.reshape(4, W, W),
            w_spatial2.reshape(9, W, W),
            w_expand2,
        ],
        [gain_mid, shift_mid, gain_wide, shift_wide],
        crops,
        per,
    )
    results = settle(results[:15])
    y_global, y_local, grad_global, grad_local = results[:4]
    expand2, spatial2, reduce2, expand, short, spatial, reduce = results[4:11]
    return (
        y_global.transpose(2, 0, 1, 3),
        y_local.reshape(3, 3, per, 2048).transpose(2, 0, 1, 3),
        grad_global.reshape(14, 14, crops, 1024).transpose(2, 0, 1, 3),
        grad_local.reshape(6, 6, per, 1024).transpose(2, 0, 1, 3),
        reduce,
        spatial,
        expand,
        short,
        reduce2,
        spatial2,
        expand2,
        *results[11:15],
    )


def solution(mesh):
    crops = P(("dp", "grp"), None, None, None)
    in_specs = (crops, crops) + (P(),) * 11 + (crops, crops)
    out_specs = (crops,) * 4 + (P("dp", None),) * 7 + (P(),) * 4
    return jax.shard_map(body, mesh=mesh, in_specs=in_specs, out_specs=out_specs, check_vma=False)
```

```python
import functools
import math

import jax
import jax.numpy as jnp
from jax import lax
from jax.experimental import pallas as pl
from jax.experimental.pallas import tpu as pltpu
from jax.sharding import PartitionSpec as P

EPS = 1e-05
MESH_ID = pl.DeviceIdType.MESH


PANEL = 512
DEPTH = 8


def chunk_list(shapes, dp_size, half):
    chunks = []
    for number, (rows, columns) in enumerate(shapes):
        own = rows // dp_size
        for panel in range(columns // PANEL):
            for start in range(0, own, 2 * half):
                chunks.append((number, start, panel * PANEL))
    return chunks


class Reducer:
    def __init__(self, sizes, shapes, half, weights, outs, scratch):
        dp_size, grp_size = sizes
        self.half = half
        self.weights = weights
        self.outs = outs
        (
            self.acc,
            self.rc,
            self.rd,
            self.fin,
            self.load_sem,
            self.out_sem,
            self.send_sem,
            self.recv_sem,
            self.credit,
        ) = scratch
        self.chunks = chunk_list(shapes, dp_size, half)
        self.dp = lax.axis_index("dp")
        self.grp = lax.axis_index("grp")
        x_bits, dp_bits, y_bits = bit_counts(sizes)
        self.x_bits, self.dp_bits = x_bits, dp_bits
        self.orders = axis_orders(sizes)
        self.steps = x_bits + dp_bits
        self.lanes = len(self.orders) // 2
        self.plan = []
        self.entered = 0
        self.stages = self.steps + x_bits + 3
        self.slots = self.lanes * (self.steps + 2)

    def bit(self, step):
        kind, index = step
        return ((self.grp >> (index + 1)) & 1) if kind == "x" else ((self.dp >> index) & 1)

    def partner(self, step):
        kind, index = step
        if kind == "x":
            return (self.dp, self.grp ^ (2 << index))
        return (self.dp ^ (1 << index), self.grp)

    def sibling(self):
        return (self.dp, self.grp ^ 1)

    def region(self, done, last_flip):
        place = [slice(None)] * self.dp_bits
        width = PANEL
        column = 0
        for number, step in enumerate(done):
            bit = self.bit(step)
            if last_flip and number == len(done) - 1:
                bit = 1 - bit
            if step[0] == "d":
                place[self.dp_bits - 1 - step[1]] = bit
            else:
                width = width // 2
                column = column + bit * width
        return place, column, width

    def view(self, ref, slot, done, flip=False):
        place, column, width = self.region(done, flip)
        if isinstance(column, int):
            cols = pl.ds(column, width)
        else:
            cols = pl.ds(pl.multiple_of(column, width), width)
        return ref.at[(slot, *place, slice(None), cols)]

    def landing(self, k, order, count):
        return self.rd[k % len(self.orders)][count - 1]

    def c_copy(self, k, slot):
        number, start, column = self.chunks[k]
        source = self.weights[number].at[
            (slice(None),) * self.dp_bits
            + (
                pl.ds(start + (1 - self.grp % 2) * self.half, self.half),
                pl.ds(column, PANEL),
            )
        ]
        return pltpu.make_async_remote_copy(
            src_ref=source,
            dst_ref=self.rc.at[k % (2 * self.lanes)],
            send_sem=self.send_sem.at[slot, 0],
            recv_sem=self.recv_sem.at[slot, 0],
            device_id=self.sibling(),
            device_id_type=MESH_ID,
        )

    def load(self, k, slot):
        number, start, column = self.chunks[k]
        source = self.weights[number].at[
            (slice(None),) * self.dp_bits
            + (pl.ds(start + (self.grp % 2) * self.half, self.half), pl.ds(column, PANEL))
        ]
        return pltpu.make_async_copy(source, self.acc.at[slot], self.load_sem.at[slot])

    def d_copy(self, k, slot, count):
        order = self.orders[k % len(self.orders)]
        return pltpu.make_async_remote_copy(
            src_ref=self.view(self.acc, slot, order[:count], True),
            dst_ref=self.landing(k, order, count),
            send_sem=self.send_sem.at[slot, count],
            recv_sem=self.recv_sem.at[slot, count],
            device_id=self.partner(order[count - 1]),
            device_id_type=MESH_ID,
        )

    def x_columns(self, count):
        steps = [("x", i) for i in range(self.x_bits - count)]
        place, column, width = self.region(steps, False)
        if isinstance(column, int):
            return pl.ds(column, width)
        return pl.ds(pl.multiple_of(column, width), width)

    def ag_copy(self, k, slot, count):
        columns = self.x_columns(count)
        block = self.fin.at[slot, :, columns]
        stage = self.steps + 1 + count
        return pltpu.make_async_remote_copy(
            src_ref=block,
            dst_ref=block,
            send_sem=self.send_sem.at[slot, stage],
            recv_sem=self.recv_sem.at[slot, stage],
            device_id=self.partner(("x", self.x_bits - 1 - count)),
            device_id_type=MESH_ID,
        )

    def out_block(self, k):
        number, start, column = self.chunks[k]
        return self.outs[number].at[
            pl.ds(start + (self.grp % 2) * self.half, self.half), pl.ds(column, PANEL)
        ]

    def out_copies(self, k, slot):
        stage = self.stages - 2
        remote = pltpu.make_async_remote_copy(
            src_ref=self.fin.at[slot],
            dst_ref=self.out_block(k),
            send_sem=self.send_sem.at[slot, stage],
            recv_sem=self.recv_sem.at[slot, stage],
            device_id=self.sibling(),
            device_id_type=MESH_ID,
        )
        local = pltpu.make_async_copy(self.fin.at[slot], self.out_block(k), self.out_sem.at[slot])
        return remote, local

    def period(self, stage):
        return 2 * self.lanes if stage <= self.steps else self.slots

    def give(self, k, stage, device):
        period = self.period(stage)
        if k + period < len(self.chunks):
            pl.semaphore_signal(
                self.credit.at[k % period, stage],
                inc=1,
                device_id=device,
                device_id_type=MESH_ID,
            )

    def take(self, k, stage):
        period = self.period(stage)
        if k >= period:
            pl.semaphore_wait(self.credit.at[k % period, stage], 1)

    def add(self, k, slot, order, count, target=None):
        done = order[:count]
        place, column, width = self.region(done, False)
        free = [number for number, value in enumerate(place) if isinstance(value, slice)]
        cols = pl.ds(column, width)
        if not isinstance(column, int):
            cols = pl.ds(pl.multiple_of(column, width), width)

        def one(index, carry):
            where = list(place)
            lead = []
            for position, axis in enumerate(free):
                value = (index >> (len(free) - 1 - position)) & 1
                where[axis] = value
                lead.append(value)
            if count == 0:
                arrived = self.rc[(k % (2 * self.lanes), *lead)]
            else:
                arrived = self.rd[k % len(self.orders)][count - 1][(*lead, slice(None), slice(None))]
            here = (slot, *where, slice(None), cols)
            if target is None:
                self.acc[here] = self.acc[here] + arrived
            else:
                self.fin[slot, :, self.x_columns(0)] = self.acc[here] + arrived
            return carry

        total = 2 ** len(free)
        if total == 1:
            one(0, 0)
        else:
            lax.fori_loop(0, total, one, 0)

    def run(self, k, stage):
        slot = k % self.slots
        order = self.orders[k % len(self.orders)]
        steps = self.steps
        if stage == 0:
            self.load(k, slot).start()
            self.take(k, 0)
            self.c_copy(k, slot).start()
        elif stage <= steps + 1:
            count = stage - 1
            if count == 0:
                self.load(k, slot).wait()
                self.c_copy(k, slot).wait()
            else:
                self.d_copy(k, slot, count).wait()
            self.add(k, slot, order, count, None if count < steps else True)
            device = self.sibling() if count == 0 else self.partner(order[count - 1])
            self.give(k, count, device)
            self.take(k, count + 1)
            if count < steps:
                self.d_copy(k, slot, count + 1).start()
            else:
                self.ag_copy(k, slot, 0).start()
        elif stage <= steps + self.x_bits:
            count = stage - steps - 1
            self.ag_copy(k, slot, count - 1).wait()
            self.take(k, stage)
            self.ag_copy(k, slot, count).start()
        elif stage == self.stages - 2:
            self.ag_copy(k, slot, self.x_bits - 1).wait()
            remote, local = self.out_copies(k, slot)
            remote.start()
            local.start()
        else:
            remote, local = self.out_copies(k, slot)
            remote.wait()
            local.wait()
            for count in range(self.x_bits):
                device = self.partner(("x", self.x_bits - 1 - count))
                self.give(k, steps + 1 + count, device)

    def step(self, weights):
        ready = sum(1 for chunk in self.chunks if chunk[0] < weights)
        after = min(ready, self.entered + self.lanes)
        self.plan.append(list(range(self.entered, after)))
        self.entered = after
        time = len(self.plan) - 1
        for stage in (1, 2, 0, *reversed(range(3, self.stages))):
            if stage <= time:
                for k in self.plan[time - stage]:
                    self.run(k, stage)

    def busy(self):
        recent = self.plan[1 - self.stages :]
        return self.entered < len(self.chunks) or any(recent)


def bit_counts(sizes):
    dp_size, grp_size = sizes
    x_bits = (grp_size // 2).bit_length() - 1
    dp_bits = dp_size.bit_length() - 1
    return x_bits, dp_bits, x_bits


def axis_orders(sizes):
    x_bits, dp_bits, y_bits = bit_counts(sizes)
    xs = [("x", i) for i in range(x_bits)]
    ys = [("d", i) for i in range(y_bits)]
    zs = [("d", i) for i in range(y_bits, dp_bits)]
    first = [xs + ys + zs, ys + zs[:1] + xs + zs[1:], zs[:1] + ys + xs + zs[1:]]
    second = [first[0], ys + xs + zs, first[2]]
    lanes = 3 if x_bits + dp_bits < 5 else 2
    return first[:lanes] + second[:lanes]


def reducer_scratch(sizes, half):
    x_bits, dp_bits, _ = bit_counts(sizes)
    steps = x_bits + dp_bits
    groups = steps + 2
    orders = axis_orders(sizes)
    slots = len(orders) // 2 * groups
    stages = steps + x_bits + 3
    landings = []
    for order in orders:
        for count in range(1, steps + 1):
            done = [step[0] for step in order[:count]]
            lead = (2,) * (dp_bits - done.count("d"))
            width = PANEL >> done.count("x")
            landings.append(pltpu.VMEM(lead + (half, width), jnp.float32))
    block = (slots,) + (2,) * dp_bits + (half, PANEL)
    return [
        pltpu.VMEM(block, jnp.float32),
        pltpu.VMEM((len(orders),) + block[1:], jnp.float32),
        *landings,
        pltpu.VMEM((slots, half, PANEL), jnp.float32),
        pltpu.SemaphoreType.DMA((slots,)),
        pltpu.SemaphoreType.DMA((slots,)),
        pltpu.SemaphoreType.DMA((slots, stages)),
        pltpu.SemaphoreType.DMA((slots, stages)),
        pltpu.SemaphoreType.REGULAR((slots, stages)),
    ]


C0 = math.sqrt(2.0 / math.pi)
C1 = C0 * 0.044715
W = 512
BLK = 16
FIRST, SECOND, THIRD, SIDE, FOURTH, FIFTH, SIXTH = 0, 1, 2, 6, 10, 11, 12


def gelu(u):
    t = jnp.tanh(u * (C0 + C1 * u * u))
    return u * (0.5 + 0.5 * t)


def gelu_both(u):
    square = u * u
    t = jnp.tanh(u * (C0 + C1 * square))
    half = 0.5 + 0.5 * t
    slope = half + 0.5 * u * (1.0 - t * t) * (C0 + 3.0 * C1 * square)
    return u * half, slope


def dot(a, b):
    return lax.dot_general(a, b, (((1,), (0,)), ((), ())), preferred_element_type=jnp.float32)


def dot_t(a, b):
    return lax.dot_general(a, b, (((1,), (1,)), ((), ())), preferred_element_type=jnp.float32)


def dot_rows(a, b):
    return lax.dot_general(a, b, (((0,), (0,)), ((), ())), preferred_element_type=jnp.float32)


H = W // 2


def chip_groups(sizes):
    dp_size, grp_size = sizes
    chips = grp_size // 2
    if dp_size * chips <= 16:
        flips = [(k // chips, 2 * (k % chips)) for k in range(1, dp_size * chips)]
        return [(lambda dp, grp: dp * chips + (grp >> 1), flips)]
    return [
        (lambda dp, grp: grp >> 1, [(0, 2 * k) for k in range(1, chips)]),
        (lambda dp, grp: dp, [(k, 0) for k in range(1, dp_size)]),
    ]


class Totals:
    def __init__(self, ref):
        self.ref = ref

    def row(self, piece, row):
        parts = [self.ref[half, piece, pl.ds(row, 1)] for half in range(2)]
        return jnp.concatenate(parts, axis=1)


class Exchange:
    def __init__(self, sizes, refs):
        self.msg, self.cbuf, self.part, self.bufs, self.tot, self.send, self.recv = refs
        self.dp = lax.axis_index("dp")
        self.grp = lax.axis_index("grp")
        self.core = self.grp % 2
        self.groups = chip_groups(sizes)
        self.halves = self.cbuf.shape[1]
        self.turn = -1
        self.copies = []

    def copy(self, place, source, target, flip):
        result = pltpu.make_async_remote_copy(
            src_ref=source,
            dst_ref=target,
            send_sem=self.send.at[self.turn, place],
            recv_sem=self.recv.at[self.turn, place],
            device_id=(self.dp ^ flip[0], self.grp ^ flip[1]),
            device_id_type=MESH_ID,
        )
        result.start()
        self.copies.append(result)

    def begin(self):
        self.turn = (self.turn + 1) % self.msg.shape[0]
        return self

    def write(self, piece, row, value):
        for half in range(2):
            self.msg[self.turn, half, piece, pl.ds(row, 1)] = value[:, half * H : (half + 1) * H]

    def start(self, pieces, cut=True):
        self.cut = cut
        self.pieces = pl.ds(0, pieces)
        self.number = pieces
        self.taken = range(1 if cut else 2)
        turn = self.turn
        if cut:
            source, target = self.msg.at[turn, 1 - self.core], self.cbuf.at[turn, 0]
            self.copy(0, source.at[self.pieces], target.at[self.pieces], (0, 1))
        else:
            source, target = self.msg.at[turn], self.cbuf.at[turn]
            self.copy(0, source.at[:, self.pieces], target.at[:, self.pieces], (0, 1))

    def wait(self):
        for copy in self.copies:
            copy.wait()
        self.copies = []

    def spread(self, number, read):
        turn = self.turn
        index, flips = self.groups[number]
        mine = index(self.dp, self.grp)
        for half in self.taken:
            for piece in range(self.number):
                value = read(half, piece)
                self.part[turn, number, half, piece] = value
                self.bufs[number][turn, mine, half, piece] = value
        first = 2 + sum(len(group[1]) for group in self.groups[:number])
        halves = pl.ds(0, len(self.taken))
        for k, flip in enumerate(flips):
            self.copy(
                first + k,
                self.part.at[turn, number, halves, self.pieces],
                self.bufs[number].at[turn, mine, halves, self.pieces],
                flip,
            )

    def gathered(self, number):
        count = len(self.groups[number][1]) + 1

        def read(half, piece):
            total = self.bufs[number][self.turn, 0, half, piece]
            for k in range(1, count):
                total = total + self.bufs[number][self.turn, k, half, piece]
            return total

        return read

    def middle(self):
        turn = self.turn
        self.wait()

        def read(half, piece):
            place = self.core if self.cut else half
            return self.msg[turn, place, piece] + self.cbuf[turn, half, piece]

        self.spread(0, read)

    def last(self):
        turn = self.turn
        self.wait()
        for number in range(1, len(self.groups)):
            self.spread(number, self.gathered(number - 1))
            self.wait()
        read = self.gathered(len(self.groups) - 1)
        for half in self.taken:
            for piece in range(self.number):
                self.tot[turn, self.core if self.cut else half, piece] = read(half, piece)
        if self.cut:
            block = self.tot.at[turn, self.core, self.pieces]
            self.copy(1, block, block, (0, 1))

    def finish(self):
        self.wait()
        return Totals(self.tot.at[self.turn])


def exchange_scratch(sizes, pieces, rows, halves, turns):
    groups = chip_groups(sizes)
    copies = 2 + sum(len(group[1]) for group in groups)
    block = (pieces, rows, H)
    return [
        pltpu.VMEM((turns, 2) + block, jnp.float32),
        pltpu.VMEM((turns, halves) + block, jnp.float32),
        pltpu.VMEM((turns, len(groups), halves) + block, jnp.float32),
        *[pltpu.VMEM((turns, len(group[1]) + 1, halves) + block, jnp.float32) for group in groups],
        pltpu.VMEM((turns, 2) + block, jnp.float32),
        pltpu.SemaphoreType.DMA((turns, copies)),
        pltpu.SemaphoreType.DMA((turns, copies)),
    ]


BOTH = (0, 1)


def first_row(group, groups):
    return 2 * group if len(groups) == 2 else 0


class Net:
    def __init__(self, sizes, geometry, refs):
        self.sizes = sizes
        self.devices = sizes[0] * sizes[1]
        self.crops, self.per = geometry
        self.top = self.crops * 56
        self.margin = -(-9 * self.crops // BLK) * BLK
        self.rows = self.top + 9 * self.per
        self.top_blocks = self.top // BLK
        self.blocks = self.rows // BLK
        for name, ref in refs.items():
            setattr(self, name, ref)
        self.slot = 0
        self.done = 0
        self.pending = [[], []]


    def load(self, number, source, target):
        copy = pltpu.make_async_copy(source, target, self.load_sem.at[number])
        copy.start()
        return copy


    def pixels(self, plane, half=None, group=None):
        columns = slice(None) if half is None else slice(half * W, (half + 1) * W)
        low, high = (0, self.rows) if group is None else self.span(group)
        value = self.img[plane, pl.ds(low // BLK, (high - low) // BLK), :, columns]
        return value.reshape(high - low, value.shape[2])

    def spread_image(self, a):
        crops = self.crops

        def one(row, carry):
            for b in range(2):
                for column in range(7):
                    value = self.raw[a, row, 2 * column + b]
                    self.turn[b, pl.ds(crops * column, crops), :] = value.astype(jnp.float32)
                block = self.turn[b].astype(jnp.bfloat16).reshape(-1, BLK, 1024)
                where = pl.ds(row * (8 * crops // BLK), 8 * crops // BLK)
                self.img[2 * a + b, where] = block
            return carry

        lax.fori_loop(0, 7, one, 0)

    def gather_image(self, a):
        crops = self.crops

        def one(row, carry):
            for b in range(2):
                where = pl.ds(row * (8 * crops // BLK), 8 * crops // BLK)
                block = self.img[2 * a + b, where].reshape(8 * crops, 1024)
                self.turn[b] = block.astype(jnp.float32)
                for column in range(7):
                    value = self.turn[b, pl.ds(crops * column, crops), :]
                    self.raw[a, row, 2 * column + b] = value.astype(jnp.bfloat16)
            return carry

        lax.fori_loop(0, 7, one, 0)

    def spread_wide(self, source, target):
        crops = self.crops

        def one(row, carry):
            for half in range(2):
                for column in range(7):
                    value = source[row, column, :, half * 1024 : (half + 1) * 1024]
                    self.turn[half, pl.ds(crops * column, crops), :] = value.astype(jnp.float32)
                for p in range(2):
                    value = self.turn[half, :, p * W : (p + 1) * W].astype(jnp.bfloat16)
                    where = pl.ds(pl.multiple_of(row * 8 * crops, BLK), 8 * crops)
                    target[2 * half + p, where, :] = value
            return carry

        lax.fori_loop(0, 7, one, 0)

    def gather_wide(self, source, target):
        crops = self.crops

        def one(row, carry):
            for half in range(2):
                for p in range(2):
                    where = pl.ds(pl.multiple_of(row * 8 * crops, BLK), 8 * crops)
                    value = source[2 * half + p, where, :].astype(jnp.float32)
                    self.turn[half, :, p * W : (p + 1) * W] = value
                for column in range(7):
                    value = self.turn[half, pl.ds(crops * column, crops), :]
                    target[row, column, :, half * 1024 : (half + 1) * 1024] = value.astype(
                        jnp.bfloat16
                    )
            return carry

        lax.fori_loop(0, 7, one, 0)


    def span(self, group):
        return (0, self.top) if group == 0 else (self.top, self.rows)

    def sweep(self, body, init, groups=BOTH):
        results = {}
        for group in groups:
            low, high = (0, self.top_blocks) if group == 0 else (self.top_blocks, self.blocks)

            def one(index, carry, group=group):
                rows = pl.ds(pl.multiple_of(index * BLK, BLK), BLK)
                return body(group, index, rows, self.keeper(group, index), carry)

            results[group] = lax.fori_loop(low, high, one, init)
        return results

    def keeper(self, group, index):
        if group == 1:
            return lambda value: value
        row = index * BLK + lax.broadcasted_iota(jnp.int32, (BLK, 128), 0)
        valid = row % (8 * self.crops) < 7 * self.crops
        valid = jnp.concatenate([valid.astype(jnp.float32)] * (W // 128), axis=1)
        return lambda value: value * valid

    def zeros(self):
        return jnp.zeros((8, W), jnp.float32)

    @staticmethod
    def fold(value):
        return value[0:8] + value[8:16]

    def put(self, msg, piece, results):
        for group in results:
            row = first_row(group, results)
            first, other = results[group][:2]
            msg.write(piece, row, jnp.sum(first, axis=0, keepdims=True))
            msg.write(piece, row + 1, jnp.sum(other, axis=0, keepdims=True))

    def count(self, group, scale):
        pixels = (49 * self.crops, 9 * self.per)[group]
        return float(pixels * scale * self.devices)

    def moments(self, total, piece, norm, group, scale=1):
        count = self.count(group, scale)
        mean = total.row(piece, 0) / count
        square = total.row(piece, 1) / count
        self.mom[norm, pl.ds(2 * group, 1)] = mean
        self.mom[norm, pl.ds(2 * group + 1, 1)] = lax.rsqrt(square - mean * mean + EPS)

    def affine(self, norm, group):
        mean = self.mom[norm, pl.ds(2 * group, 1)]
        scale = self.mom[norm, pl.ds(2 * group + 1, 1)] * self.gain[norm]
        return scale, self.shift[norm] - mean * scale

    def standard(self, norm, group):
        mean = self.mom[norm, pl.ds(2 * group, 1)]
        deviation = self.mom[norm, pl.ds(2 * group + 1, 1)]
        return deviation, -mean * deviation

    def measure(self, source, masked, groups, store=None):
        def body(group, index, rows, keep, carry):
            value = source[rows, :]
            if store is not None:
                store[rows, :] = value.astype(store.dtype)
            if masked:
                value = keep(value)
            total, square = carry
            return total + self.fold(value), square + self.fold(value * value)

        return self.sweep(body, (self.zeros(), self.zeros()), groups)

    def activate(self, source, norm, target, groups):
        params = {group: self.affine(norm, group) for group in groups}

        def body(group, index, rows, keep, carry):
            scale, offset = params[group]
            target(group, index, rows, keep(gelu(source[rows, :] * scale + offset)))
            return carry

        self.sweep(body, 0, groups)


    def shifted(self, source, target, down, across):
        offset = (8 * down + across) * self.crops
        start = self.margin + offset
        aligned = start // 8 * 8
        skip = start - aligned

        def one(index, carry):
            rows = pl.ds(pl.multiple_of(index * BLK, BLK), BLK)
            if skip:
                value = source[pl.ds(pl.multiple_of(index * BLK + aligned, 8), 24), :]
                value = value[skip : skip + BLK]
            else:
                value = source[pl.ds(pl.multiple_of(index * BLK + aligned, 8), BLK), :]
            target[rows, :] = value.astype(jnp.bfloat16)
            return carry

        lax.fori_loop(0, self.top_blocks, one, 0)

    def moved(self, source, first, target, down, across):
        per = self.per
        for a in range(3):
            for b in range(3):
                here = pl.ds(self.top + (3 * a + b) * per, per)
                if 0 <= a + down < 3 and 0 <= b + across < 3:
                    there = pl.ds(first + (3 * (a + down) + b + across) * per, per)
                    target[here, :] = source[there, :]
                else:
                    target[here, :] = jnp.zeros((per, W), jnp.bfloat16)

    def clear_margins(self, ref):
        zero = jnp.zeros((self.margin, W), jnp.float32)
        ref[pl.ds(0, self.margin), :] = zero
        ref[pl.ds(self.margin + self.top, self.margin), :] = zero

    @staticmethod
    def parameter(norm):
        if norm in (FIRST, SECOND):
            return 0, norm, slice(0, W)
        if norm in (FOURTH, FIFTH):
            return 0, norm - FOURTH + 2, slice(0, W)
        row, panel = (2, norm - SIXTH) if norm >= SIXTH else divmod(norm - THIRD, 4)
        return 1, row, slice(panel * W, (panel + 1) * W)


    def back(self, norm, total, piece, cross):
        kind, row, columns = self.parameter(norm)
        where = (slice(row, row + 1), columns)
        self.dshift[kind][where] = total.row(piece, 0) + total.row(piece, 2)
        self.dgain[kind][where] = total.row(*cross[0]) + total.row(*cross[1])

    def back_params(self, norm, group, total, piece, row, cross, scale):
        count = self.count(group, scale)
        mean_grad = total.row(piece, row) / count
        mean_cross = total.row(*cross) / count
        factor = self.gain[norm] * self.mom[norm, pl.ds(2 * group + 1, 1)]
        return factor, mean_grad, mean_cross

    def back_sweep(
        self, norm, total, piece, grad, hidden, target, scale=1, cross=None, groups=BOTH
    ):
        cross = cross or {group: (piece, first_row(group, groups) + 1) for group in groups}
        if len(groups) == 2:
            self.back(norm, total, piece, cross)
        params = {}
        for group in groups:
            row = first_row(group, groups)
            params[group] = self.back_params(norm, group, total, piece, row, cross[group], scale)
            params[group] += self.standard(norm, group)

        def body(group, index, rows, keep, carry):
            factor, mean_grad, mean_cross, a, b = params[group]
            scaled = hidden[rows, :].astype(jnp.float32) * a + b
            value = factor * (grad[rows, :] - mean_grad - scaled * mean_cross)
            target(group, index, rows, keep(value))
            return carry

        self.sweep(body, 0, groups)

    def through(self, msg, piece, norm, grad, hidden, masked):
        params = [self.affine(norm, group) + self.standard(norm, group) for group in range(2)]

        def body(group, index, rows, keep, carry):
            scale, offset, a, b = params[group]
            value = hidden[rows, :].astype(jnp.float32)
            slope = gelu_both(value * scale + offset)[1]
            result = grad[rows, :] * slope
            if masked:
                result = keep(result)
            grad[rows, :] = result
            first, cross = carry
            return first + self.fold(result), cross + self.fold(result * (value * a + b))

        results = self.sweep(body, (self.zeros(), self.zeros()))
        if piece is not None:
            self.put(msg, piece, results)
        return results


    def emit(self, number, row, column, value):
        slot = self.slot
        self.slot = 1 - slot
        self.drain(slot)
        self.stage[slot] = value
        grads = self.grads[number]
        own = grads.shape[-2]
        bits = len(grads.shape) - 2
        place = row
        while place < row + W:
            owner = place // own
            size = min(own - place % own, row + W - place)
            index = tuple((owner >> (bits - 1 - i)) & 1 for i in range(bits))
            copy = pltpu.make_async_copy(
                self.stage.at[slot, pl.ds(place - row, size)],
                grads.at[index + (pl.ds(place % own, size), pl.ds(column, W))],
                self.stage_sem.at[slot, len(self.pending[slot])],
            )
            copy.start()
            self.pending[slot].append(copy)
            place += size

    def drain(self, slot):
        for copy in self.pending[slot]:
            copy.wait()
        self.pending[slot] = []

    def flush(self, weights):
        self.drain(0)
        self.drain(1)
        self.done = weights


def network(net, exchange, exchanges, sides, reducer):
    rows = net.rows
    top = net.top

    def reduce_step():
        reducer.step(net.done)

    hbm = net.hbm
    loads = {}
    for a in range(2):
        loads["img", a] = net.load(a, hbm["image_global"].at[:, a], net.raw.at[a])
    edge, wide = net.top_blocks, net.per // BLK
    for plane in range(4):
        for row in range(3):
            loads["img", plane, row] = net.load(
                24 + 3 * plane + row,
                hbm["image_local"].at[row, plane // 2, :, plane % 2],
                net.img.at[plane, pl.ds(edge + 3 * wide * row, 3 * wide)],
            )
    loads["wr"] = net.load(4, hbm["w_reduce"], net.wr)

    def load_short():
        for k in range(2):
            for p in range(4):
                loads["short", 4 * k + p] = net.load(
                    8 + 4 * k + p,
                    hbm["w_short"].at[pl.ds(k * W, W), pl.ds(p * W, W)],
                    net.wb.at[4 * k + p],
                )

    net.arrive()
    for plane in range(4):
        net.clear_margins(net.gz.at[plane])
    net.clear_margins(net.t4)
    net.turn[...] = jnp.zeros(net.turn.shape, jnp.float32)
    for norm in range(16):
        kind, row, columns = net.parameter(norm)
        net.gain[norm] = hbm[("gain_mid", "gain_wide")[kind]][row : row + 1, columns]
        net.shift[norm] = hbm[("shift_mid", "shift_wide")[kind]][row : row + 1, columns]

    loads["wr"].wait()

    def plain(ref):
        def keep(group, index, where, value):
            ref[where, :] = value.astype(ref.dtype)

        return keep

    def around(ref):
        def keep(group, index, where, value):
            if group == 0:
                net.t4[pl.ds(pl.multiple_of(index * BLK + net.margin, BLK), BLK), :] = value
            ref[where, :] = value.astype(jnp.bfloat16)

        return keep

    def join(p, group):
        a3, b3 = net.affine(THIRD + p, group)
        a4, b4 = net.affine(SIDE + p, group)
        return a3, a4, b3 + b4

    sixth_totals = {}
    outs = {0: [], 1: []}

    def load_more():
        loads["we"] = net.load(16, hbm["w_expand"], net.we)
        loads["wr2"] = net.load(17, hbm["w_reduce2"], net.wr2)
        loads["we2"] = net.load(18, hbm["w_expand2"], net.we2)
        loads["cot"] = net.load(2, hbm["cot_global"], net.wide)
        for p in range(4):
            for place in range(9):
                loads["cot", p, place] = net.load(
                    40 + 9 * p + place,
                    hbm["cot_local"].at[place, :, pl.ds(p * W, W)],
                    net.gh.at[p, pl.ds(top + place * net.per, net.per)],
                )

    def forward(group):
        exchange, side = exchanges[group], sides[group]
        only = (group,)
        low, high = net.span(group)
        here = pl.ds(low, high - low)
        results = None
        for plane in range(4):
            if group == 0:
                if plane % 2 == 0:
                    loads["img", plane // 2].wait()
                    net.spread_image(plane // 2)
                if plane == 0:
                    load_short()
                    loads["ws"] = net.load(7, hbm["w_spatial"], net.wa)
            else:
                for row in range(3):
                    loads["img", plane, row].wait()
            net.f1[plane, here] = dot(net.pixels(plane, None, group), net.wr[...])
            new = net.measure(net.f1.at[plane], False, only, net.h1.at[plane])
            results = new if results is None else jax.tree.map(jnp.add, results, new)
        net.put(exchange.begin(), 0, results)
        if group == 0:
            net.entered()
        exchange.start(1, False)
        exchange.middle()
        side.begin()
        for p in range(4):
            if group == 0:
                loads["short", p].wait()
                loads["short", 4 + p].wait()
            net.f3[here] = dot(net.pixels(0, 0, group), net.wb[p]) + dot(
                net.pixels(0, 1, group), net.wb[4 + p]
            )
            net.put(side, p, net.measure(net.f3, False, only, net.hs.at[p]))
        if group == 0:
            load_more()
        yield
        exchange.last()
        total = exchange.finish()
        side.start(4)
        net.moments(total, 0, FIRST, group, 4)
        for plane in range(4):

            def keep_first(group, index, where, value, plane=plane):
                if group == 0:
                    there = pl.ds(pl.multiple_of(index * BLK + net.margin, BLK), BLK)
                    net.gz[plane, there, :] = value
                else:
                    there = pl.ds(pl.multiple_of((index - net.top_blocks) * BLK, BLK), BLK)
                    net.nl[plane, there, :] = value.astype(jnp.bfloat16)

            net.activate(net.f1.at[plane], FIRST, keep_first, only)
        side.middle()
        for tap in range(9):
            i, j = divmod(tap, 3)
            plane = 2 * (i != 1) + (j != 1)
            if group == 0:
                net.shifted(net.gz.at[plane], net.x.at[tap], -(i == 0), -(j == 0))
            else:
                net.moved(net.nl.at[plane], 0, net.x.at[tap], -(i == 0), -(j == 0))
        if group == 0:
            loads["ws"].wait()

        def conv():
            total = dot(net.x[0, here], net.wa[0])
            for tap in range(1, 9):
                total = total + dot(net.x[tap, here], net.wa[tap])
            return total

        net.f3[here] = conv()
        net.put(exchange.begin(), 0, net.measure(net.f3, True, only, net.h2))
        exchange.start(1, False)
        exchange.middle()
        if group == 0:
            loads["cot"].wait()
            net.spread_wide(net.wide, net.gh)
        else:
            loads["ws2"] = net.load(7, hbm["w_spatial2"], net.wa)
            loads["x"] = pltpu.make_async_copy(net.x, hbm["x_keep"], net.load_sem.at[23])
            loads["x"].start()
        yield
        exchange.last()
        total = exchange.finish()
        side.last()
        net.moments(total, 0, SECOND, group)
        net.activate(net.f3, SECOND, plain(net.n2), only)
        if group == 0:
            loads["we"].wait()
        exchange.begin()
        for p in range(4):
            net.f1[p, here] = dot(net.n2[here], net.we[:, p * W : (p + 1) * W])
            net.put(exchange, p, net.measure(net.f1.at[p], False, only, net.h3.at[p]))
        exchange.start(4)
        exchange.middle()
        total_side = side.finish()
        for p in range(4):
            net.moments(total_side, p, SIDE + p, group)
        yield
        exchange.last()
        total = exchange.finish()
        for p in range(4):
            net.moments(total, p, THIRD + p, group)
        for p in range(4):
            params = join(p, group)

            def join_body(group, index, where, keep, carry, p=p, params=params):
                a3, a4, b = params
                u = net.f1[p, where, :] * a3 + net.hs[p, where, :].astype(jnp.float32) * a4 + b
                net.o1[p, where, :] = keep(gelu(u)).astype(jnp.bfloat16)
                return carry

            net.sweep(join_body, 0, only)
        if group == 0:
            loads["wr2"].wait()
        value = dot(net.o1[0, here], net.wr2[0])
        for p in range(1, 4):
            value = value + dot(net.o1[p, here], net.wr2[p])
        net.f3[here] = value
        net.put(exchange.begin(), 0, net.measure(net.f3, False, only, net.h4))
        exchange.start(1, False)
        exchange.middle()
        yield
        exchange.last()
        total = exchange.finish()
        net.moments(total, 0, FOURTH, group)
        net.activate(net.f3, FOURTH, around(net.small), only)
        if group == 0:
            loads["x"].wait()
        for tap in range(9):
            i, j = divmod(tap, 3)
            if group == 0:
                net.shifted(net.t4, net.x.at[tap], i - 1, j - 1)
            else:
                net.moved(net.small, top, net.x.at[tap], i - 1, j - 1)
        if group == 0:
            loads["ws2"].wait()
        net.f3[here] = conv()
        net.put(exchange.begin(), 0, net.measure(net.f3, True, only, net.h5))
        exchange.start(1, False)
        exchange.middle()
        yield
        exchange.last()
        total = exchange.finish()
        net.moments(total, 0, FIFTH, group)
        net.activate(net.f3, FIFTH, plain(net.n5), only)
        if group == 0:
            loads["we2"].wait()
        exchange.begin()
        for p in range(4):
            net.f1[p, here] = dot(net.n5[here], net.we2[:, p * W : (p + 1) * W])
            net.put(exchange, p, net.measure(net.f1.at[p], False, only))
        exchange.start(4)
        exchange.middle()
        yield
        exchange.last()
        total = exchange.finish()
        exchange.begin()
        for p in range(4):
            net.moments(total, p, SIXTH + p, group)
            if group == 1:
                for place in range(9):
                    loads["cot", p, place].wait()
            params = net.affine(SIXTH + p, group) + net.standard(SIXTH + p, group)

            def out_body(group, index, where, keep, carry, p=p, params=params):
                scale, offset, a, b = params
                h = net.f1[p, where, :]
                u = h * scale + offset + net.o1[p, where, :].astype(jnp.float32)
                y, slope = gelu_both(u)
                grad = net.gh[p, where, :].astype(jnp.float32) * slope
                net.gh[p, where, :] = y.astype(jnp.bfloat16)
                net.gz[p, where, :] = grad
                first, cross = carry
                return first + net.fold(grad), cross + net.fold(grad * (h * a + b))

            net.put(exchange, p, net.sweep(out_body, (net.zeros(), net.zeros()), only))
        exchange.start(4)
        exchange.middle()
        if group == 0:
            net.gather_wide(net.gh, net.wide)
            out = pltpu.make_async_copy(net.wide, hbm["y_global"], net.load_sem.at[2])
            out.start()
            outs[0].append(out)
        else:
            for p in range(4):
                for place in range(9):
                    out = pltpu.make_async_copy(
                        net.gh.at[p, pl.ds(top + place * net.per, net.per)],
                        hbm["y_local"].at[place, :, pl.ds(p * W, W)],
                        net.load_sem.at[40 + 9 * p + place],
                    )
                    out.start()
                    outs[1].append(out)
        yield
        exchange.last()
        total = exchange.finish()
        sixth_totals[group] = total
        if group == 1:
            for out in outs[1]:
                out.wait()
        for p in range(4):
            net.back_sweep(
                SIXTH + p, total, p, net.gz.at[p], net.f1.at[p], plain(net.gh.at[p]), groups=only
            )

    streams = [forward(0), forward(1)]
    running = True
    while running:
        running = [next(stream, stream) is not stream for stream in streams][1]
    for p in range(4):
        kind, row, columns = net.parameter(SIXTH + p)
        place = (slice(row, row + 1), columns)
        low, high = sixth_totals[0], sixth_totals[1]
        net.dshift[kind][place] = low.row(p, 0) + high.row(p, 0)
        net.dgain[kind][place] = low.row(p, 1) + high.row(p, 1)
    value = dot_t(net.gh[0], net.we2[:, 0:W])
    for p in range(1, 4):
        value = value + dot_t(net.gh[p], net.we2[:, p * W : (p + 1) * W])
    net.f3[...] = value
    msg = exchange.begin()
    net.through(msg, 0, FIFTH, net.f3, net.h5, False)
    exchange.start(1)
    exchange.middle()
    for p in range(2):
        net.emit(0, 0, p * W, dot_rows(net.n5[...], net.gh[p]))
    for p in range(2, 4):
        net.emit(0, 0, p * W, dot_rows(net.n5[...], net.gh[p]))
    net.flush(1)
    reduce_step()
    exchange.last()
    total = exchange.finish()
    net.back_sweep(FIFTH, total, 0, net.f3, net.h5, around(net.small))
    for tap in range(9):
        i, j = divmod(tap, 3)
        net.shifted(net.t4, net.wb.at[tap], 1 - i, 1 - j)
        net.moved(net.small, top, net.wb.at[tap], 1 - i, 1 - j)
    where = pl.ds(0, rows)
    value = dot_t(net.wb[0, where, :], net.wa[0])
    for tap in range(1, 9):
        value = value + dot_t(net.wb[tap, where, :], net.wa[tap])
    reduce_step()
    net.f3[...] = value
    loads["ws"] = net.load(7, hbm["w_spatial"], net.wa)
    msg = exchange.begin()
    net.through(msg, 0, FOURTH, net.f3, net.h4, True)
    exchange.start(1)
    exchange.middle()
    for tap in range(5):
        net.emit(1, tap * W, 0, dot_rows(net.x[tap], net.small[...]))
    for tap in range(5, 9):
        net.emit(1, tap * W, 0, dot_rows(net.x[tap], net.small[...]))
    net.flush(2)
    reduce_step()
    loads["x"] = pltpu.make_async_copy(hbm["x_keep"], net.x, net.load_sem.at[23])
    loads["x"].start()
    exchange.last()
    total = exchange.finish()
    reduce_step()
    net.back_sweep(FOURTH, total, 0, net.f3, net.h4, plain(net.small))
    msg = exchange.begin()
    for p in range(4):
        net.gz[p] = net.gz[p] + dot_t(net.small[...], net.wr2[p])
        params = [
            join(p, group)
            + net.standard(THIRD + p, group)
            + net.standard(SIDE + p, group)
            for group in range(2)
        ]

        def join_back(group, index, where, keep, carry, p=p, params=params):
            a3, a4, b, sa3, sb3, sa4, sb4 = params[group]
            h3 = net.h3[p, where, :].astype(jnp.float32)
            hs = net.hs[p, where, :].astype(jnp.float32)
            slope = gelu_both(h3 * a3 + hs * a4 + b)[1]
            grad = net.gz[p, where, :] * slope
            net.gz[p, where, :] = grad
            first, cross3, cross4 = carry
            return (
                first + net.fold(grad),
                cross3 + net.fold(grad * (h3 * sa3 + sb3)),
                cross4 + net.fold(grad * (hs * sa4 + sb4)),
            )

        results = net.sweep(join_back, (net.zeros(), net.zeros(), net.zeros()))
        net.put(msg, p, results)
        for group in range(2):
            value = jnp.sum(results[group][2], axis=0, keepdims=True)
            msg.write(4 + p // 2, 2 * (p % 2) + group, value)
    reduce_step()
    exchange.start(6)
    exchange.middle()
    for p in range(2):
        net.emit(2, p * W, 0, dot_rows(net.o1[p], net.small[...]))
    for p in range(2, 4):
        net.emit(2, p * W, 0, dot_rows(net.o1[p], net.small[...]))
    net.flush(3)
    reduce_step()
    exchange.last()
    total = exchange.finish()
    for p in range(4):
        net.back_sweep(THIRD + p, total, p, net.gz.at[p], net.h3.at[p], plain(net.h3.at[p]))
        cross = {group: (4 + p // 2, 2 * (p % 2) + group) for group in BOTH}
        net.back_sweep(
            SIDE + p, total, p, net.gz.at[p], net.hs.at[p], plain(net.hs.at[p]), cross=cross
        )
    for p in range(4):
        net.emit(3, 0, p * W, dot_rows(net.n2[...], net.h3[p]))
    net.flush(4)
    reduce_step()
    value = dot_t(net.h3[0], net.we[:, 0:W])
    for p in range(1, 4):
        value = value + dot_t(net.h3[p], net.we[:, p * W : (p + 1) * W])
    net.f3[...] = value
    msg = exchange.begin()
    net.through(msg, 0, SECOND, net.f3, net.h2, False)
    exchange.start(1)
    exchange.middle()
    for k in range(2):
        for p in range(4):
            net.emit(4, k * W, p * W, dot_rows(net.pixels(0, k), net.hs[p]))
    net.flush(5)
    reduce_step()
    exchange.last()
    total = exchange.finish()
    reduce_step()
    net.back_sweep(SECOND, total, 0, net.f3, net.h2, around(net.small))
    for s in range(4):
        net.shifted(net.t4, net.wb.at[s], s // 2, s % 2)
        net.moved(net.small, top, net.wb.at[s], s // 2, s % 2)
    loads["ws"].wait()
    msg = exchange.begin()
    results = None
    for plane in range(4):
        value = None
        for tap in range(9):
            i, j = divmod(tap, 3)
            if 2 * (i != 1) + (j != 1) == plane:
                term = dot_t(net.wb[2 * (i == 0) + (j == 0), where, :], net.wa[tap])
                value = term if value is None else value + term
        net.f1[plane] = value
        new = net.through(msg, None, FIRST, net.f1.at[plane], net.h1.at[plane], True)
        results = new if results is None else jax.tree.map(jnp.add, results, new)
    reduce_step()
    net.put(msg, 0, results)
    for k in range(2):
        for p in range(4):
            loads["short", 4 * k + p] = net.load(
                8 + 4 * k + p,
                hbm["w_short"].at[pl.ds(k * W, W), pl.ds(p * W, W)],
                net.wb.at[4 * k + p],
            )
    exchange.start(1)
    exchange.middle()
    loads["x"].wait()
    for tap in range(5):
        net.emit(5, tap * W, 0, dot_rows(net.x[tap], net.small[...]))
    for tap in range(5, 9):
        net.emit(5, tap * W, 0, dot_rows(net.x[tap], net.small[...]))
    net.flush(6)
    reduce_step()
    exchange.last()
    total = exchange.finish()
    reduce_step()
    for plane in range(4):
        net.back_sweep(
            FIRST, total, 0, net.f1.at[plane], net.h1.at[plane], plain(net.h1.at[plane]), 4
        )
    for k in range(2):
        value = dot_rows(net.pixels(0, k), net.h1[0])
        for plane in range(1, 4):
            value = value + dot_rows(net.pixels(plane, k), net.h1[plane])
        net.emit(6, k * W, 0, value)
    net.flush(7)
    reduce_step()
    outs = outs[0]
    for plane in range(4):
        for k in range(2):
            value = dot_t(net.h1[plane], net.wr[k * W : (k + 1) * W, :])
            if plane == 0:
                for p in range(4):
                    if k == 0:
                        loads["short", p].wait()
                        loads["short", 4 + p].wait()
                    value = value + dot_t(net.hs[p], net.wb[4 * k + p])
            value = value.astype(jnp.bfloat16).reshape(rows // BLK, BLK, W)
            net.img[plane, :, :, k * W : (k + 1) * W] = value
        for row in range(3):
            out = pltpu.make_async_copy(
                net.img.at[plane, pl.ds(edge + 3 * wide * row, 3 * wide)],
                hbm["grad_local"].at[row, plane // 2, :, plane % 2],
                net.load_sem.at[24 + 3 * plane + row],
            )
            out.start()
            outs.append(out)
        if plane % 2:
            net.gather_image(plane // 2)
            out = pltpu.make_async_copy(
                net.raw.at[plane // 2],
                hbm["grad_global"].at[:, plane // 2],
                net.load_sem.at[plane // 2],
            )
            out.start()
            outs.append(out)
            reduce_step()
    while reducer.busy():
        reduce_step()
    for out in outs:
        out.wait()


HBM_IN = (
    "image_global",
    "image_local",
    "cot_global",
    "cot_local",
    "w_reduce",
    "w_spatial",
    "w_expand",
    "w_short",
    "w_reduce2",
    "w_spatial2",
    "w_expand2",
    "gain_mid",
    "shift_mid",
    "gain_wide",
    "shift_wide",
)
HBM_OUT = ("y_global", "y_local", "grad_global", "grad_local")
SHAPES = ((512, 2048), (4608, 512), (2048, 512), (512, 2048), (1024, 2048), (4608, 512), (1024, 512))


def whole_kernel(sizes, geometry, names, half, *refs):
    x_bits, dp_bits, _ = bit_counts(sizes)
    steps = x_bits + dp_bits
    place = [0]

    def some(number):
        start = place[0]
        place[0] += number
        return refs[start : place[0]]

    hbm = dict(zip(HBM_IN, some(len(HBM_IN))))
    hbm.update(zip(HBM_OUT, some(len(HBM_OUT))))
    outs = some(7)
    small = some(4)
    grads = some(7)
    (hbm["x_keep"],) = some(1)
    parts = dict(zip(names, some(len(names))))
    groups = len(chip_groups(sizes))

    def some_exchange():
        taken = some(6 + groups)
        return Exchange(sizes, (*taken[:3], taken[3 : 3 + groups], *taken[3 + groups :]))

    exchange, *others = [some_exchange() for _ in range(5)]
    lanes = len(axis_orders(sizes))
    rest = some(2 + lanes * steps + 6)
    landings = [rest[2 + steps * i : 2 + steps * (i + 1)] for i in range(lanes)]
    scratch = (rest[0], rest[1], landings) + tuple(rest[2 + lanes * steps :])
    reducer = Reducer(sizes, SHAPES, half, grads, outs, scratch)
    net = Net(sizes, geometry, parts)
    net.hbm, net.grads = hbm, grads
    net.dgain, net.dshift = (small[0], small[2]), (small[1], small[3])

    flips = [(0, 1)] + [flip for group in chip_groups(sizes) for flip in group[1]]
    semaphore = pltpu.get_barrier_semaphore()

    def arrive():
        for down, across in flips:
            device = (reducer.dp ^ down, reducer.grp ^ across)
            pl.semaphore_signal(semaphore, inc=1, device_id=device, device_id_type=MESH_ID)

    def entered():
        pl.semaphore_wait(semaphore, len(flips))

    net.arrive, net.entered = arrive, entered
    network(net, exchange, others[:2], others[2:], reducer)


def settle_kernel(*refs):
    count = (len(refs) - 2) // 3
    ins, outs, held = refs[:count], refs[count : 2 * count], refs[2 * count : 3 * count]
    first = [pltpu.make_async_copy(ins[i], held[i], refs[-2].at[i]) for i in range(count)]
    second = [pltpu.make_async_copy(held[i], outs[i], refs[-1].at[i]) for i in range(count)]
    for copy in first:
        copy.start()
    for i in range(count):
        first[i].wait()
        second[i].start()
    for copy in second:
        copy.wait()


def settle(values):
    anywhere = pl.BlockSpec(memory_space=pl.ANY)
    count = len(values)
    return pl.pallas_call(
        settle_kernel,
        out_shape=[jax.ShapeDtypeStruct(value.shape, value.dtype) for value in values],
        in_specs=[anywhere] * count,
        out_specs=[anywhere] * count,
        scratch_shapes=[pltpu.VMEM(value.shape, value.dtype) for value in values]
        + [pltpu.SemaphoreType.DMA((count,))] * 2,
        compiler_params=pltpu.CompilerParams(vmem_limit_bytes=VMEM_LIMIT),
    )(*values)


def run_network(arrays, weights, norms, crops, per):
    sizes = (lax.axis_size("dp"), lax.axis_size("grp"))
    dp_size, grp_size = sizes
    dp_bits = dp_size.bit_length() - 1
    half = 256 // dp_size
    rows = crops * 56 + 9 * per
    margin = -(-9 * crops // BLK) * BLK
    bf16, f32 = jnp.bfloat16, jnp.float32
    scratch = {
        "img": pltpu.VMEM((4, rows // BLK, BLK, 1024), bf16),
        "h1": pltpu.VMEM((4, rows, W), bf16),
        "x": pltpu.VMEM((9, rows, W), bf16),
        "f1": pltpu.VMEM((4, rows, W), f32),
        "h3": pltpu.VMEM((4, rows, W), bf16),
        "hs": pltpu.VMEM((4, rows, W), bf16),
        "o1": pltpu.VMEM((4, rows, W), bf16),
        "h2": pltpu.VMEM((rows, W), bf16),
        "h4": pltpu.VMEM((rows, W), bf16),
        "h5": pltpu.VMEM((rows, W), bf16),
        "n2": pltpu.VMEM((rows, W), bf16),
        "n5": pltpu.VMEM((rows, W), bf16),
        "small": pltpu.VMEM((rows, W), bf16),
        "gz": pltpu.VMEM((4, rows, W), f32),
        "gh": pltpu.VMEM((4, rows, W), bf16),
        "t4": pltpu.VMEM((crops * 56 + 2 * margin, W), f32),
        "nl": pltpu.VMEM((4, 9 * per, W), bf16),
        "f3": pltpu.VMEM((rows, W), f32),
        "stage": pltpu.VMEM((2, W, W), f32),
        "wr": pltpu.VMEM((1024, W), bf16),
        "we": pltpu.VMEM((W, 2048), bf16),
        "wr2": pltpu.VMEM((4, W, W), bf16),
        "we2": pltpu.VMEM((W, 2048), bf16),
        "wa": pltpu.VMEM((9, W, W), bf16),
        "wb": pltpu.VMEM((9, W, W), bf16),
        "gain": pltpu.VMEM((16, 1, W), f32),
        "shift": pltpu.VMEM((16, 1, W), f32),
        "mom": pltpu.VMEM((16, 4, W), f32),
        "raw": pltpu.VMEM((2, 7, 14, crops, 1024), bf16),
        "wide": pltpu.VMEM((7, 7, crops, 2048), bf16),
        "turn": pltpu.VMEM((2, 8 * crops, 1024), f32),
        "load_sem": pltpu.SemaphoreType.DMA((76,)),
        "stage_sem": pltpu.SemaphoreType.DMA((2, 32)),
    }
    exchange = exchange_scratch(sizes, 6, 4, 1, 2)
    for _ in range(2):
        exchange += exchange_scratch(sizes, 4, 2, 2, 2)
    for _ in range(2):
        exchange += exchange_scratch(sizes, 4, 2, 1, 1)
    anywhere = pl.BlockSpec(memory_space=pl.ANY)
    inside = pl.BlockSpec(memory_space=pltpu.VMEM)
    shape = jax.ShapeDtypeStruct
    out_shape = (
        [
            shape((7, 7, crops, 2048), bf16),
            shape((9, per, 2048), bf16),
            shape((7, 2, 14, crops, 1024), bf16),
            shape((3, 2, 3, 2, per, 1024), bf16),
        ]
        + [shape((r // dp_size, c), f32) for r, c in SHAPES]
        + [shape((4, W), f32)] * 2
        + [shape((3, 2048), f32)] * 2
        + [shape((2,) * dp_bits + (r // dp_size, c), f32) for r, c in SHAPES]
        + [shape((9, rows, W), bf16)]
    )
    return pl.pallas_call(
        functools.partial(whole_kernel, sizes, (crops, per), tuple(scratch), half),
        out_shape=out_shape,
        in_specs=[anywhere] * (len(HBM_IN) - 4) + [inside] * 4,
        out_specs=[anywhere] * 11 + [inside] * 4 + [anywhere] * 8,
        scratch_shapes=list(scratch.values()) + exchange + reducer_scratch(sizes, half),
        compiler_params=pltpu.CompilerParams(
            collective_id=1, has_side_effects=True, vmem_limit_bytes=VMEM_LIMIT
        ),
    )(*arrays, *weights, *norms)


VMEM_LIMIT = 64 * 2**20 - 2**16


def body(
    image_global,
    image_local,
    w_reduce,
    w_spatial,
    w_expand,
    w_short,
    w_reduce2,
    w_spatial2,
    w_expand2,
    gain_mid,
    shift_mid,
    gain_wide,
    shift_wide,
    cotangent_global,
    cotangent_local,
):
    crops, per = image_global.shape[0], image_local.shape[0]
    results = run_network(
        [
            image_global.transpose(1, 2, 0, 3).reshape(7, 2, 14, crops, 1024),
            image_local.transpose(1, 2, 0, 3).reshape(3, 2, 3, 2, per, 1024),
            cotangent_global.transpose(1, 2, 0, 3),
            cotangent_local.transpose(1, 2, 0, 3).reshape(9, per, 2048),
        ],
        [
            w_reduce,
            w_spatial.reshape(9, W, W),
            w_expand,
            w_short,
            w_reduce2.reshape(4, W, W),
            w_spatial2.reshape(9, W, W),
            w_expand2,
        ],
        [gain_mid, shift_mid, gain_wide, shift_wide],
        crops,
        per,
    )
    results = settle(results[:15])
    y_global, y_local, grad_global, grad_local = results[:4]
    expand2, spatial2, reduce2, expand, short, spatial, reduce = results[4:11]
    return (
        y_global.transpose(2, 0, 1, 3),
        y_local.reshape(3, 3, per, 2048).transpose(2, 0, 1, 3),
        grad_global.reshape(14, 14, crops, 1024).transpose(2, 0, 1, 3),
        grad_local.reshape(6, 6, per, 1024).transpose(2, 0, 1, 3),
        reduce,
        spatial,
        expand,
        short,
        reduce2,
        spatial2,
        expand2,
        *results[11:15],
    )


def solution(mesh):
    crops = P(("dp", "grp"), None, None, None)
    in_specs = (crops, crops) + (P(),) * 11 + (crops, crops)
    out_specs = (crops,) * 4 + (P("dp", None),) * 7 + (P(),) * 4
    return jax.shard_map(body, mesh=mesh, in_specs=in_specs, out_specs=out_specs, check_vma=False)
```

```python
import functools
import math

import jax
import jax.numpy as jnp
from jax import lax
from jax.experimental import pallas as pl
from jax.experimental.pallas import tpu as pltpu
from jax.sharding import PartitionSpec as P

EPS = 1e-05
MESH_ID = pl.DeviceIdType.MESH


PANEL = 512
DEPTH = 8


def chunk_list(shapes, dp_size, half):
    chunks = []
    for number, (rows, columns) in enumerate(shapes):
        own = rows // dp_size
        for panel in range(columns // PANEL):
            for start in range(0, own, 2 * half):
                chunks.append((number, start, panel * PANEL))
    return chunks


class Reducer:
    def __init__(self, sizes, shapes, half, weights, outs, scratch):
        dp_size, grp_size = sizes
        self.half = half
        self.weights = weights
        self.outs = outs
        (
            self.acc,
            self.rc,
            self.rd,
            self.fin,
            self.load_sem,
            self.out_sem,
            self.send_sem,
            self.recv_sem,
            self.credit,
        ) = scratch
        self.chunks = chunk_list(shapes, dp_size, half)
        self.dp = lax.axis_index("dp")
        self.grp = lax.axis_index("grp")
        x_bits, dp_bits, y_bits = bit_counts(sizes)
        self.x_bits, self.dp_bits = x_bits, dp_bits
        self.orders = axis_orders(sizes)
        self.steps = x_bits + dp_bits
        self.lanes = len(self.orders) // 2
        self.plan = []
        self.entered = 0
        self.stages = self.steps + x_bits + 3
        self.slots = self.lanes * (self.steps + 2)

    def bit(self, step):
        kind, index = step
        return ((self.grp >> (index + 1)) & 1) if kind == "x" else ((self.dp >> index) & 1)

    def partner(self, step):
        kind, index = step
        if kind == "x":
            return (self.dp, self.grp ^ (2 << index))
        return (self.dp ^ (1 << index), self.grp)

    def sibling(self):
        return (self.dp, self.grp ^ 1)

    def region(self, done, last_flip):
        place = [slice(None)] * self.dp_bits
        width = PANEL
        column = 0
        for number, step in enumerate(done):
            bit = self.bit(step)
            if last_flip and number == len(done) - 1:
                bit = 1 - bit
            if step[0] == "d":
                place[self.dp_bits - 1 - step[1]] = bit
            else:
                width = width // 2
                column = column + bit * width
        return place, column, width

    def view(self, ref, slot, done, flip=False):
        place, column, width = self.region(done, flip)
        if isinstance(column, int):
            cols = pl.ds(column, width)
        else:
            cols = pl.ds(pl.multiple_of(column, width), width)
        return ref.at[(slot, *place, slice(None), cols)]

    def landing(self, k, order, count):
        return self.rd[k % len(self.orders)][count - 1]

    def c_copy(self, k, slot):
        number, start, column = self.chunks[k]
        source = self.weights[number].at[
            (slice(None),) * self.dp_bits
            + (
                pl.ds(start + (1 - self.grp % 2) * self.half, self.half),
                pl.ds(column, PANEL),
            )
        ]
        return pltpu.make_async_remote_copy(
            src_ref=source,
            dst_ref=self.rc.at[k % (2 * self.lanes)],
            send_sem=self.send_sem.at[slot, 0],
            recv_sem=self.recv_sem.at[slot, 0],
            device_id=self.sibling(),
            device_id_type=MESH_ID,
        )

    def load(self, k, slot):
        number, start, column = self.chunks[k]
        source = self.weights[number].at[
            (slice(None),) * self.dp_bits
            + (pl.ds(start + (self.grp % 2) * self.half, self.half), pl.ds(column, PANEL))
        ]
        return pltpu.make_async_copy(source, self.acc.at[slot], self.load_sem.at[slot])

    def d_copy(self, k, slot, count):
        order = self.orders[k % len(self.orders)]
        return pltpu.make_async_remote_copy(
            src_ref=self.view(self.acc, slot, order[:count], True),
            dst_ref=self.landing(k, order, count),
            send_sem=self.send_sem.at[slot, count],
            recv_sem=self.recv_sem.at[slot, count],
            device_id=self.partner(order[count - 1]),
            device_id_type=MESH_ID,
        )

    def x_columns(self, count):
        steps = [("x", i) for i in range(self.x_bits - count)]
        place, column, width = self.region(steps, False)
        if isinstance(column, int):
            return pl.ds(column, width)
        return pl.ds(pl.multiple_of(column, width), width)

    def ag_copy(self, k, slot, count):
        columns = self.x_columns(count)
        block = self.fin.at[slot, :, columns]
        stage = self.steps + 1 + count
        return pltpu.make_async_remote_copy(
            src_ref=block,
            dst_ref=block,
            send_sem=self.send_sem.at[slot, stage],
            recv_sem=self.recv_sem.at[slot, stage],
            device_id=self.partner(("x", self.x_bits - 1 - count)),
            device_id_type=MESH_ID,
        )

    def out_block(self, k):
        number, start, column = self.chunks[k]
        return self.outs[number].at[
            pl.ds(start + (self.grp % 2) * self.half, self.half), pl.ds(column, PANEL)
        ]

    def out_copies(self, k, slot):
        stage = self.stages - 2
        remote = pltpu.make_async_remote_copy(
            src_ref=self.fin.at[slot],
            dst_ref=self.out_block(k),
            send_sem=self.send_sem.at[slot, stage],
            recv_sem=self.recv_sem.at[slot, stage],
            device_id=self.sibling(),
            device_id_type=MESH_ID,
        )
        local = pltpu.make_async_copy(self.fin.at[slot], self.out_block(k), self.out_sem.at[slot])
        return remote, local

    def period(self, stage):
        return 2 * self.lanes if stage <= self.steps else self.slots

    def give(self, k, stage, device):
        period = self.period(stage)
        if k + period < len(self.chunks):
            pl.semaphore_signal(
                self.credit.at[k % period, stage],
                inc=1,
                device_id=device,
                device_id_type=MESH_ID,
            )

    def take(self, k, stage):
        period = self.period(stage)
        if k >= period:
            pl.semaphore_wait(self.credit.at[k % period, stage], 1)

    def add(self, k, slot, order, count, target=None):
        done = order[:count]
        place, column, width = self.region(done, False)
        free = [number for number, value in enumerate(place) if isinstance(value, slice)]
        cols = pl.ds(column, width)
        if not isinstance(column, int):
            cols = pl.ds(pl.multiple_of(column, width), width)

        def one(index, carry):
            where = list(place)
            lead = []
            for position, axis in enumerate(free):
                value = (index >> (len(free) - 1 - position)) & 1
                where[axis] = value
                lead.append(value)
            if count == 0:
                arrived = self.rc[(k % (2 * self.lanes), *lead)]
            else:
                arrived = self.rd[k % len(self.orders)][count - 1][(*lead, slice(None), slice(None))]
            here = (slot, *where, slice(None), cols)
            if target is None:
                self.acc[here] = self.acc[here] + arrived
            else:
                self.fin[slot, :, self.x_columns(0)] = self.acc[here] + arrived
            return carry

        total = 2 ** len(free)
        if total == 1:
            one(0, 0)
        else:
            lax.fori_loop(0, total, one, 0)

    def run(self, k, stage):
        slot = k % self.slots
        order = self.orders[k % len(self.orders)]
        steps = self.steps
        if stage == 0:
            self.load(k, slot).start()
            self.take(k, 0)
            self.c_copy(k, slot).start()
        elif stage <= steps + 1:
            count = stage - 1
            if count == 0:
                self.load(k, slot).wait()
                self.c_copy(k, slot).wait()
            else:
                self.d_copy(k, slot, count).wait()
            self.add(k, slot, order, count, None if count < steps else True)
            device = self.sibling() if count == 0 else self.partner(order[count - 1])
            self.give(k, count, device)
            self.take(k, count + 1)
            if count < steps:
                self.d_copy(k, slot, count + 1).start()
            else:
                self.ag_copy(k, slot, 0).start()
        elif stage <= steps + self.x_bits:
            count = stage - steps - 1
            self.ag_copy(k, slot, count - 1).wait()
            self.take(k, stage)
            self.ag_copy(k, slot, count).start()
        elif stage == self.stages - 2:
            self.ag_copy(k, slot, self.x_bits - 1).wait()
            remote, local = self.out_copies(k, slot)
            remote.start()
            local.start()
        else:
            remote, local = self.out_copies(k, slot)
            remote.wait()
            local.wait()
            for count in range(self.x_bits):
                device = self.partner(("x", self.x_bits - 1 - count))
                self.give(k, steps + 1 + count, device)

    def step(self, weights):
        ready = sum(1 for chunk in self.chunks if chunk[0] < weights)
        after = min(ready, self.entered + self.lanes)
        self.plan.append(list(range(self.entered, after)))
        self.entered = after
        time = len(self.plan) - 1
        for stage in (1, 2, 0, *reversed(range(3, self.stages))):
            if stage <= time:
                for k in self.plan[time - stage]:
                    self.run(k, stage)

    def busy(self):
        recent = self.plan[1 - self.stages :]
        return self.entered < len(self.chunks) or any(recent)


def bit_counts(sizes):
    dp_size, grp_size = sizes
    x_bits = (grp_size // 2).bit_length() - 1
    dp_bits = dp_size.bit_length() - 1
    return x_bits, dp_bits, x_bits


def axis_orders(sizes):
    x_bits, dp_bits, y_bits = bit_counts(sizes)
    xs = [("x", i) for i in range(x_bits)]
    ys = [("d", i) for i in range(y_bits)]
    zs = [("d", i) for i in range(y_bits, dp_bits)]
    first = [xs + ys + zs, ys + zs[:1] + xs + zs[1:], zs[:1] + ys + xs + zs[1:]]
    second = [first[0], ys + xs + zs, first[2]]
    lanes = 3 if x_bits + dp_bits < 5 else 2
    return first[:lanes] + second[:lanes]


def reducer_scratch(sizes, half):
    x_bits, dp_bits, _ = bit_counts(sizes)
    steps = x_bits + dp_bits
    groups = steps + 2
    orders = axis_orders(sizes)
    slots = len(orders) // 2 * groups
    stages = steps + x_bits + 3
    landings = []
    for order in orders:
        for count in range(1, steps + 1):
            done = [step[0] for step in order[:count]]
            lead = (2,) * (dp_bits - done.count("d"))
            width = PANEL >> done.count("x")
            landings.append(pltpu.VMEM(lead + (half, width), jnp.float32))
    block = (slots,) + (2,) * dp_bits + (half, PANEL)
    return [
        pltpu.VMEM(block, jnp.float32),
        pltpu.VMEM((len(orders),) + block[1:], jnp.float32),
        *landings,
        pltpu.VMEM((slots, half, PANEL), jnp.float32),
        pltpu.SemaphoreType.DMA((slots,)),
        pltpu.SemaphoreType.DMA((slots,)),
        pltpu.SemaphoreType.DMA((slots, stages)),
        pltpu.SemaphoreType.DMA((slots, stages)),
        pltpu.SemaphoreType.REGULAR((slots, stages)),
    ]


C0 = math.sqrt(2.0 / math.pi)
C1 = C0 * 0.044715
W = 512
BLK = 16
FIRST, SECOND, THIRD, SIDE, FOURTH, FIFTH, SIXTH = 0, 1, 2, 6, 10, 11, 12


def gelu(u):
    t = jnp.tanh(u * (C0 + C1 * u * u))
    return u * (0.5 + 0.5 * t)


def gelu_both(u):
    square = u * u
    t = jnp.tanh(u * (C0 + C1 * square))
    half = 0.5 + 0.5 * t
    slope = half + 0.5 * u * (1.0 - t * t) * (C0 + 3.0 * C1 * square)
    return u * half, slope


def dot(a, b):
    return lax.dot_general(a, b, (((1,), (0,)), ((), ())), preferred_element_type=jnp.float32)


def dot_t(a, b):
    return lax.dot_general(a, b, (((1,), (1,)), ((), ())), preferred_element_type=jnp.float32)


def dot_rows(a, b):
    return lax.dot_general(a, b, (((0,), (0,)), ((), ())), preferred_element_type=jnp.float32)


H = W // 2


def chip_groups(sizes):
    dp_size, grp_size = sizes
    chips = grp_size // 2
    if dp_size * chips <= 16:
        flips = [(k // chips, 2 * (k % chips)) for k in range(1, dp_size * chips)]
        return [(lambda dp, grp: dp * chips + (grp >> 1), flips)]
    return [
        (lambda dp, grp: grp >> 1, [(0, 2 * k) for k in range(1, chips)]),
        (lambda dp, grp: dp, [(k, 0) for k in range(1, dp_size)]),
    ]


class Totals:
    def __init__(self, ref):
        self.ref = ref

    def row(self, piece, row):
        parts = [self.ref[half, piece, pl.ds(row, 1)] for half in range(2)]
        return jnp.concatenate(parts, axis=1)


class Exchange:
    def __init__(self, sizes, refs):
        self.msg, self.cbuf, self.part, self.bufs, self.tot, self.send, self.recv = refs
        self.dp = lax.axis_index("dp")
        self.grp = lax.axis_index("grp")
        self.core = self.grp % 2
        self.groups = chip_groups(sizes)
        self.halves = self.cbuf.shape[1]
        self.turn = -1
        self.copies = []
        self.sent = [[] for _ in range(self.msg.shape[0])]

    def copy(self, place, source, target, flip):
        result = pltpu.make_async_remote_copy(
            src_ref=source,
            dst_ref=target,
            send_sem=self.send.at[self.turn, place],
            recv_sem=self.recv.at[self.turn, place],
            device_id=(self.dp ^ flip[0], self.grp ^ flip[1]),
            device_id_type=MESH_ID,
        )
        result.start()
        self.copies.append(result)

    def begin(self):
        self.turn = (self.turn + 1) % self.msg.shape[0]
        self.settle(self.turn)
        return self

    def write(self, piece, row, value):
        for half in range(2):
            self.msg[self.turn, half, piece, pl.ds(row, 1)] = value[:, half * H : (half + 1) * H]

    def start(self, pieces, cut=True):
        self.cut = cut
        self.pieces = pl.ds(0, pieces)
        self.number = pieces
        self.taken = range(1 if cut else 2)
        turn = self.turn
        if cut:
            source, target = self.msg.at[turn, 1 - self.core], self.cbuf.at[turn, 0]
            self.copy(0, source.at[self.pieces], target.at[self.pieces], (0, 1))
        else:
            source, target = self.msg.at[turn], self.cbuf.at[turn]
            self.copy(0, source.at[:, self.pieces], target.at[:, self.pieces], (0, 1))

    def wait(self):
        for copy in self.copies:
            copy.wait_recv()
        self.sent[self.turn] += self.copies
        self.copies = []

    def settle(self, turn):
        for copy in self.sent[turn]:
            copy.wait_send()
        self.sent[turn] = []

    def spread(self, number, read):
        turn = self.turn
        index, flips = self.groups[number]
        mine = index(self.dp, self.grp)
        for half in self.taken:
            for piece in range(self.number):
                value = read(half, piece)
                self.part[turn, number, half, piece] = value
                self.bufs[number][turn, mine, half, piece] = value
        first = 2 + sum(len(group[1]) for group in self.groups[:number])
        halves = pl.ds(0, len(self.taken))
        for k, flip in enumerate(flips):
            self.copy(
                first + k,
                self.part.at[turn, number, halves, self.pieces],
                self.bufs[number].at[turn, mine, halves, self.pieces],
                flip,
            )

    def gathered(self, number):
        count = len(self.groups[number][1]) + 1

        def read(half, piece):
            total = self.bufs[number][self.turn, 0, half, piece]
            for k in range(1, count):
                total = total + self.bufs[number][self.turn, k, half, piece]
            return total

        return read

    def middle(self):
        turn = self.turn
        self.wait()

        def read(half, piece):
            place = self.core if self.cut else half
            return self.msg[turn, place, piece] + self.cbuf[turn, half, piece]

        self.spread(0, read)

    def last(self):
        turn = self.turn
        self.wait()
        for number in range(1, len(self.groups)):
            self.spread(number, self.gathered(number - 1))
            self.wait()
        read = self.gathered(len(self.groups) - 1)
        for half in self.taken:
            for piece in range(self.number):
                self.tot[turn, self.core if self.cut else half, piece] = read(half, piece)
        if self.cut:
            block = self.tot.at[turn, self.core, self.pieces]
            self.copy(1, block, block, (0, 1))

    def finish(self):
        self.wait()
        return Totals(self.tot.at[self.turn])


def exchange_scratch(sizes, pieces, rows, halves, turns):
    groups = chip_groups(sizes)
    copies = 2 + sum(len(group[1]) for group in groups)
    block = (pieces, rows, H)
    return [
        pltpu.VMEM((turns, 2) + block, jnp.float32),
        pltpu.VMEM((turns, halves) + block, jnp.float32),
        pltpu.VMEM((turns, len(groups), halves) + block, jnp.float32),
        *[pltpu.VMEM((turns, len(group[1]) + 1, halves) + block, jnp.float32) for group in groups],
        pltpu.VMEM((turns, 2) + block, jnp.float32),
        pltpu.SemaphoreType.DMA((turns, copies)),
        pltpu.SemaphoreType.DMA((turns, copies)),
    ]


BOTH = (0, 1)


def first_row(group, groups):
    return 2 * group if len(groups) == 2 else 0


class Net:
    def __init__(self, sizes, geometry, refs):
        self.sizes = sizes
        self.devices = sizes[0] * sizes[1]
        self.crops, self.per = geometry
        self.top = self.crops * 56
        self.margin = -(-9 * self.crops // BLK) * BLK
        self.rows = self.top + 9 * self.per
        self.top_blocks = self.top // BLK
        self.blocks = self.rows // BLK
        for name, ref in refs.items():
            setattr(self, name, ref)
        self.slot = 0
        self.done = 0
        self.pending = [[], []]


    def load(self, number, source, target):
        copy = pltpu.make_async_copy(source, target, self.load_sem.at[number])
        copy.start()
        return copy


    def pixels(self, plane, half=None, group=None):
        columns = slice(None) if half is None else slice(half * W, (half + 1) * W)
        low, high = (0, self.rows) if group is None else self.span(group)
        value = self.img[plane, pl.ds(low // BLK, (high - low) // BLK), :, columns]
        return value.reshape(high - low, value.shape[2])

    def spread_image(self, a):
        crops = self.crops

        def one(row, carry):
            for b in range(2):
                for column in range(7):
                    value = self.raw[a, row, 2 * column + b]
                    self.turn[b, pl.ds(crops * column, crops), :] = value.astype(jnp.float32)
                block = self.turn[b].astype(jnp.bfloat16).reshape(-1, BLK, 1024)
                where = pl.ds(row * (8 * crops // BLK), 8 * crops // BLK)
                self.img[2 * a + b, where] = block
            return carry

        lax.fori_loop(0, 7, one, 0)

    def gather_image(self, a):
        crops = self.crops

        def one(row, carry):
            for b in range(2):
                where = pl.ds(row * (8 * crops // BLK), 8 * crops // BLK)
                block = self.img[2 * a + b, where].reshape(8 * crops, 1024)
                self.turn[b] = block.astype(jnp.float32)
                for column in range(7):
                    value = self.turn[b, pl.ds(crops * column, crops), :]
                    self.raw[a, row, 2 * column + b] = value.astype(jnp.bfloat16)
            return carry

        lax.fori_loop(0, 7, one, 0)

    def spread_wide(self, source, target):
        crops = self.crops

        def one(row, carry):
            for half in range(2):
                for column in range(7):
                    value = source[row, column, :, half * 1024 : (half + 1) * 1024]
                    self.turn[half, pl.ds(crops * column, crops), :] = value.astype(jnp.float32)
                for p in range(2):
                    value = self.turn[half, :, p * W : (p + 1) * W].astype(jnp.bfloat16)
                    where = pl.ds(pl.multiple_of(row * 8 * crops, BLK), 8 * crops)
                    target[2 * half + p, where, :] = value
            return carry

        lax.fori_loop(0, 7, one, 0)

    def gather_wide(self, source, target):
        crops = self.crops

        def one(row, carry):
            for half in range(2):
                for p in range(2):
                    where = pl.ds(pl.multiple_of(row * 8 * crops, BLK), 8 * crops)
                    value = source[2 * half + p, where, :].astype(jnp.float32)
                    self.turn[half, :, p * W : (p + 1) * W] = value
                for column in range(7):
                    value = self.turn[half, pl.ds(crops * column, crops), :]
                    target[row, column, :, half * 1024 : (half + 1) * 1024] = value.astype(
                        jnp.bfloat16
                    )
            return carry

        lax.fori_loop(0, 7, one, 0)


    def span(self, group):
        return (0, self.top) if group == 0 else (self.top, self.rows)

    def sweep(self, body, init, groups=BOTH):
        results = {}
        for group in groups:
            low, high = (0, self.top_blocks) if group == 0 else (self.top_blocks, self.blocks)

            def one(index, carry, group=group):
                rows = pl.ds(pl.multiple_of(index * BLK, BLK), BLK)
                return body(group, index, rows, self.keeper(group, index), carry)

            results[group] = lax.fori_loop(low, high, one, init)
        return results

    def keeper(self, group, index):
        if group == 1:
            return lambda value: value
        row = index * BLK + lax.broadcasted_iota(jnp.int32, (BLK, 128), 0)
        valid = row % (8 * self.crops) < 7 * self.crops
        valid = jnp.concatenate([valid.astype(jnp.float32)] * (W // 128), axis=1)
        return lambda value: value * valid

    def zeros(self):
        return jnp.zeros((8, W), jnp.float32)

    @staticmethod
    def fold(value):
        return value[0:8] + value[8:16]

    def put(self, msg, piece, results):
        for group in results:
            row = first_row(group, results)
            first, other = results[group][:2]
            msg.write(piece, row, jnp.sum(first, axis=0, keepdims=True))
            msg.write(piece, row + 1, jnp.sum(other, axis=0, keepdims=True))

    def count(self, group, scale):
        pixels = (49 * self.crops, 9 * self.per)[group]
        return float(pixels * scale * self.devices)

    def moments(self, total, piece, norm, group, scale=1):
        count = self.count(group, scale)
        mean = total.row(piece, 0) / count
        square = total.row(piece, 1) / count
        self.mom[norm, pl.ds(2 * group, 1)] = mean
        self.mom[norm, pl.ds(2 * group + 1, 1)] = lax.rsqrt(square - mean * mean + EPS)

    def affine(self, norm, group):
        mean = self.mom[norm, pl.ds(2 * group, 1)]
        scale = self.mom[norm, pl.ds(2 * group + 1, 1)] * self.gain[norm]
        return scale, self.shift[norm] - mean * scale

    def standard(self, norm, group):
        mean = self.mom[norm, pl.ds(2 * group, 1)]
        deviation = self.mom[norm, pl.ds(2 * group + 1, 1)]
        return deviation, -mean * deviation

    def measure(self, source, masked, groups, store=None):
        def body(group, index, rows, keep, carry):
            value = source[rows, :]
            if store is not None:
                store[rows, :] = value.astype(store.dtype)
            if masked:
                value = keep(value)
            total, square = carry
            return total + self.fold(value), square + self.fold(value * value)

        return self.sweep(body, (self.zeros(), self.zeros()), groups)

    def activate(self, source, norm, target, groups):
        params = {group: self.affine(norm, group) for group in groups}

        def body(group, index, rows, keep, carry):
            scale, offset = params[group]
            target(group, index, rows, keep(gelu(source[rows, :] * scale + offset)))
            return carry

        self.sweep(body, 0, groups)


    def shifted(self, source, target, down, across):
        offset = (8 * down + across) * self.crops
        start = self.margin + offset
        aligned = start // 8 * 8
        skip = start - aligned

        def one(index, carry):
            rows = pl.ds(pl.multiple_of(index * BLK, BLK), BLK)
            if skip:
                value = source[pl.ds(pl.multiple_of(index * BLK + aligned, 8), 24), :]
                value = value[skip : skip + BLK]
            else:
                value = source[pl.ds(pl.multiple_of(index * BLK + aligned, 8), BLK), :]
            target[rows, :] = value.astype(jnp.bfloat16)
            return carry

        lax.fori_loop(0, self.top_blocks, one, 0)

    def moved(self, source, first, target, down, across):
        per = self.per
        for a in range(3):
            for b in range(3):
                here = pl.ds(self.top + (3 * a + b) * per, per)
                if 0 <= a + down < 3 and 0 <= b + across < 3:
                    there = pl.ds(first + (3 * (a + down) + b + across) * per, per)
                    target[here, :] = source[there, :]
                else:
                    target[here, :] = jnp.zeros((per, W), jnp.bfloat16)

    def clear_margins(self, ref):
        zero = jnp.zeros((self.margin, W), jnp.float32)
        ref[pl.ds(0, self.margin), :] = zero
        ref[pl.ds(self.margin + self.top, self.margin), :] = zero

    @staticmethod
    def parameter(norm):
        if norm in (FIRST, SECOND):
            return 0, norm, slice(0, W)
        if norm in (FOURTH, FIFTH):
            return 0, norm - FOURTH + 2, slice(0, W)
        row, panel = (2, norm - SIXTH) if norm >= SIXTH else divmod(norm - THIRD, 4)
        return 1, row, slice(panel * W, (panel + 1) * W)


    def back(self, norm, total, piece, cross):
        kind, row, columns = self.parameter(norm)
        where = (slice(row, row + 1), columns)
        self.dshift[kind][where] = total.row(piece, 0) + total.row(piece, 2)
        self.dgain[kind][where] = total.row(*cross[0]) + total.row(*cross[1])

    def back_params(self, norm, group, total, piece, row, cross, scale):
        count = self.count(group, scale)
        mean_grad = total.row(piece, row) / count
        mean_cross = total.row(*cross) / count
        factor = self.gain[norm] * self.mom[norm, pl.ds(2 * group + 1, 1)]
        return factor, mean_grad, mean_cross

    def back_sweep(
        self, norm, total, piece, grad, hidden, target, scale=1, cross=None, groups=BOTH
    ):
        cross = cross or {group: (piece, first_row(group, groups) + 1) for group in groups}
        if len(groups) == 2:
            self.back(norm, total, piece, cross)
        params = {}
        for group in groups:
            row = first_row(group, groups)
            params[group] = self.back_params(norm, group, total, piece, row, cross[group], scale)
            params[group] += self.standard(norm, group)

        def body(group, index, rows, keep, carry):
            factor, mean_grad, mean_cross, a, b = params[group]
            scaled = hidden[rows, :].astype(jnp.float32) * a + b
            value = factor * (grad[rows, :] - mean_grad - scaled * mean_cross)
            target(group, index, rows, keep(value))
            return carry

        self.sweep(body, 0, groups)

    def through(self, msg, piece, norm, grad, hidden, masked, groups=BOTH):
        params = {group: self.affine(norm, group) + self.standard(norm, group) for group in groups}

        def body(group, index, rows, keep, carry):
            scale, offset, a, b = params[group]
            value = hidden[rows, :].astype(jnp.float32)
            slope = gelu_both(value * scale + offset)[1]
            result = grad[rows, :] * slope
            if masked:
                result = keep(result)
            grad[rows, :] = result
            first, cross = carry
            return first + self.fold(result), cross + self.fold(result * (value * a + b))

        results = self.sweep(body, (self.zeros(), self.zeros()), groups)
        if piece is not None:
            self.put(msg, piece, results)
        return results


    def emit(self, number, row, column, value):
        slot = self.slot
        self.slot = 1 - slot
        self.drain(slot)
        self.stage[slot] = value
        grads = self.grads[number]
        own = grads.shape[-2]
        bits = len(grads.shape) - 2
        place = row
        while place < row + W:
            owner = place // own
            size = min(own - place % own, row + W - place)
            index = tuple((owner >> (bits - 1 - i)) & 1 for i in range(bits))
            copy = pltpu.make_async_copy(
                self.stage.at[slot, pl.ds(place - row, size)],
                grads.at[index + (pl.ds(place % own, size), pl.ds(column, W))],
                self.stage_sem.at[slot, len(self.pending[slot])],
            )
            copy.start()
            self.pending[slot].append(copy)
            place += size

    def drain(self, slot):
        for copy in self.pending[slot]:
            copy.wait()
        self.pending[slot] = []

    def flush(self, weights):
        self.drain(0)
        self.drain(1)
        self.done = weights


def network(net, exchange, exchanges, sides, reducer):
    rows = net.rows
    top = net.top

    def reduce_step():
        reducer.step(net.done)

    hbm = net.hbm
    loads = {}
    for a in range(2):
        loads["img", a] = net.load(a, hbm["image_global"].at[:, a], net.raw.at[a])
    edge, wide = net.top_blocks, net.per // BLK
    for plane in range(4):
        for row in range(3):
            loads["img", plane, row] = net.load(
                24 + 3 * plane + row,
                hbm["image_local"].at[row, plane // 2, :, plane % 2],
                net.img.at[plane, pl.ds(edge + 3 * wide * row, 3 * wide)],
            )
    loads["wr"] = net.load(4, hbm["w_reduce"], net.wr)

    def load_short():
        for k in range(2):
            for p in range(4):
                loads["short", 4 * k + p] = net.load(
                    8 + 4 * k + p,
                    hbm["w_short"].at[pl.ds(k * W, W), pl.ds(p * W, W)],
                    net.wb.at[4 * k + p],
                )

    net.arrive()
    for plane in range(4):
        net.clear_margins(net.gz.at[plane])
    net.clear_margins(net.t4)
    net.turn[...] = jnp.zeros(net.turn.shape, jnp.float32)
    for norm in range(16):
        kind, row, columns = net.parameter(norm)
        net.gain[norm] = hbm[("gain_mid", "gain_wide")[kind]][row : row + 1, columns]
        net.shift[norm] = hbm[("shift_mid", "shift_wide")[kind]][row : row + 1, columns]

    loads["wr"].wait()

    def plain(ref):
        def keep(group, index, where, value):
            ref[where, :] = value.astype(ref.dtype)

        return keep

    def around(ref):
        def keep(group, index, where, value):
            if group == 0:
                net.t4[pl.ds(pl.multiple_of(index * BLK + net.margin, BLK), BLK), :] = value
            ref[where, :] = value.astype(jnp.bfloat16)

        return keep

    def join(p, group):
        a3, b3 = net.affine(THIRD + p, group)
        a4, b4 = net.affine(SIDE + p, group)
        return a3, a4, b3 + b4

    sixth_totals = {}
    fifth_sums = {}
    outs = {0: [], 1: []}

    def load_more():
        loads["we"] = net.load(16, hbm["w_expand"], net.we)
        loads["wr2"] = net.load(17, hbm["w_reduce2"], net.wr2)
        loads["we2"] = net.load(18, hbm["w_expand2"], net.we2)
        loads["cot"] = net.load(2, hbm["cot_global"], net.wide)
        for p in range(4):
            for place in range(9):
                loads["cot", p, place] = net.load(
                    40 + 9 * p + place,
                    hbm["cot_local"].at[place, :, pl.ds(p * W, W)],
                    net.gh.at[p, pl.ds(top + place * net.per, net.per)],
                )

    def forward(group):
        exchange, side = exchanges[group], sides[group]
        only = (group,)
        low, high = net.span(group)
        here = pl.ds(low, high - low)
        results = None
        for plane in range(4):
            if group == 0:
                if plane % 2 == 0:
                    loads["img", plane // 2].wait()
                    net.spread_image(plane // 2)
                if plane == 0:
                    load_short()
                    loads["ws"] = net.load(7, hbm["w_spatial"], net.wa)
            else:
                for row in range(3):
                    loads["img", plane, row].wait()
            net.f1[plane, here] = dot(net.pixels(plane, None, group), net.wr[...])
            new = net.measure(net.f1.at[plane], False, only, net.h1.at[plane])
            results = new if results is None else jax.tree.map(jnp.add, results, new)
        net.put(exchange.begin(), 0, results)
        if group == 0:
            net.entered()
        exchange.start(1, False)
        exchange.middle()
        def side_branch():
            side.begin()
            for p in range(4):
                if group == 0:
                    loads["short", p].wait()
                    loads["short", 4 + p].wait()
                place = net.f3 if group == 0 else net.f1.at[p]
                place[here] = dot(net.pixels(0, 0, group), net.wb[p]) + dot(
                    net.pixels(0, 1, group), net.wb[4 + p]
                )
                net.put(side, p, net.measure(place, False, only, net.hs.at[p]))

        if group == 0:
            side_branch()
        if group == 0:
            load_more()
        yield
        exchange.last()
        total = exchange.finish()
        if group == 0:
            side.start(4)
        net.moments(total, 0, FIRST, group, 4)
        for plane in range(4):

            def keep_first(group, index, where, value, plane=plane):
                if group == 0:
                    there = pl.ds(pl.multiple_of(index * BLK + net.margin, BLK), BLK)
                    net.gz[plane, there, :] = value
                else:
                    there = pl.ds(pl.multiple_of((index - net.top_blocks) * BLK, BLK), BLK)
                    net.nl[plane, there, :] = value.astype(jnp.bfloat16)

            net.activate(net.f1.at[plane], FIRST, keep_first, only)
        if group == 0:
            side.middle()
        for tap in range(9):
            i, j = divmod(tap, 3)
            plane = 2 * (i != 1) + (j != 1)
            if group == 0:
                net.shifted(net.gz.at[plane], net.x.at[tap], -(i == 0), -(j == 0))
            else:
                net.moved(net.nl.at[plane], 0, net.x.at[tap], -(i == 0), -(j == 0))
        if group == 0:
            loads["ws"].wait()

        def conv():
            total = dot(net.x[0, here], net.wa[0])
            for tap in range(1, 9):
                total = total + dot(net.x[tap, here], net.wa[tap])
            return total

        net.f3[here] = conv()
        net.put(exchange.begin(), 0, net.measure(net.f3, True, only, net.h2))
        exchange.start(1, False)
        exchange.middle()
        if group == 0:
            loads["cot"].wait()
            net.spread_wide(net.wide, net.gh)
        else:
            loads["ws2"] = net.load(7, hbm["w_spatial2"], net.wa)
            loads["x"] = pltpu.make_async_copy(net.x, hbm["x_keep"], net.load_sem.at[23])
            loads["x"].start()
            side_branch()
            side.start(4)
            side.middle()
        yield
        exchange.last()
        total = exchange.finish()
        net.moments(total, 0, SECOND, group)
        net.activate(net.f3, SECOND, plain(net.n2), only)
        if group == 0:
            loads["we"].wait()
        exchange.begin()
        for p in range(4):
            net.f1[p, here] = dot(net.n2[here], net.we[:, p * W : (p + 1) * W])
            net.put(exchange, p, net.measure(net.f1.at[p], False, only, net.h3.at[p]))
        exchange.start(4)
        exchange.middle()
        side.last()
        total_side = side.finish()
        for p in range(4):
            net.moments(total_side, p, SIDE + p, group)
        yield
        exchange.last()
        total = exchange.finish()
        for p in range(4):
            net.moments(total, p, THIRD + p, group)
        for p in range(4):
            params = join(p, group)

            def join_body(group, index, where, keep, carry, p=p, params=params):
                a3, a4, b = params
                u = net.f1[p, where, :] * a3 + net.hs[p, where, :].astype(jnp.float32) * a4 + b
                net.o1[p, where, :] = keep(gelu(u)).astype(jnp.bfloat16)
                return carry

            net.sweep(join_body, 0, only)
        if group == 0:
            loads["wr2"].wait()
        value = dot(net.o1[0, here], net.wr2[0])
        for p in range(1, 4):
            value = value + dot(net.o1[p, here], net.wr2[p])
        net.f3[here] = value
        net.put(exchange.begin(), 0, net.measure(net.f3, False, only, net.h4))
        exchange.start(1, False)
        exchange.middle()
        yield
        exchange.last()
        total = exchange.finish()
        net.moments(total, 0, FOURTH, group)
        net.activate(net.f3, FOURTH, around(net.small), only)
        if group == 0:
            loads["x"].wait()
        for tap in range(9):
            i, j = divmod(tap, 3)
            if group == 0:
                net.shifted(net.t4, net.x.at[tap], i - 1, j - 1)
            else:
                net.moved(net.small, top, net.x.at[tap], i - 1, j - 1)
        if group == 0:
            loads["ws2"].wait()
        net.f3[here] = conv()
        net.put(exchange.begin(), 0, net.measure(net.f3, True, only, net.h5))
        exchange.start(1, False)
        exchange.middle()
        yield
        exchange.last()
        total = exchange.finish()
        net.moments(total, 0, FIFTH, group)
        net.activate(net.f3, FIFTH, plain(net.n5), only)
        if group == 0:
            loads["we2"].wait()
        exchange.begin()
        for p in range(4):
            net.f1[p, here] = dot(net.n5[here], net.we2[:, p * W : (p + 1) * W])
            net.put(exchange, p, net.measure(net.f1.at[p], False, only))
        exchange.start(4)
        exchange.middle()
        yield
        exchange.last()
        total = exchange.finish()
        exchange.begin()
        for p in range(4):
            net.moments(total, p, SIXTH + p, group)
            if group == 1:
                for place in range(9):
                    loads["cot", p, place].wait()
            params = net.affine(SIXTH + p, group) + net.standard(SIXTH + p, group)

            def out_body(group, index, where, keep, carry, p=p, params=params):
                scale, offset, a, b = params
                h = net.f1[p, where, :]
                u = h * scale + offset + net.o1[p, where, :].astype(jnp.float32)
                y, slope = gelu_both(u)
                grad = net.gh[p, where, :].astype(jnp.float32) * slope
                net.gh[p, where, :] = y.astype(jnp.bfloat16)
                net.gz[p, where, :] = grad
                first, cross = carry
                return first + net.fold(grad), cross + net.fold(grad * (h * a + b))

            net.put(exchange, p, net.sweep(out_body, (net.zeros(), net.zeros()), only))
        exchange.start(4)
        exchange.middle()
        if group == 0:
            net.gather_wide(net.gh, net.wide)
            out = pltpu.make_async_copy(net.wide, hbm["y_global"], net.load_sem.at[2])
            out.start()
            outs[0].append(out)
        else:
            for p in range(4):
                for place in range(9):
                    out = pltpu.make_async_copy(
                        net.gh.at[p, pl.ds(top + place * net.per, net.per)],
                        hbm["y_local"].at[place, :, pl.ds(p * W, W)],
                        net.load_sem.at[40 + 9 * p + place],
                    )
                    out.start()
                    outs[1].append(out)
        yield
        exchange.last()
        total = exchange.finish()
        sixth_totals[group] = total
        if group == 1:
            for out in outs[1]:
                out.wait()
        for p in range(4):
            net.back_sweep(
                SIXTH + p, total, p, net.gz.at[p], net.f1.at[p], plain(net.gh.at[p]), groups=only
            )
        value = dot_t(net.gh[0, here], net.we2[:, 0:W])
        for p in range(1, 4):
            value = value + dot_t(net.gh[p, here], net.we2[:, p * W : (p + 1) * W])
        net.f3[here] = value
        fifth_sums.update(net.through(None, None, FIFTH, net.f3, net.h5, False, only))

    streams = [forward(0), forward(1)]
    running = True
    while running:
        running = [next(stream, stream) is not stream for stream in streams][1]
    msg = exchange.begin()
    net.put(msg, 0, fifth_sums)
    exchange.start(1)
    exchange.middle()
    for p in range(4):
        kind, row, columns = net.parameter(SIXTH + p)
        place = (slice(row, row + 1), columns)
        low, high = sixth_totals[0], sixth_totals[1]
        net.dshift[kind][place] = low.row(p, 0) + high.row(p, 0)
        net.dgain[kind][place] = low.row(p, 1) + high.row(p, 1)
    for p in range(2):
        net.emit(0, 0, p * W, dot_rows(net.n5[...], net.gh[p]))
    for p in range(2, 4):
        net.emit(0, 0, p * W, dot_rows(net.n5[...], net.gh[p]))
    net.flush(1)
    reduce_step()
    exchange.last()
    total = exchange.finish()
    net.back_sweep(FIFTH, total, 0, net.f3, net.h5, around(net.small))
    for tap in range(9):
        i, j = divmod(tap, 3)
        net.shifted(net.t4, net.wb.at[tap], 1 - i, 1 - j)
        net.moved(net.small, top, net.wb.at[tap], 1 - i, 1 - j)
    where = pl.ds(0, rows)
    value = dot_t(net.wb[0, where, :], net.wa[0])
    for tap in range(1, 9):
        value = value + dot_t(net.wb[tap, where, :], net.wa[tap])
    reduce_step()
    net.f3[...] = value
    loads["ws"] = net.load(7, hbm["w_spatial"], net.wa)
    msg = exchange.begin()
    net.through(msg, 0, FOURTH, net.f3, net.h4, True)
    exchange.start(1)
    exchange.middle()
    for tap in range(5):
        net.emit(1, tap * W, 0, dot_rows(net.x[tap], net.small[...]))
    for tap in range(5, 9):
        net.emit(1, tap * W, 0, dot_rows(net.x[tap], net.small[...]))
    net.flush(2)
    reduce_step()
    loads["x"] = pltpu.make_async_copy(hbm["x_keep"], net.x, net.load_sem.at[23])
    loads["x"].start()
    exchange.last()
    total = exchange.finish()
    reduce_step()
    net.back_sweep(FOURTH, total, 0, net.f3, net.h4, plain(net.small))
    msg = exchange.begin()
    for p in range(4):
        net.gz[p] = net.gz[p] + dot_t(net.small[...], net.wr2[p])
        params = [
            join(p, group)
            + net.standard(THIRD + p, group)
            + net.standard(SIDE + p, group)
            for group in range(2)
        ]

        def join_back(group, index, where, keep, carry, p=p, params=params):
            a3, a4, b, sa3, sb3, sa4, sb4 = params[group]
            h3 = net.h3[p, where, :].astype(jnp.float32)
            hs = net.hs[p, where, :].astype(jnp.float32)
            slope = gelu_both(h3 * a3 + hs * a4 + b)[1]
            grad = net.gz[p, where, :] * slope
            net.gz[p, where, :] = grad
            first, cross3, cross4 = carry
            return (
                first + net.fold(grad),
                cross3 + net.fold(grad * (h3 * sa3 + sb3)),
                cross4 + net.fold(grad * (hs * sa4 + sb4)),
            )

        results = net.sweep(join_back, (net.zeros(), net.zeros(), net.zeros()))
        net.put(msg, p, results)
        for group in range(2):
            value = jnp.sum(results[group][2], axis=0, keepdims=True)
            msg.write(4 + p // 2, 2 * (p % 2) + group, value)
    reduce_step()
    exchange.start(6)
    exchange.middle()
    for p in range(2):
        net.emit(2, p * W, 0, dot_rows(net.o1[p], net.small[...]))
    for p in range(2, 4):
        net.emit(2, p * W, 0, dot_rows(net.o1[p], net.small[...]))
    net.flush(3)
    reduce_step()
    exchange.last()
    total = exchange.finish()
    for p in range(4):
        net.back_sweep(THIRD + p, total, p, net.gz.at[p], net.h3.at[p], plain(net.h3.at[p]))
        cross = {group: (4 + p // 2, 2 * (p % 2) + group) for group in BOTH}
        net.back_sweep(
            SIDE + p, total, p, net.gz.at[p], net.hs.at[p], plain(net.hs.at[p]), cross=cross
        )
    for p in range(4):
        net.emit(3, 0, p * W, dot_rows(net.n2[...], net.h3[p]))
    net.flush(4)
    reduce_step()
    value = dot_t(net.h3[0], net.we[:, 0:W])
    for p in range(1, 4):
        value = value + dot_t(net.h3[p], net.we[:, p * W : (p + 1) * W])
    net.f3[...] = value
    msg = exchange.begin()
    net.through(msg, 0, SECOND, net.f3, net.h2, False)
    exchange.start(1)
    exchange.middle()
    for k in range(2):
        for p in range(4):
            net.emit(4, k * W, p * W, dot_rows(net.pixels(0, k), net.hs[p]))
    net.flush(5)
    reduce_step()
    exchange.last()
    total = exchange.finish()
    reduce_step()
    net.back_sweep(SECOND, total, 0, net.f3, net.h2, around(net.small))
    for s in range(4):
        net.shifted(net.t4, net.wb.at[s], s // 2, s % 2)
        net.moved(net.small, top, net.wb.at[s], s // 2, s % 2)
    loads["ws"].wait()
    msg = exchange.begin()
    results = None
    for plane in range(4):
        value = None
        for tap in range(9):
            i, j = divmod(tap, 3)
            if 2 * (i != 1) + (j != 1) == plane:
                term = dot_t(net.wb[2 * (i == 0) + (j == 0), where, :], net.wa[tap])
                value = term if value is None else value + term
        net.f1[plane] = value
        new = net.through(msg, None, FIRST, net.f1.at[plane], net.h1.at[plane], True)
        results = new if results is None else jax.tree.map(jnp.add, results, new)
    reduce_step()
    net.put(msg, 0, results)
    for k in range(2):
        for p in range(4):
            loads["short", 4 * k + p] = net.load(
                8 + 4 * k + p,
                hbm["w_short"].at[pl.ds(k * W, W), pl.ds(p * W, W)],
                net.wb.at[4 * k + p],
            )
    exchange.start(1)
    exchange.middle()
    loads["x"].wait()
    for tap in range(5):
        net.emit(5, tap * W, 0, dot_rows(net.x[tap], net.small[...]))
    for tap in range(5, 9):
        net.emit(5, tap * W, 0, dot_rows(net.x[tap], net.small[...]))
    net.flush(6)
    reduce_step()
    exchange.last()
    total = exchange.finish()
    reduce_step()
    for plane in range(4):
        net.back_sweep(
            FIRST, total, 0, net.f1.at[plane], net.h1.at[plane], plain(net.h1.at[plane]), 4
        )
    for k in range(2):
        value = dot_rows(net.pixels(0, k), net.h1[0])
        for plane in range(1, 4):
            value = value + dot_rows(net.pixels(plane, k), net.h1[plane])
        net.emit(6, k * W, 0, value)
    net.flush(7)
    reduce_step()
    outs = outs[0]
    for plane in range(4):
        for k in range(2):
            value = dot_t(net.h1[plane], net.wr[k * W : (k + 1) * W, :])
            if plane == 0:
                for p in range(4):
                    if k == 0:
                        loads["short", p].wait()
                        loads["short", 4 + p].wait()
                    value = value + dot_t(net.hs[p], net.wb[4 * k + p])
            value = value.astype(jnp.bfloat16).reshape(rows // BLK, BLK, W)
            net.img[plane, :, :, k * W : (k + 1) * W] = value
        for row in range(3):
            out = pltpu.make_async_copy(
                net.img.at[plane, pl.ds(edge + 3 * wide * row, 3 * wide)],
                hbm["grad_local"].at[row, plane // 2, :, plane % 2],
                net.load_sem.at[24 + 3 * plane + row],
            )
            out.start()
            outs.append(out)
        if plane % 2:
            net.gather_image(plane // 2)
            out = pltpu.make_async_copy(
                net.raw.at[plane // 2],
                hbm["grad_global"].at[:, plane // 2],
                net.load_sem.at[plane // 2],
            )
            out.start()
            outs.append(out)
            reduce_step()
    while reducer.busy():
        reduce_step()
    for used in (exchange, *exchanges, *sides):
        for turn in range(len(used.sent)):
            used.settle(turn)
    for out in outs:
        out.wait()


HBM_IN = (
    "image_global",
    "image_local",
    "cot_global",
    "cot_local",
    "w_reduce",
    "w_spatial",
    "w_expand",
    "w_short",
    "w_reduce2",
    "w_spatial2",
    "w_expand2",
    "gain_mid",
    "shift_mid",
    "gain_wide",
    "shift_wide",
)
HBM_OUT = ("y_global", "y_local", "grad_global", "grad_local")
SHAPES = ((512, 2048), (4608, 512), (2048, 512), (512, 2048), (1024, 2048), (4608, 512), (1024, 512))


def whole_kernel(sizes, geometry, names, half, *refs):
    x_bits, dp_bits, _ = bit_counts(sizes)
    steps = x_bits + dp_bits
    place = [0]

    def some(number):
        start = place[0]
        place[0] += number
        return refs[start : place[0]]

    hbm = dict(zip(HBM_IN, some(len(HBM_IN))))
    hbm.update(zip(HBM_OUT, some(len(HBM_OUT))))
    outs = some(7)
    small = some(4)
    grads = some(7)
    (hbm["x_keep"],) = some(1)
    parts = dict(zip(names, some(len(names))))
    groups = len(chip_groups(sizes))

    def some_exchange():
        taken = some(6 + groups)
        return Exchange(sizes, (*taken[:3], taken[3 : 3 + groups], *taken[3 + groups :]))

    exchange, *others = [some_exchange() for _ in range(5)]
    lanes = len(axis_orders(sizes))
    rest = some(2 + lanes * steps + 6)
    landings = [rest[2 + steps * i : 2 + steps * (i + 1)] for i in range(lanes)]
    scratch = (rest[0], rest[1], landings) + tuple(rest[2 + lanes * steps :])
    reducer = Reducer(sizes, SHAPES, half, grads, outs, scratch)
    net = Net(sizes, geometry, parts)
    net.hbm, net.grads = hbm, grads
    net.dgain, net.dshift = (small[0], small[2]), (small[1], small[3])

    flips = [(0, 1)] + [flip for group in chip_groups(sizes) for flip in group[1]]
    semaphore = pltpu.get_barrier_semaphore()

    def arrive():
        for down, across in flips:
            device = (reducer.dp ^ down, reducer.grp ^ across)
            pl.semaphore_signal(semaphore, inc=1, device_id=device, device_id_type=MESH_ID)

    def entered():
        pl.semaphore_wait(semaphore, len(flips))

    net.arrive, net.entered = arrive, entered
    network(net, exchange, others[:2], others[2:], reducer)


def settle_kernel(*refs):
    count = (len(refs) - 2) // 3
    ins, outs, held = refs[:count], refs[count : 2 * count], refs[2 * count : 3 * count]
    first = [pltpu.make_async_copy(ins[i], held[i], refs[-2].at[i]) for i in range(count)]
    second = [pltpu.make_async_copy(held[i], outs[i], refs[-1].at[i]) for i in range(count)]
    for copy in first:
        copy.start()
    for i in range(count):
        first[i].wait()
        second[i].start()
    for copy in second:
        copy.wait()


def settle(values):
    anywhere = pl.BlockSpec(memory_space=pl.ANY)
    count = len(values)
    return pl.pallas_call(
        settle_kernel,
        out_shape=[jax.ShapeDtypeStruct(value.shape, value.dtype) for value in values],
        in_specs=[anywhere] * count,
        out_specs=[anywhere] * count,
        scratch_shapes=[pltpu.VMEM(value.shape, value.dtype) for value in values]
        + [pltpu.SemaphoreType.DMA((count,))] * 2,
        compiler_params=pltpu.CompilerParams(vmem_limit_bytes=VMEM_LIMIT),
    )(*values)


def run_network(arrays, weights, norms, crops, per):
    sizes = (lax.axis_size("dp"), lax.axis_size("grp"))
    dp_size, grp_size = sizes
    dp_bits = dp_size.bit_length() - 1
    half = 256 // dp_size
    rows = crops * 56 + 9 * per
    margin = -(-9 * crops // BLK) * BLK
    bf16, f32 = jnp.bfloat16, jnp.float32
    scratch = {
        "img": pltpu.VMEM((4, rows // BLK, BLK, 1024), bf16),
        "h1": pltpu.VMEM((4, rows, W), bf16),
        "x": pltpu.VMEM((9, rows, W), bf16),
        "f1": pltpu.VMEM((4, rows, W), f32),
        "h3": pltpu.VMEM((4, rows, W), bf16),
        "hs": pltpu.VMEM((4, rows, W), bf16),
        "o1": pltpu.VMEM((4, rows, W), bf16),
        "h2": pltpu.VMEM((rows, W), bf16),
        "h4": pltpu.VMEM((rows, W), bf16),
        "h5": pltpu.VMEM((rows, W), bf16),
        "n2": pltpu.VMEM((rows, W), bf16),
        "n5": pltpu.VMEM((rows, W), bf16),
        "small": pltpu.VMEM((rows, W), bf16),
        "gz": pltpu.VMEM((4, rows, W), f32),
        "gh": pltpu.VMEM((4, rows, W), bf16),
        "t4": pltpu.VMEM((crops * 56 + 2 * margin, W), f32),
        "nl": pltpu.VMEM((4, 9 * per, W), bf16),
        "f3": pltpu.VMEM((rows, W), f32),
        "stage": pltpu.VMEM((2, W, W), f32),
        "wr": pltpu.VMEM((1024, W), bf16),
        "we": pltpu.VMEM((W, 2048), bf16),
        "wr2": pltpu.VMEM((4, W, W), bf16),
        "we2": pltpu.VMEM((W, 2048), bf16),
        "wa": pltpu.VMEM((9, W, W), bf16),
        "wb": pltpu.VMEM((9, W, W), bf16),
        "gain": pltpu.VMEM((16, 1, W), f32),
        "shift": pltpu.VMEM((16, 1, W), f32),
        "mom": pltpu.VMEM((16, 4, W), f32),
        "raw": pltpu.VMEM((2, 7, 14, crops, 1024), bf16),
        "wide": pltpu.VMEM((7, 7, crops, 2048), bf16),
        "turn": pltpu.VMEM((2, 8 * crops, 1024), f32),
        "load_sem": pltpu.SemaphoreType.DMA((76,)),
        "stage_sem": pltpu.SemaphoreType.DMA((2, 32)),
    }
    exchange = exchange_scratch(sizes, 6, 4, 1, 2)
    for _ in range(2):
        exchange += exchange_scratch(sizes, 4, 2, 2, 2)
    for _ in range(2):
        exchange += exchange_scratch(sizes, 4, 2, 1, 1)
    anywhere = pl.BlockSpec(memory_space=pl.ANY)
    inside = pl.BlockSpec(memory_space=pltpu.VMEM)
    shape = jax.ShapeDtypeStruct
    out_shape = (
        [
            shape((7, 7, crops, 2048), bf16),
            shape((9, per, 2048), bf16),
            shape((7, 2, 14, crops, 1024), bf16),
            shape((3, 2, 3, 2, per, 1024), bf16),
        ]
        + [shape((r // dp_size, c), f32) for r, c in SHAPES]
        + [shape((4, W), f32)] * 2
        + [shape((3, 2048), f32)] * 2
        + [shape((2,) * dp_bits + (r // dp_size, c), f32) for r, c in SHAPES]
        + [shape((9, rows, W), bf16)]
    )
    return pl.pallas_call(
        functools.partial(whole_kernel, sizes, (crops, per), tuple(scratch), half),
        out_shape=out_shape,
        in_specs=[anywhere] * (len(HBM_IN) - 4) + [inside] * 4,
        out_specs=[anywhere] * 11 + [inside] * 4 + [anywhere] * 8,
        scratch_shapes=list(scratch.values()) + exchange + reducer_scratch(sizes, half),
        compiler_params=pltpu.CompilerParams(
            collective_id=1, has_side_effects=True, vmem_limit_bytes=VMEM_LIMIT
        ),
    )(*arrays, *weights, *norms)


VMEM_LIMIT = 64 * 2**20 - 2**16


def body(
    image_global,
    image_local,
    w_reduce,
    w_spatial,
    w_expand,
    w_short,
    w_reduce2,
    w_spatial2,
    w_expand2,
    gain_mid,
    shift_mid,
    gain_wide,
    shift_wide,
    cotangent_global,
    cotangent_local,
):
    crops, per = image_global.shape[0], image_local.shape[0]
    results = run_network(
        [
            image_global.transpose(1, 2, 0, 3).reshape(7, 2, 14, crops, 1024),
            image_local.transpose(1, 2, 0, 3).reshape(3, 2, 3, 2, per, 1024),
            cotangent_global.transpose(1, 2, 0, 3),
            cotangent_local.transpose(1, 2, 0, 3).reshape(9, per, 2048),
        ],
        [
            w_reduce,
            w_spatial.reshape(9, W, W),
            w_expand,
            w_short,
            w_reduce2.reshape(4, W, W),
            w_spatial2.reshape(9, W, W),
            w_expand2,
        ],
        [gain_mid, shift_mid, gain_wide, shift_wide],
        crops,
        per,
    )
    results = settle(results[:15])
    y_global, y_local, grad_global, grad_local = results[:4]
    expand2, spatial2, reduce2, expand, short, spatial, reduce = results[4:11]
    return (
        y_global.transpose(2, 0, 1, 3),
        y_local.reshape(3, 3, per, 2048).transpose(2, 0, 1, 3),
        grad_global.reshape(14, 14, crops, 1024).transpose(2, 0, 1, 3),
        grad_local.reshape(6, 6, per, 1024).transpose(2, 0, 1, 3),
        reduce,
        spatial,
        expand,
        short,
        reduce2,
        spatial2,
        expand2,
        *results[11:15],
    )


def solution(mesh):
    crops = P(("dp", "grp"), None, None, None)
    in_specs = (crops, crops) + (P(),) * 11 + (crops, crops)
    out_specs = (crops,) * 4 + (P("dp", None),) * 7 + (P(),) * 4
    return jax.shard_map(body, mesh=mesh, in_specs=in_specs, out_specs=out_specs, check_vma=False)
```
